32 devices in a mesh: sub: 4 (over y, x), grp: 8 (over z, core).
Axes of the slice: x: 2, y: 2, z: 4, core: 2. Of those that a mesh axis runs over, the one named last changes fastest.
Arguments:
- applied_loads: float32 [4, 8, 64, 1536], P('sub', 'grp')
- flex_matrix: bfloat16 [4, 8, 1536, 1536], P('sub', 'grp'), as said below
- schur_matrix: bfloat16 [4, 8, 1536, 1536], P('sub', 'grp'), as said below
- corner_coupling: float32 [4, 8, 12, 1536], P('sub', 'grp'), may hold values from -0.625 to 0.625
- coarse_inverse: float32 [96, 96], replicated, as said below
- face_match: int32 [4, 8, 4, 384], P('sub', 'grp'), may hold values from 0 to 383, as said below
- corner_map: int32 [4, 8, 12], P('sub', 'grp'), may hold values from 0 to 95, as said below
Outputs:
- multipliers: float32 [4, 8, 64, 4, 384], P('sub', 'grp')
- residual: float32 [4, 8, 64, 4, 384], P('sub', 'grp')
The draws below stay inside these ranges and needn't reach their ends.
Inputs may be any that keep to these rules, and one draw needn't show every extreme that they name: `flex_matrix`: each subdomain's matrix is symmetric positive definite. `schur_matrix`: each subdomain's matrix is symmetric positive definite. `coarse_inverse`: lower triangular with a positive diagonal. face_match[s, g, 1] is a permutation of the 384 face nodes and face_match[s+1, g, 0] is its inverse; face_match[s, g, 3] and face_match[s, g+1, 2] likewise (indices wrap). `corner_map`: the 12 entries of one subdomain are distinct; every corner unknown is named by exactly four subdomains.
All inputs are finite; a program needn't handle non-finite values.
Results may differ from the reference program's by a relative error of at most 0.0088.
Values sent between devices are 32-bit elements; how exact they have to be, the bound alone decides.
No kernel may reach another device: no remote copies, remote signals or barrier semaphores. Data moves between devices by JAX's collectives and lax.ppermute only.
A program may use at most 64 MiB of HBM per device.

```python
import math
import jax
import jax.numpy as jnp
from jax import lax

FACE = 384
LOADS = 64
DOF_NODE = 3
ITERS = 2
NI = 1536
NCL = 12
NC = 96
N_SUB = 4
N_GRP = 8


def positive_block(key):

    def one_matrix(index):
        subkeys = jax.random.split(jax.random.fold_in(key, index), 2)
        entries = jax.random.normal(subkeys[0], (NI, NI), jnp.float32) * (0.6 / math.sqrt(NI))
        symmetric = (entries + entries.T) * (1.0 / math.sqrt(2.0))
        diagonal = jax.random.uniform(subkeys[1], (NI, 1), jnp.float32, 1.5, 3.0)
        on_diagonal = (jnp.arange(NI)[:, None] == jnp.arange(NI)[None, :]).astype(jnp.float32)
        matrix = symmetric + on_diagonal * diagonal
        return matrix.astype(jnp.bfloat16)
    stacked = lax.map(one_matrix, jnp.arange(N_SUB * N_GRP))
    return stacked.reshape(N_SUB, N_GRP, NI, NI)


def draw_flex_matrix(key, part):
    key = jax.random.fold_in(key, 11)
    return positive_block(key)


def draw_schur_matrix(key, part):
    key = jax.random.fold_in(key, 12)
    return positive_block(key)


def draw_coarse_inverse(key, part):
    key = jax.random.fold_in(key, 13)
    subkeys = jax.random.split(key, 2)
    row_index = jnp.arange(NC)[:, None]
    col_index = jnp.arange(NC)[None, :]
    off_diagonal = jax.random.normal(subkeys[0], (NC, NC), jnp.float32) * (0.3 / math.sqrt(NC))
    diagonal = jax.random.uniform(subkeys[1], (NC, NC), jnp.float32, 0.6, 1.2)
    return jnp.where(row_index > col_index, off_diagonal, 0.0) + jnp.where(row_index == col_index, diagonal, 0.0)


def draw_applied_loads(key, part):
    key = jax.random.fold_in(key, 14)
    subkeys = jax.random.split(key, 1)
    position = (jnp.arange(N_SUB)[:, None] * N_GRP + jnp.arange(N_GRP)[None, :]).astype(jnp.float32)
    factor = 1.0 + 2.0 * position / max(N_SUB * N_GRP - 1, 1)
    entries = jax.random.normal(subkeys[0], (N_SUB, N_GRP, LOADS, NI), jnp.float32)
    return entries * factor[:, :, None, None]


def draw_face_match(key, part):
    key = jax.random.fold_in(key, 15)
    subkeys = jax.random.split(key, 2)

    def orderings(base):
        return jax.vmap(lambda single: jax.random.permutation(single, FACE))(jax.random.split(base, N_SUB * N_GRP)).reshape(N_SUB, N_GRP, FACE).astype(jnp.int32)
    along_sub = orderings(subkeys[0])
    along_grp = orderings(subkeys[1])
    inverse_sub = jnp.argsort(along_sub, axis=-1).astype(jnp.int32)
    inverse_grp = jnp.argsort(along_grp, axis=-1).astype(jnp.int32)
    return jnp.stack([jnp.roll(inverse_sub, 1, axis=0), along_sub, jnp.roll(inverse_grp, 1, axis=1), along_grp], axis=2)


def draw_corner_map(key, part):
    key = jax.random.fold_in(key, 16)
    ordering = jax.random.permutation(key, N_SUB * N_GRP).reshape(N_SUB, N_GRP).astype(jnp.int32)
    shifted = jnp.roll(ordering, -1, axis=0)
    corner_nodes = jnp.stack([ordering, shifted, jnp.roll(ordering, -1, axis=1), jnp.roll(shifted, -1, axis=1)], axis=-1)
    coarse_ids = corner_nodes[:, :, :, None] * DOF_NODE + jnp.arange(DOF_NODE, dtype=jnp.int32)[None, None, None, :]
    return coarse_ids.reshape(N_SUB, N_GRP, NCL).astype(jnp.int32)


def block_scale(own_key, extent, pieces, least, largest):
    level = 1.0
    for dim, blocks in pieces:
        steps = jax.random.uniform(jax.random.fold_in(jax.random.fold_in(own_key, 6), dim), (blocks,), jnp.float32, least / len(pieces), largest / len(pieces))
        level = level * jnp.repeat(jnp.exp(steps), extent[dim] // blocks).reshape((-1,) + (1,) * (len(extent) - 1 - dim))
    return level


def bell_draw(key, shape, width, most, cuts=(), kind=jnp.bfloat16):
    level = block_scale(key, shape, cuts, -0.22, 0.18) if cuts else 1.0
    drawn = jax.random.normal(key, shape, jnp.float32) * width * level
    return jnp.minimum(jnp.maximum(drawn, -most), most).astype(kind)


def setup_inputs(seed: int = 0) -> dict:
    key_of = jax.random.split(jax.random.key(seed), 8)
    applied_loads = draw_applied_loads(jax.random.fold_in(key_of[7], 71), 0)
    flex_matrix = draw_flex_matrix(jax.random.fold_in(key_of[7], 71), 0)
    schur_matrix = draw_schur_matrix(jax.random.fold_in(key_of[7], 71), 0)
    corner_coupling = bell_draw(key_of[3], (N_SUB, N_GRP, NCL, NI), (NI // 16) ** -0.5, 0.625, ((0, 4), (1, 8)), jnp.float32)
    coarse_inverse = draw_coarse_inverse(jax.random.fold_in(key_of[7], 71), 0)
    face_match = draw_face_match(jax.random.fold_in(key_of[7], 71), 0)
    corner_map = draw_corner_map(jax.random.fold_in(key_of[7], 71), 0)
    return dict(applied_loads=applied_loads, flex_matrix=flex_matrix, schur_matrix=schur_matrix, corner_coupling=corner_coupling, coarse_inverse=coarse_inverse, face_match=face_match, corner_map=corner_map)


def reorder(values, indices):
    return jnp.take_along_axis(values, jnp.broadcast_to(indices[:, :, None, :], values.shape), axis=3)


def neighbour_jump(displaced, matching):
    from_left_sub = reorder(jnp.roll(displaced[:, :, :, 1], 1, axis=0), matching[:, :, 0])
    from_right_sub = reorder(jnp.roll(displaced[:, :, :, 0], -1, axis=0), matching[:, :, 1])
    from_left_grp = reorder(jnp.roll(displaced[:, :, :, 3], 1, axis=1), matching[:, :, 2])
    from_right_grp = reorder(jnp.roll(displaced[:, :, :, 2], -1, axis=1), matching[:, :, 3])
    return jnp.stack([from_left_sub - displaced[:, :, :, 0], displaced[:, :, :, 1] - from_right_sub,
                      from_left_grp - displaced[:, :, :, 2], displaced[:, :, :, 3] - from_right_grp], axis=3)


def local_products(vectors, matrices):
    flat_vectors = vectors.reshape(N_SUB * N_GRP, LOADS, NI)
    flat_matrices = matrices.reshape(N_SUB * N_GRP, NI, NI)
    result = lax.map(lambda operands: jnp.dot(operands[0], operands[1], preferred_element_type=jnp.float32),
                     (flat_vectors, flat_matrices))
    return result.reshape(N_SUB, N_GRP, LOADS, NI)


def reference(applied_loads, flex_matrix, schur_matrix, corner_coupling, coarse_inverse, face_match, corner_map):
    highest = lax.Precision.HIGHEST
    layout = (N_SUB, N_GRP, LOADS, 4, FACE)
    face_signs = jnp.array([-1.0, 1.0, -1.0, 1.0], jnp.float32)[:, None]
    corner_flat = corner_map.reshape(-1)

    def apply_flex(direction):
        forces = (direction * face_signs).reshape(N_SUB, N_GRP, LOADS, NI)
        free = local_products(forces.astype(jnp.bfloat16), flex_matrix)
        corner = jnp.einsum('abkn,abjn->abkj', forces, corner_coupling, precision=highest)
        coarse_rhs = jnp.zeros((LOADS, NC), jnp.float32).at[:, corner_flat].add(
            jnp.transpose(corner, (2, 0, 1, 3)).reshape(LOADS, -1))
        lowered = jnp.dot(coarse_rhs, coarse_inverse.T, precision=highest)
        coarse_sol = jnp.dot(lowered, coarse_inverse, precision=highest)
        picked = jnp.transpose(coarse_sol[:, corner_flat].reshape(LOADS, N_SUB, N_GRP, NCL), (1, 2, 0, 3))
        displaced = free + jnp.einsum('abkj,abjn->abkn', picked, corner_coupling, precision=highest)
        curvature = jnp.sum(forces * displaced, axis=(0, 1, 3))
        return neighbour_jump(displaced.reshape(layout), face_match), curvature

    def apply_precond(current):
        weighted = (0.5 * current * face_signs).astype(jnp.bfloat16).reshape(N_SUB, N_GRP, LOADS, NI)
        response = local_products(weighted, schur_matrix)
        return 0.5 * neighbour_jump(response.reshape(layout), face_match)

    def inner(former, latter):
        return 0.5 * jnp.sum(former * latter, axis=(0, 1, 3, 4))

    right_side = neighbour_jump(applied_loads.reshape(layout), face_match)
    multipliers = jnp.zeros(layout, jnp.float32)
    residual = right_side
    precond = apply_precond(residual)
    precond_dot = inner(residual, precond)
    direction = precond
    for iteration in range(ITERS):
        image, curvature = apply_flex(direction)
        step_size = (precond_dot / curvature)[None, None, :, None, None]
        multipliers = multipliers + step_size * direction
        residual = residual - step_size * image
        if iteration + 1 < ITERS:
            precond = apply_precond(residual)
            next_dot = inner(residual, precond)
            direction = precond + (next_dot / precond_dot)[None, None, :, None, None] * direction
            precond_dot = next_dot
    return multipliers, residual
```

```python
import jax
import jax.numpy as jnp
from jax import lax
from jax.sharding import PartitionSpec as P

HIGHEST = lax.Precision.HIGHEST
LAST = (((1,), (1,)), ((), ()))


def sum_over(values, axis):
    peers = lax.axis_size(axis)
    if peers & (peers - 1):
        return lax.psum(values, axis)
    step = 1
    while step < peers:
        swap = [(i, i ^ step) for i in range(peers)]
        values = values + lax.ppermute(values, axis, swap)
        step *= 2
    return values


def sum_all(values):
    return sum_over(sum_over(values, "grp"), "sub")


def exchange(faces):
    received = []
    for axis, (low, high) in (("sub", faces[0:2]), ("grp", faces[2:4])):
        peers = lax.axis_size(axis)
        up = [(i, (i + 1) % peers) for i in range(peers)]
        down = [(j, i) for i, j in up]
        received.append(lax.ppermute(high, axis, up))
        received.append(lax.ppermute(low, axis, down))
    return received


def split_faces(field):
    size = field.shape[1] // 4
    return [field[:, i * size : (i + 1) * size] for i in range(4)]


def jump(received, own):
    return jnp.concatenate(
        [received[0] - own[0], own[1] - received[1], received[2] - own[2], own[3] - received[3]],
        axis=1,
    )


def two_part_dot(values, matrix):
    high = values.astype(jnp.bfloat16)
    low = (values - high.astype(jnp.float32)).astype(jnp.bfloat16)
    rows = values.shape[0]
    both = jnp.dot(
        jnp.concatenate([high, low], axis=0), matrix, preferred_element_type=jnp.float32
    )
    return both[:rows] + both[rows:]


def shards(
    applied_loads,
    flex_matrix,
    schur_matrix,
    corner_coupling,
    coarse_inverse,
    face_match,
    corner_map,
):
    loads = applied_loads[0, 0]
    flex = flex_matrix[0, 0]
    schur = schur_matrix[0, 0]
    coupling = corner_coupling[0, 0]
    matching = face_match[0, 0]
    corners = corner_map[0, 0]
    cases, interface = loads.shape
    face = interface // 4
    slots = coupling.shape[0]
    coarse_size = coarse_inverse.shape[0]
    signs = jnp.repeat(jnp.array([-1.0, 1.0, -1.0, 1.0], jnp.float32), face)[None, :]

    def matched(received):
        return [jnp.take(received[i], matching[i], axis=1) for i in range(4)]

    def selector(numbers):
        every = jnp.arange(coarse_size, dtype=jnp.int32)
        return (numbers[:, None] == every[None, :]).astype(jnp.float32)

    def spread(numbers, rows):
        return lax.dot_general(
            selector(numbers), rows, (((0,), (0,)), ((), ())), precision=HIGHEST
        )

    numbers = jnp.zeros((1, face), jnp.float32).at[0, :slots].set(corners.astype(jnp.float32))
    own_loads = split_faces(loads)
    own_coupling = split_faces(coupling)
    first = exchange(
        [jnp.concatenate([own_loads[i], own_coupling[i], numbers], axis=0) for i in range(4)]
    )
    first_matched = matched(first)
    residual = jump([x[:cases] for x in first_matched], own_loads)
    own_spread = [spread(corners, x) for x in own_coupling]
    near_spread = [
        spread(
            jnp.round(first[i][cases + slots, :slots]).astype(jnp.int32),
            first_matched[i][cases : cases + slots],
        )
        for i in range(4)
    ]
    coarse_image = jump(near_spread, own_spread)
    own_spread = jnp.concatenate(own_spread, axis=1)

    def precondition(current):
        weighted = (0.5 * current * signs).astype(jnp.bfloat16)
        response = jnp.dot(weighted, schur, preferred_element_type=jnp.float32)
        own = split_faces(response)
        return 0.5 * jump(matched(exchange(own)), own)

    def total(x, y):
        return jnp.sum(x * y, axis=1, keepdims=True)

    def coarse_solve(right):
        lowered = lax.dot_general(right, coarse_inverse, LAST, precision=HIGHEST)
        return jnp.dot(lowered, coarse_inverse, precision=HIGHEST), total(lowered, lowered)

    precond = precondition(residual)
    forces = precond * signs
    free = jnp.dot(forces.astype(jnp.bfloat16), flex, preferred_element_type=jnp.float32)
    sums = sum_all(
        jnp.concatenate(
            [
                lax.dot_general(forces, own_spread, LAST, precision=HIGHEST),
                0.5 * total(residual, precond),
                total(forces, free),
            ],
            axis=1,
        )
    )
    own = split_faces(free)
    free_jump = jump(matched(exchange(own)), own)
    right, rz, local = sums[:, :coarse_size], sums[:, -2:-1], sums[:, -1:]
    coarse, energy = coarse_solve(right)
    curvature = local + energy
    step = rz / curvature
    direction = precond
    multipliers = step * direction
    residual = residual - step * (free_jump + jnp.dot(coarse, coarse_image, precision=HIGHEST))

    precond = precondition(residual)
    forces_next = precond * signs
    free_next = two_part_dot(forces_next, flex)
    sums = sum_all(
        jnp.concatenate(
            [
                lax.dot_general(forces_next, own_spread, LAST, precision=HIGHEST),
                0.5 * total(residual, precond),
                total(forces_next, free_next),
                total(forces_next, free) + total(forces, free_next),
            ],
            axis=1,
        )
    )
    own = split_faces(free_next)
    next_jump = jump(matched(exchange(own)), own)
    beta = sums[:, -3:-2] / rz
    coarse, energy = coarse_solve(sums[:, :coarse_size] + beta * right)
    curvature = sums[:, -2:-1] + beta * sums[:, -1:] + beta * beta * local + energy
    step = sums[:, -3:-2] / curvature
    direction = precond + beta * direction
    image = next_jump + beta * free_jump + jnp.dot(coarse, coarse_image, precision=HIGHEST)
    multipliers = multipliers + step * direction
    residual = residual - step * image
    layout = (1, 1, cases, 4, face)
    return multipliers.reshape(layout), residual.reshape(layout)


def solution(mesh):
    return jax.shard_map(
        shards,
        mesh=mesh,
        in_specs=(
            P("sub", "grp", None, None),
            P("sub", "grp", None, None),
            P("sub", "grp", None, None),
            P("sub", "grp", None, None),
            P(),
            P("sub", "grp", None, None),
            P("sub", "grp", None),
        ),
        out_specs=(P("sub", "grp", None, None, None), P("sub", "grp", None, None, None)),
        check_vma=False,
    )
```

```python
import jax
import jax.numpy as jnp
from jax import lax
from jax.sharding import PartitionSpec as P

HIGHEST = lax.Precision.HIGHEST
LAST = (((1,), (1,)), ((), ()))


def sum_all(values):
    peers = lax.axis_size("sub") * lax.axis_size("grp")
    stages = [("sub", "grp")] if peers * values.size <= 2**20 else ["grp", "sub"]
    for axes in stages:
        values = jnp.sum(lax.all_gather(values, axes), axis=0)
    return values


def exchange(faces):
    received = []
    for axis, (low, high) in (("sub", faces[0:2]), ("grp", faces[2:4])):
        peers = lax.axis_size(axis)
        up = [(i, (i + 1) % peers) for i in range(peers)]
        down = [(j, i) for i, j in up]
        received.append(lax.ppermute(high, axis, up))
        received.append(lax.ppermute(low, axis, down))
    return received


def split_faces(field):
    size = field.shape[1] // 4
    return [field[:, i * size : (i + 1) * size] for i in range(4)]


def jump(received, own):
    return jnp.concatenate(
        [received[0] - own[0], own[1] - received[1], received[2] - own[2], own[3] - received[3]],
        axis=1,
    )


def two_part_dot(values, matrix):
    high = values.astype(jnp.bfloat16)
    low = (values - high.astype(jnp.float32)).astype(jnp.bfloat16)
    rows = values.shape[0]
    both = jnp.dot(
        jnp.concatenate([high, low], axis=0), matrix, preferred_element_type=jnp.float32
    )
    return both[:rows] + both[rows:]


def shards(
    applied_loads,
    flex_matrix,
    schur_matrix,
    corner_coupling,
    coarse_inverse,
    face_match,
    corner_map,
):
    loads = applied_loads[0, 0]
    flex = flex_matrix[0, 0]
    schur = schur_matrix[0, 0]
    coupling = corner_coupling[0, 0]
    matching = face_match[0, 0]
    corners = corner_map[0, 0]
    cases, interface = loads.shape
    face = interface // 4
    slots = coupling.shape[0]
    coarse_size = coarse_inverse.shape[0]
    signs = jnp.repeat(jnp.array([-1.0, 1.0, -1.0, 1.0], jnp.float32), face)[None, :]

    def matched(received):
        return [jnp.take(received[i], matching[i], axis=1) for i in range(4)]

    def selector(numbers):
        every = jnp.arange(coarse_size, dtype=jnp.int32)
        return (numbers[:, None] == every[None, :]).astype(jnp.float32)

    def spread(numbers, rows):
        return lax.dot_general(
            selector(numbers), rows, (((0,), (0,)), ((), ())), precision=HIGHEST
        )

    numbers = jnp.zeros((1, face), jnp.float32).at[0, :slots].set(corners.astype(jnp.float32))
    own_loads = split_faces(loads)
    own_coupling = split_faces(coupling)
    first = exchange(
        [jnp.concatenate([own_loads[i], own_coupling[i], numbers], axis=0) for i in range(4)]
    )
    first_matched = matched(first)
    residual = jump([x[:cases] for x in first_matched], own_loads)
    own_spread = [spread(corners, x) for x in own_coupling]
    near_spread = [
        spread(
            jnp.round(first[i][cases + slots, :slots]).astype(jnp.int32),
            first_matched[i][cases : cases + slots],
        )
        for i in range(4)
    ]
    coarse_image = jump(near_spread, own_spread)
    own_spread = jnp.concatenate(own_spread, axis=1)

    def precondition(current):
        weighted = (0.5 * current * signs).astype(jnp.bfloat16)
        response = jnp.dot(weighted, schur, preferred_element_type=jnp.float32)
        own = split_faces(response)
        return 0.5 * jump(matched(exchange(own)), own)

    def total(x, y):
        return jnp.sum(x * y, axis=1, keepdims=True)

    def coarse_solve(right):
        lowered = lax.dot_general(right, coarse_inverse, LAST, precision=HIGHEST)
        return jnp.dot(lowered, coarse_inverse, precision=HIGHEST), total(lowered, lowered)

    precond = precondition(residual)
    forces = precond * signs
    free = jnp.dot(forces.astype(jnp.bfloat16), flex, preferred_element_type=jnp.float32)
    sums = sum_all(
        jnp.concatenate(
            [
                lax.dot_general(forces, own_spread, LAST, precision=HIGHEST),
                0.5 * total(residual, precond),
                total(forces, free),
            ],
            axis=1,
        )
    )
    own = split_faces(free)
    free_jump = jump(matched(exchange(own)), own)
    right, rz, local = sums[:, :coarse_size], sums[:, -2:-1], sums[:, -1:]
    coarse, energy = coarse_solve(right)
    curvature = local + energy
    step = rz / curvature
    direction = precond
    multipliers = step * direction
    residual = residual - step * (free_jump + jnp.dot(coarse, coarse_image, precision=HIGHEST))

    precond = precondition(residual)
    forces_next = precond * signs
    free_next = two_part_dot(forces_next, flex)
    sums = sum_all(
        jnp.concatenate(
            [
                lax.dot_general(forces_next, own_spread, LAST, precision=HIGHEST),
                0.5 * total(residual, precond),
                total(forces_next, free_next),
                total(forces_next, free) + total(forces, free_next),
            ],
            axis=1,
        )
    )
    own = split_faces(free_next)
    next_jump = jump(matched(exchange(own)), own)
    beta = sums[:, -3:-2] / rz
    coarse, energy = coarse_solve(sums[:, :coarse_size] + beta * right)
    curvature = sums[:, -2:-1] + beta * sums[:, -1:] + beta * beta * local + energy
    step = sums[:, -3:-2] / curvature
    direction = precond + beta * direction
    image = next_jump + beta * free_jump + jnp.dot(coarse, coarse_image, precision=HIGHEST)
    multipliers = multipliers + step * direction
    residual = residual - step * image
    layout = (1, 1, cases, 4, face)
    return multipliers.reshape(layout), residual.reshape(layout)


def solution(mesh):
    return jax.shard_map(
        shards,
        mesh=mesh,
        in_specs=(
            P("sub", "grp", None, None),
            P("sub", "grp", None, None),
            P("sub", "grp", None, None),
            P("sub", "grp", None, None),
            P(),
            P("sub", "grp", None, None),
            P("sub", "grp", None),
        ),
        out_specs=(P("sub", "grp", None, None, None), P("sub", "grp", None, None, None)),
        check_vma=False,
    )
```

```python
import functools

import jax
import jax.numpy as jnp
from jax import lax
from jax.experimental import pallas as pl
from jax.experimental.pallas import tpu as pltpu
from jax.sharding import PartitionSpec as P

HIGHEST = lax.Precision.HIGHEST
PLAIN = (((1,), (0,)), ((), ()))
LAST = (((1,), (1,)), ((), ()))
LANES = 128
SIGNS = (-1.0, 1.0, -1.0, 1.0)


def sum_over(values, axis):
    peers = lax.axis_size(axis)
    if peers & (peers - 1):
        return lax.psum(values, axis)
    step = 1
    while step < peers:
        swap = [(i, i ^ step) for i in range(peers)]
        values = values + lax.ppermute(values, axis, swap)
        step *= 2
    return values


def sum_all(values):
    return sum_over(sum_over(values, "grp"), "sub")


def exchange(faces):
    received = []
    for axis, (low, high) in (("sub", faces[0:2]), ("grp", faces[2:4])):
        peers = lax.axis_size(axis)
        up = [(i, (i + 1) % peers) for i in range(peers)]
        down = [(j, i) for i, j in up]
        received.append(lax.ppermute(high, axis, up))
        received.append(lax.ppermute(low, axis, down))
    return received


def one_hot(match_ref, i):
    row = match_ref[i : i + 1, :]
    size = row.shape[1]
    nodes = lax.broadcasted_iota(jnp.int32, (size, size), 0)
    return jnp.where(nodes == row, 1.0, 0.0).astype(jnp.bfloat16)


def parts(x, count):
    out = []
    for _ in range(count):
        part = x.astype(jnp.bfloat16)
        out.append(part)
        x = x - part.astype(jnp.float32)
    return out


def mxu(x, y, dims=PLAIN):
    return lax.dot_general(x, y, dims, preferred_element_type=jnp.float32)


def exact(x, y, dims=PLAIN):
    return lax.dot_general(x, y, dims, precision=HIGHEST, preferred_element_type=jnp.float32)


def reorder(x, hot, dims):
    rows = x.shape[0]
    both = mxu(jnp.concatenate(parts(x, 3), axis=0), hot, dims)
    return both[:rows] + both[rows : 2 * rows] + both[2 * rows :]


def turn(x, hot):
    return reorder(x, hot, LAST)


def turn_back(x, hot):
    return reorder(x, hot, PLAIN)


def jump(received, own):
    return [
        received[0] - own[0],
        own[1] - received[1],
        received[2] - own[2],
        own[3] - received[3],
    ]


def faces_of(ref, size):
    return [ref[:, i * size : (i + 1) * size] for i in range(4)]


def store(ref, faces):
    size = faces[0].shape[1]
    for i in range(4):
        ref[:, i * size : (i + 1) * size] = faces[i]


def total(xs, ys):
    return sum(jnp.sum(x * y, axis=1, keepdims=True) for x, y in zip(xs, ys))


def blocks_of(interface):
    width = 256 if interface % 256 == 0 else interface
    return [slice(i, i + width) for i in range(0, interface, width)]


def fetch(matrix_ref, held_ref, sems):
    copies = []
    for i, block in enumerate(blocks_of(matrix_ref.shape[1])):
        copies.append(
            pltpu.make_async_copy(matrix_ref.at[:, block], held_ref.at[:, block], sems.at[i])
        )
        copies[-1].start()
    return copies


def product(copies, held_ref, result_ref, left):
    rows = result_ref.shape[0]
    for copy, block in zip(copies, blocks_of(held_ref.shape[1])):
        copy.wait()
        both = mxu(left, held_ref[:, block])
        value = both[:rows]
        for i in range(1, left.shape[0] // rows):
            value = value + both[i * rows : (i + 1) * rows]
        result_ref[:, block] = value


def local_order(faces, hots, count):
    split = [jnp.concatenate(parts(x, count), axis=0) for x in faces]
    split[0] = mxu(split[0], hots[0]).astype(jnp.bfloat16)
    split[2] = mxu(split[2], hots[1]).astype(jnp.bfloat16)
    return jnp.concatenate(split, axis=1)


def turned_result(result_ref, hots):
    size = result_ref.shape[1] // 4
    own = faces_of(result_ref, size)
    own[0] = turn(own[0], hots[0])
    own[2] = turn(own[2], hots[1])
    return own


def schur_response(residual, hots, copies, held_ref, result_ref):
    weighted = [(0.5 * s) * x for s, x in zip(SIGNS, residual)]
    product(copies, held_ref, result_ref, local_order(weighted, hots, 1))
    return turned_result(result_ref, hots)


def signed(faces):
    return [s * x for s, x in zip(SIGNS, faces)]


def lane_is(shape, lane):
    return lax.broadcasted_iota(jnp.int32, shape, 1) == lane


def pick(values, lane):
    return jnp.sum(jnp.where(lane_is(values.shape, lane), values, 0.0), axis=1, keepdims=True)


def spread(rows, numbers, width):
    nodes = lax.broadcasted_iota(jnp.int32, (width, numbers.shape[1]), 0)
    hot = jnp.where(nodes.astype(jnp.float32) == numbers, 1.0, 0.0)
    return exact(hot[:, : rows.shape[0]], rows)


def partial_sums(forces, own_rows, numbers, scalars, coarse_size, width):
    out = 0.0
    for x, rows in zip(forces, own_rows):
        out = out + exact(x, rows, LAST)
    nodes = lax.broadcasted_iota(jnp.int32, (width, numbers.shape[1]), 0)
    hot = jnp.where(nodes.astype(jnp.float32) == numbers, 1.0, 0.0)[:, : out.shape[1]]
    out = exact(out, hot, LAST)
    for i, value in enumerate(scalars):
        out = out + jnp.where(lane_is(out.shape, coarse_size + i), value, 0.0)
    return out


def coarse_solve(right, inverse):
    lowered = exact(right, inverse, LAST)
    return exact(lowered, inverse), jnp.sum(lowered * lowered, axis=1, keepdims=True)


def coarse_part(sums, coarse_size):
    lanes = lax.broadcasted_iota(jnp.int32, sums.shape, 1)
    return jnp.where(lanes < coarse_size, sums, 0.0)


def first_kernel(loads_ref, near0, near1, near2, near3, match_ref, extra_ref, schur_ref,
                 residual_ref, send0, send1, send2, send3, held_ref, result_ref, sems):
    copies = fetch(schur_ref, held_ref, sems)
    cases = loads_ref.shape[0]
    size = loads_ref.shape[1] // 4
    hots = [one_hot(match_ref, 0), one_hot(match_ref, 2)]
    own = faces_of(loads_ref, size)
    residual = [
        near0[...] - turn(own[0], hots[0]),
        own[1] - reorder(near1[...], one_hot(match_ref, 1), PLAIN),
        near2[...] - turn(own[2], hots[1]),
        own[3] - reorder(near3[...], one_hot(match_ref, 3), PLAIN),
    ]
    store(residual_ref, residual)
    extra = faces_of(extra_ref, size)
    turned = [turn(extra[0], hots[0]), extra[1], turn(extra[2], hots[1]), extra[3]]
    rows = lax.broadcasted_iota(jnp.int32, extra[0].shape, 0)
    slots = extra_ref.shape[0] - 4
    response = schur_response(residual, hots, copies, held_ref, result_ref)
    for i, send in enumerate((send0, send1, send2, send3)):
        send[:cases, :] = response[i]
        send[cases:, :] = jnp.where(rows < slots, turned[i], extra[i])


def coarse_kernel(slots, own0, own1, own2, own3, near0, near1, near2, near3, image_ref):
    width = image_ref.shape[0]
    cases = own0.shape[0] - slots - 4

    def field(ref):
        rows = ref[cases:, :]
        return spread(rows, ref[cases + slots : cases + slots + 1, :LANES], width)
    own = [field(ref) for ref in (own0, own1, own2, own3)]
    near = [field(ref) for ref in (near0, near1, near2, near3)]
    store(image_ref, jump(near, own))


def direction_kernel(coarse_size, count, cases, *refs):
    slots = refs[8].shape[0] - cases - 4
    own = refs[0:4]
    near = refs[4:8]
    extra = refs[8:12]
    residual_ref, match_ref, flex_ref = refs[12:15]
    n = 15
    if count > 1:
        before_ref = refs[15]
        before_free = refs[16:20]
        n = 20
    precond_ref, free0, free1, free2, free3, sums_ref, held_ref, result_ref, sems = refs[n:]
    copies = fetch(flex_ref, held_ref, sems)
    size = own[0].shape[1]
    hots = [one_hot(match_ref, 0), one_hot(match_ref, 2)]
    precond = jump([x[:cases, :] for x in near], [x[:cases, :] for x in own])
    precond = [0.5 * x for x in precond]
    store(precond_ref, precond)
    forces = signed(precond)
    product(copies, held_ref, result_ref, local_order(forces, hots, count))
    free = turned_result(result_ref, hots)
    for ref, value in zip((free0, free1, free2, free3), free):
        ref[...] = value
    residual = faces_of(residual_ref, size)
    scalars = [0.5 * total(residual, precond), total(forces, free)]
    if count > 1:
        before = signed(faces_of(before_ref, size))
        scalars.append(total(forces, [x[...] for x in before_free]) + total(before, free))
    rows = [x[cases:, :] for x in extra]
    numbers = extra[0][cases + slots : cases + slots + 1, :LANES]
    sums_ref[...] = partial_sums(
        forces, rows, numbers, scalars, coarse_size, sums_ref.shape[1]
    )


def step_kernel(coarse_size, *refs):
    sums_ref, inverse_ref, image_ref = refs[0:3]
    own = refs[3:7]
    near = refs[7:11]
    residual_ref, match_ref, schur_ref = refs[11:14]
    new_ref, jump_ref, step_ref, send0, send1, send2, send3, held_ref, result_ref, sems = refs[14:]
    copies = fetch(schur_ref, held_ref, sems)
    size = own[0].shape[1]
    sums = sums_ref[...]
    hots = [one_hot(match_ref, 0), one_hot(match_ref, 2)]
    coarse, energy = coarse_solve(coarse_part(sums, coarse_size), inverse_ref[...])
    step = pick(sums, coarse_size) / (pick(sums, coarse_size + 1) + energy)
    step_ref[...] = jnp.broadcast_to(step, step_ref.shape)
    moved = jump([x[...] for x in near], [x[...] for x in own])
    store(jump_ref, moved)
    images = faces_of(image_ref, size)
    residual = faces_of(residual_ref, size)
    residual = [r - step * (m + exact(coarse, g)) for r, m, g in zip(residual, moved, images)]
    store(new_ref, residual)
    response = schur_response(residual, hots, copies, held_ref, result_ref)
    for ref, value in zip((send0, send1, send2, send3), response):
        ref[...] = value


def last_kernel(coarse_size, *refs):
    first_ref, sums_ref, inverse_ref, image_ref = refs[0:4]
    own = refs[4:8]
    near = refs[8:12]
    residual_ref, before_ref, precond_ref, jump_ref, step_ref, match_ref = refs[12:18]
    multipliers_ref, out_ref = refs[18:]
    size = own[0].shape[1]
    first = first_ref[...]
    sums = sums_ref[...]
    hots = [one_hot(match_ref, 0), one_hot(match_ref, 2)]
    beta = pick(sums, coarse_size) / pick(first, coarse_size)
    right = coarse_part(sums, coarse_size) + beta * coarse_part(first, coarse_size)
    coarse, energy = coarse_solve(right, inverse_ref[...])
    local = pick(sums, coarse_size + 1) + beta * (
        pick(sums, coarse_size + 2) + beta * pick(first, coarse_size + 1)
    )
    step = pick(sums, coarse_size) / (local + energy)
    step_before = step_ref[:, 0:1]
    moved = jump([x[...] for x in near], [x[...] for x in own])
    images = faces_of(image_ref, size)
    residual = faces_of(residual_ref, size)
    before = faces_of(before_ref, size)
    precond = faces_of(precond_ref, size)
    jumps = faces_of(jump_ref, size)
    for i in range(4):
        image = moved[i] + beta * jumps[i] + exact(coarse, images[i])
        r = residual[i] - step * image
        m = step_before * before[i] + step * (precond[i] + beta * before[i])
        if i in (0, 2):
            r = turn_back(r, hots[i // 2])
            m = turn_back(m, hots[i // 2])
        out_ref[:, i, :] = r
        multipliers_ref[:, i, :] = m


VMEM = pl.BlockSpec(memory_space=pltpu.VMEM)
ANY = pl.BlockSpec(memory_space=pl.ANY)


def call(kernel, args, outs, dense=None, cases=None, flops=0):
    specs = [VMEM] * len(args)
    scratch = []
    if dense is not None:
        specs[dense] = ANY
        interface = args[dense].shape[0]
        scratch = [
            pltpu.VMEM((interface, interface), jnp.bfloat16),
            pltpu.VMEM((cases, interface), jnp.float32),
            pltpu.SemaphoreType.DMA((len(blocks_of(interface)),)),
        ]
    return pl.pallas_call(
        kernel,
        in_specs=specs,
        out_specs=[VMEM] * len(outs),
        out_shape=[jax.ShapeDtypeStruct(x, jnp.float32) for x in outs],
        scratch_shapes=scratch,
        compiler_params=pltpu.CompilerParams(vmem_limit_bytes=40 * 2**20),
        cost_estimate=pl.CostEstimate(flops=flops, bytes_accessed=2**22, transcendentals=0),
    )(*args)


def shards(
    applied_loads,
    flex_matrix,
    schur_matrix,
    corner_coupling,
    coarse_inverse,
    face_match,
    corner_map,
):
    loads = applied_loads[0, 0]
    flex = flex_matrix[0, 0]
    schur = schur_matrix[0, 0]
    match = face_match[0, 0]
    cases, interface = loads.shape
    size = interface // 4
    slots = corner_coupling.shape[2]
    coarse_size = coarse_inverse.shape[0]
    width = -(-(coarse_size + 3) // LANES) * LANES
    work = 2 * cases * interface * interface

    numbers = jnp.full((1, size), -1.0, jnp.float32)
    numbers = numbers.at[0, :slots].set(corner_map[0, 0].astype(jnp.float32))
    extra = jnp.concatenate(
        [corner_coupling[0, 0], jnp.tile(numbers, (1, 4)), jnp.zeros((3, interface), jnp.float32)],
        axis=0,
    )
    inverse = jnp.pad(coarse_inverse, ((0, width - coarse_size), (0, width - coarse_size)))
    field = (cases, interface)
    face = (cases, size)
    tall = (cases + slots + 4, size)

    near = exchange([loads[:, i * size : (i + 1) * size] for i in range(4)])
    residual, *own_first = call(
        first_kernel,
        [loads, *near, match, extra, schur],
        [field] + [tall] * 4,
        dense=7,
        cases=cases,
        flops=work,
    )
    near = exchange(own_first)
    before, *own, sums = call(
        functools.partial(direction_kernel, coarse_size, 1, cases),
        [*own_first, *near, *own_first, residual, match, flex],
        [field] + [face] * 4 + [(cases, width)],
        dense=14,
        cases=cases,
        flops=work,
    )
    (image,) = call(functools.partial(coarse_kernel, slots), [*own_first, *near], [(width, interface)], flops=work // 4)
    own_free = own
    near = exchange(own)
    first_sums = sum_all(sums)
    residual, moved, step, *own = call(
        functools.partial(step_kernel, coarse_size),
        [first_sums, inverse, image, *own, *near, residual, match, schur],
        [field, field, (cases, LANES)] + [face] * 4,
        dense=13,
        cases=cases,
        flops=work,
    )
    near = exchange(own)
    precond, *own, sums = call(
        functools.partial(direction_kernel, coarse_size, 2, cases),
        [*own, *near, *own_first, residual, match, flex, before, *own_free],
        [field] + [face] * 4 + [(cases, width)],
        dense=14,
        cases=cases,
        flops=work,
    )
    near = exchange(own)
    sums = sum_all(sums)
    layout = (cases, 4, size)
    multipliers, residual = call(
        functools.partial(last_kernel, coarse_size),
        [first_sums, sums, inverse, image, *own, *near, residual, before, precond, moved, step, match],
        [layout, layout],
        flops=work // 4,
    )
    return multipliers[None, None], residual[None, None]


def solution(mesh):
    return jax.shard_map(
        shards,
        mesh=mesh,
        in_specs=(
            P("sub", "grp", None, None),
            P("sub", "grp", None, None),
            P("sub", "grp", None, None),
            P("sub", "grp", None, None),
            P(),
            P("sub", "grp", None, None),
            P("sub", "grp", None),
        ),
        out_specs=(P("sub", "grp", None, None, None), P("sub", "grp", None, None, None)),
        check_vma=False,
    )
```

```python
import functools

import jax
import jax.numpy as jnp
from jax import lax
from jax.experimental import pallas as pl
from jax.experimental.pallas import tpu as pltpu
from jax.sharding import PartitionSpec as P

HIGHEST = lax.Precision.HIGHEST
PLAIN = (((1,), (0,)), ((), ()))
LAST = (((1,), (1,)), ((), ()))
LANES = 128
SIGNS = (-1.0, 1.0, -1.0, 1.0)


def sum_over(values, axis):
    peers = lax.axis_size(axis)
    if peers & (peers - 1):
        return lax.psum(values, axis)
    step = 1
    while step < peers:
        swap = [(i, i ^ step) for i in range(peers)]
        values = values + lax.ppermute(values, axis, swap)
        step *= 2
    return values


def exchange(faces):
    received = []
    for axis, (low, high) in (("sub", faces[0:2]), ("grp", faces[2:4])):
        peers = lax.axis_size(axis)
        up = [(i, (i + 1) % peers) for i in range(peers)]
        down = [(j, i) for i, j in up]
        received.append(lax.ppermute(high, axis, up))
        received.append(lax.ppermute(low, axis, down))
    return received


def one_hot(match_ref, i):
    row = match_ref[i : i + 1, :]
    size = row.shape[1]
    nodes = lax.broadcasted_iota(jnp.int32, (size, size), 0)
    return jnp.where(nodes == row, 1.0, 0.0).astype(jnp.bfloat16)


def parts(x, count):
    out = []
    for _ in range(count):
        part = x.astype(jnp.bfloat16)
        out.append(part)
        x = x - part.astype(jnp.float32)
    return out


def mxu(x, y, dims=PLAIN):
    return lax.dot_general(x, y, dims, preferred_element_type=jnp.float32)


def exact(x, y, dims=PLAIN):
    return lax.dot_general(x, y, dims, precision=HIGHEST, preferred_element_type=jnp.float32)


def reorder(x, hot, dims):
    rows = x.shape[0]
    both = mxu(jnp.concatenate(parts(x, 3), axis=0), hot, dims)
    return both[:rows] + both[rows : 2 * rows] + both[2 * rows :]


def turn(x, hot):
    return reorder(x, hot, LAST)


def turn_back(x, hot):
    return reorder(x, hot, PLAIN)


def jump(received, own):
    return [
        received[0] - own[0],
        own[1] - received[1],
        received[2] - own[2],
        own[3] - received[3],
    ]


def faces_of(ref, size):
    return [ref[:, i * size : (i + 1) * size] for i in range(4)]


def store(ref, faces):
    size = faces[0].shape[1]
    for i in range(4):
        ref[:, i * size : (i + 1) * size] = faces[i]


def total(xs, ys):
    return sum(jnp.sum(x * y, axis=1, keepdims=True) for x, y in zip(xs, ys))


def blocks_of(interface):
    width = 256 if interface % 256 == 0 else interface
    return [slice(i, i + width) for i in range(0, interface, width)]


def product(matrix_ref, result_ref, left, groups):
    for block in blocks_of(matrix_ref.shape[1]):
        both = mxu(left, matrix_ref[:, block])
        at = 0
        for first, rows, count in groups:
            value = both[first : first + rows]
            for i in range(1, count):
                value = value + both[first + i * rows : first + (i + 1) * rows]
            result_ref[at : at + rows, block] = value
            at += rows


def local_order(faces, hots, count):
    split = [jnp.concatenate(parts(x, count), axis=0) for x in faces]
    split[0] = mxu(split[0], hots[0]).astype(jnp.bfloat16)
    split[2] = mxu(split[2], hots[2]).astype(jnp.bfloat16)
    return jnp.concatenate(split, axis=1)


def turned_result(result_ref, hots):
    size = result_ref.shape[1] // 4
    own = faces_of(result_ref, size)
    own[0] = turn(own[0], hots[0])
    own[2] = turn(own[2], hots[2])
    return own


def weighted(faces):
    return [(0.5 * s) * x for s, x in zip(SIGNS, faces)]


def hots_of(hots_ref):
    size = hots_ref.shape[1]
    return [hots_ref[i * size : (i + 1) * size, :] for i in range(4)]


def signed(faces):
    return [s * x for s, x in zip(SIGNS, faces)]


def lane_is(shape, lane):
    return lax.broadcasted_iota(jnp.int32, shape, 1) == lane


def pick(values, lane):
    return jnp.sum(jnp.where(lane_is(values.shape, lane), values, 0.0), axis=1, keepdims=True)


def numbering(extra, slots, width):
    numbers = extra[slots : slots + 1, :LANES]
    nodes = lax.broadcasted_iota(jnp.int32, (width, LANES), 0).astype(jnp.float32)
    return jnp.where(nodes == numbers, 1.0, 0.0)[:, : extra.shape[0]]


def partial_sums(forces, extra, slots, scalars, coarse_size, width):
    out = 0.0
    for x, rows in zip(forces, extra):
        out = out + exact(x, rows, LAST)
    out = exact(out, numbering(extra[0], slots, width), LAST)
    for i, value in enumerate(scalars):
        out = out + jnp.where(lane_is(out.shape, coarse_size + i), value, 0.0)
    return out


def coarse_solve(right, inverse):
    lowered = exact(right, inverse, LAST)
    return exact(lowered, inverse), jnp.sum(lowered * lowered, axis=1, keepdims=True)


def coarse_part(sums, coarse_size):
    lanes = lax.broadcasted_iota(jnp.int32, sums.shape, 1)
    return jnp.where(lanes < coarse_size, sums, 0.0)


def two_high(x):
    return jnp.concatenate(parts(x, 2), axis=0)


def two_wide(x):
    high, low = parts(x, 2)
    return jnp.concatenate(
        [jnp.concatenate([high, high], axis=1), jnp.concatenate([low, low], axis=1)], axis=0
    )


def coarse_times(coarse, image):
    rows = coarse.shape[0]
    both = mxu(two_wide(coarse), image)
    return both[:rows] + both[rows:]


def prepare_kernel(coupling_ref, corners_ref, loads_ref, match_ref, schur_ref,
                   loads_out, extra_out, hots_out, schur_out, match_held, sems):
    copies = [
        pltpu.make_async_copy(x, y, sems.at[i])
        for i, (x, y) in enumerate(
            ((match_ref, match_held), (loads_ref, loads_out), (schur_ref, schur_out))
        )
    ]
    for copy in copies:
        copy.start()
    size = loads_ref.shape[1] // 4
    slots = coupling_ref.shape[0]
    extra_out[slots:, :] = jnp.full((extra_out.shape[0] - slots, 4 * size), -1.0, jnp.float32)
    corners = corners_ref[...].astype(jnp.float32)
    for i in range(4):
        extra_out[slots : slots + 1, i * size : i * size + slots] = corners
    copies[0].wait()
    for i in range(4):
        hots_out[i * size : (i + 1) * size, :] = one_hot(match_held, i)
    coupling = faces_of(coupling_ref, size)
    for i in (0, 2):
        coupling[i] = turn(coupling[i], hots_out[i * size : (i + 1) * size, :])
    for i in range(4):
        extra_out[:slots, i * size : (i + 1) * size] = coupling[i]
    copies[1].wait()
    for i in (0, 2):
        block = slice(i * size, (i + 1) * size)
        loads_out[:, block] = turn(loads_out[:, block], hots_out[block, :])
    copies[2].wait()


def first_kernel(near0, near1, near2, near3, loads_ref, extra_ref, hots_ref, schur_ref,
                 residual_ref, send0, send1, send2, send3, result_ref):
    cases = loads_ref.shape[0]
    size = loads_ref.shape[1] // 4
    hots = hots_of(hots_ref)
    near = [
        near0[...],
        reorder(near1[...], hots[1], PLAIN),
        near2[...],
        reorder(near3[...], hots[3], PLAIN),
    ]
    residual = jump(near, faces_of(loads_ref, size))
    store(residual_ref, residual)
    product(schur_ref, result_ref, local_order(weighted(residual), hots, 1), [(0, cases, 1)])
    extra = faces_of(extra_ref, size)
    for i, (ref, value) in enumerate(
        zip((send0, send1, send2, send3), turned_result(result_ref, hots))
    ):
        ref[:cases, :] = value
        ref[cases:, :] = extra[i]


def coarse_kernel(own_ref, near0, near1, near2, near3, residual_ref, hots_ref, schur_ref,
                  image_ref, response_ref, low_ref, result_ref):
    width = image_ref.shape[0] // 2
    cases = low_ref.shape[0]
    size = hots_ref.shape[1]
    slots = own_ref.shape[0] - 4
    hots = hots_of(hots_ref)
    own = faces_of(own_ref, size)
    near = [x[cases:, :] for x in (near0, near1, near2, near3)]
    own = [exact(numbering(x, slots, width), x) for x in own]
    near = [exact(numbering(x, slots, width), x) for x in near]
    image = jump(near, own)
    store(image_ref, [two_high(x) for x in image])
    left = local_order(weighted(image), hots, 2)
    rest = weighted(faces_of(residual_ref, size))
    rest = [x - x.astype(jnp.bfloat16).astype(jnp.float32) for x in rest]
    left = jnp.concatenate([left, local_order(rest, hots, 1)], axis=0)
    product(schur_ref, result_ref, left, [(0, width, 2), (2 * width, cases, 1)])
    response = turned_result(result_ref, hots)
    store(response_ref, [two_high(x[:width]) for x in response])
    store(low_ref, [x[width:] for x in response])


def direction_kernel(coarse_size, count, *refs):
    own = refs[0:4]
    near = refs[4:8]
    extra_ref, residual_ref, hots_ref, flex_ref = refs[8:12]
    n = 12
    if count > 1:
        before_ref = refs[12]
        before_free = refs[13:17]
        n = 17
    precond_ref, free0, free1, free2, free3, sums_ref, result_ref = refs[n:]
    size = own[0].shape[1]
    cases = residual_ref.shape[0]
    slots = extra_ref.shape[0] - 4
    hots = hots_of(hots_ref)
    precond = jump([x[:cases, :] for x in near], [x[:cases, :] for x in own])
    precond = [0.5 * x for x in precond]
    store(precond_ref, precond)
    forces = signed(precond)
    product(flex_ref, result_ref, local_order(forces, hots, count), [(0, cases, count)])
    free = turned_result(result_ref, hots)
    for ref, value in zip((free0, free1, free2, free3), free):
        ref[...] = value
    scalars = [0.5 * total(faces_of(residual_ref, size), precond), total(forces, free)]
    if count > 1:
        before = signed(faces_of(before_ref, size))
        scalars.append(total(forces, [x[...] for x in before_free]) + total(before, free))
    sums_ref[...] = partial_sums(
        forces, faces_of(extra_ref, size), slots, scalars, coarse_size, sums_ref.shape[1]
    )


def image_kernel(own0, own1, own2, own3, near0, near1, near2, near3, hots_ref, schur_ref,
                 jump_ref, response_ref, result_ref):
    cases = own0.shape[0]
    hots = hots_of(hots_ref)
    moved = jump(
        [x[...] for x in (near0, near1, near2, near3)], [x[...] for x in (own0, own1, own2, own3)]
    )
    store(jump_ref, moved)
    product(schur_ref, result_ref, local_order(weighted(moved), hots, 2), [(0, cases, 2)])
    store(response_ref, turned_result(result_ref, hots))


def step_kernel(coarse_size, sums_ref, inverse_ref, coarse_response_ref, image_response_ref,
                low_ref, own0, own1, own2, own3, step_ref, coarse_ref, send0, send1, send2, send3):
    size = own0.shape[1]
    sums = sums_ref[...]
    coarse, energy = coarse_solve(coarse_part(sums, coarse_size), inverse_ref[...])
    step = pick(sums, coarse_size) / (pick(sums, coarse_size + 1) + energy)
    step_ref[...] = jnp.broadcast_to(step, step_ref.shape)
    coarse_ref[...] = coarse
    change = coarse_times(coarse, coarse_response_ref[...]) + image_response_ref[...]
    own = (own0, own1, own2, own3)
    for i, send in enumerate((send0, send1, send2, send3)):
        block = slice(i * size, (i + 1) * size)
        send[...] = own[i][: sums.shape[0], :] + low_ref[:, block] - step * change[:, block]


def residual_kernel(residual_ref, jump_ref, image_ref, step_ref, coarse_ref, new_ref):
    image = jump_ref[...] + coarse_times(coarse_ref[...], image_ref[...])
    new_ref[...] = residual_ref[...] - step_ref[:, 0:1] * image


def home_kernel(residual_ref, before_ref, precond_ref, jump_ref, image_ref, hots_ref,
                own0, own1, own2, own3, near0, near1, near2, near3,
                residual_out, before_out, precond_out, jump_out, image_out, next_out):
    size = own0.shape[1]
    hots = hots_of(hots_ref)
    moved = jump(
        [x[...] for x in (near0, near1, near2, near3)], [x[...] for x in (own0, own1, own2, own3)]
    )
    fields = [faces_of(x, size) for x in (residual_ref, before_ref, precond_ref, jump_ref)]
    image = faces_of(image_ref, size)
    for i in (0, 2):
        image[i] = mxu(image[i], hots[i]).astype(jnp.bfloat16)
        for field in [*fields, moved]:
            field[i] = turn_back(field[i], hots[i])
    store(image_out, image)
    for ref, field in zip(
        (residual_out, before_out, precond_out, jump_out, next_out), [*fields, moved]
    ):
        store(ref, field)


def last_kernel(coarse_size, first_ref, sums_ref, inverse_ref, step_ref, residual_ref, before_ref,
                precond_ref, jump_ref, image_ref, next_ref, multipliers_ref, out_ref):
    size = residual_ref.shape[1] // 4
    first = first_ref[...]
    sums = sums_ref[...]
    beta = pick(sums, coarse_size) / pick(first, coarse_size)
    right = coarse_part(sums, coarse_size) + beta * coarse_part(first, coarse_size)
    coarse, energy = coarse_solve(right, inverse_ref[...])
    local = pick(sums, coarse_size + 1) + beta * (
        pick(sums, coarse_size + 2) + beta * pick(first, coarse_size + 1)
    )
    step = pick(sums, coarse_size) / (local + energy)
    step_before = step_ref[:, 0:1]
    image = coarse_times(coarse, image_ref[...])
    for i in range(4):
        block = slice(i * size, (i + 1) * size)
        moved = next_ref[:, block] + beta * jump_ref[:, block] + image[:, block]
        out_ref[:, i, :] = residual_ref[:, block] - step * moved
        before = before_ref[:, block]
        direction = precond_ref[:, block] + beta * before
        multipliers_ref[:, i, :] = step_before * before + step * direction


VMEM = pl.BlockSpec(memory_space=pltpu.VMEM)
OUTSIDE = pl.BlockSpec(memory_space=pltpu.HBM)


def call(kernel, args, outs, scratch=(), outside=(), flops=0):
    specs = [OUTSIDE if i in outside else VMEM for i in range(len(args))]
    shapes = [(x, jnp.float32) if isinstance(x[0], int) else x for x in outs]
    return pl.pallas_call(
        kernel,
        in_specs=specs,
        out_specs=[VMEM] * len(outs),
        out_shape=[jax.ShapeDtypeStruct(*x) for x in shapes],
        scratch_shapes=list(scratch),
        compiler_params=pltpu.CompilerParams(vmem_limit_bytes=28 * 2**20),
        cost_estimate=pl.CostEstimate(flops=flops, bytes_accessed=2**22, transcendentals=0),
    )(*args)


def shards(
    applied_loads,
    flex_matrix,
    schur_matrix,
    corner_coupling,
    coarse_inverse,
    face_match,
    corner_map,
):
    loads = applied_loads[0, 0]
    flex = flex_matrix[0, 0]
    schur = schur_matrix[0, 0]
    match = face_match[0, 0]
    cases, interface = loads.shape
    size = interface // 4
    slots = corner_coupling.shape[2]
    coarse_size = coarse_inverse.shape[0]
    width = -(-(coarse_size + 3) // LANES) * LANES
    work = 2 * cases * interface * interface

    inverse = jnp.pad(coarse_inverse, ((0, width - coarse_size), (0, width - coarse_size)))
    field = (cases, interface)
    face = (cases, size)
    result = pltpu.VMEM(field, jnp.float32)
    both_parts = ((2 * width, interface), jnp.bfloat16)

    held = [pltpu.with_memory_space_constraint(x, pltpu.HBM) for x in (loads, match, schur)]
    near = exchange([loads[:, i * size : (i + 1) * size] for i in range(4)])
    loads, extra, hots, schur = call(
        prepare_kernel,
        [corner_coupling[0, 0], corner_map[0], *held],
        [
            field,
            (slots + 4, interface),
            ((4 * size, size), jnp.bfloat16),
            (schur.shape, jnp.bfloat16),
        ],
        [pltpu.VMEM(match.shape, jnp.int32), pltpu.SemaphoreType.DMA((3,))],
        outside=(2, 3, 4),
        flops=work,
    )
    residual, *own_first = call(
        first_kernel,
        [*near, loads, extra, hots, schur],
        [field] + [(cases + slots + 4, size)] * 4,
        [result],
        flops=work,
    )
    near_first = exchange(own_first)
    before, *own_free, sums = call(
        functools.partial(direction_kernel, coarse_size, 1),
        [*own_first, *near_first, extra, residual, hots, flex],
        [field] + [face] * 4 + [(cases, width)],
        [result],
        flops=work,
    )
    near = exchange(own_free)
    sums = sum_over(sums, "grp")
    coarse_fields = call(
        coarse_kernel,
        [extra, *near_first, residual, hots, schur],
        [both_parts, both_parts, field],
        [pltpu.VMEM((cases + width, interface), jnp.float32)],
        flops=work,
    )
    sums, image, coarse_response, low = lax.optimization_barrier((sums, *coarse_fields))
    first_sums = sum_over(sums, "sub")
    moved, response = call(
        image_kernel, [*own_free, *near, hots, schur], [field, field], [result], flops=work
    )
    step, coarse, *own = call(
        functools.partial(step_kernel, coarse_size),
        [first_sums, inverse, coarse_response, response, low, *own_first],
        [(cases, LANES), (cases, width)] + [face] * 4,
        flops=work // 4,
    )
    near = exchange(own)
    (residual,) = call(residual_kernel, [residual, moved, image, step, coarse], [field], flops=work // 4)
    precond, *own, sums = call(
        functools.partial(direction_kernel, coarse_size, 2),
        [*own, *near, extra, residual, hots, flex, before, *own_free],
        [field] + [face] * 4 + [(cases, width)],
        [result],
        flops=work,
    )
    near = exchange(own)
    sums = sum_over(sum_over(sums, "grp"), "sub")
    fields = call(
        home_kernel,
        [residual, before, precond, moved, image, hots, *own, *near],
        [field] * 4 + [both_parts, field],
        flops=work // 2,
    )
    layout = (cases, 4, size)
    multipliers, residual = call(
        functools.partial(last_kernel, coarse_size),
        [first_sums, sums, inverse, step, *fields],
        [layout, layout],
        flops=work // 4,
    )
    return multipliers[None, None], residual[None, None]


def solution(mesh):
    return jax.shard_map(
        shards,
        mesh=mesh,
        in_specs=(
            P("sub", "grp", None, None),
            P("sub", "grp", None, None),
            P("sub", "grp", None, None),
            P("sub", "grp", None, None),
            P(),
            P("sub", "grp", None, None),
            P("sub", "grp", None),
        ),
        out_specs=(P("sub", "grp", None, None, None), P("sub", "grp", None, None, None)),
        check_vma=False,
    )
```

```python
import functools

import jax
import jax.numpy as jnp
from jax import lax
from jax.experimental import pallas as pl
from jax.experimental.pallas import tpu as pltpu
from jax.sharding import PartitionSpec as P

HIGHEST = lax.Precision.HIGHEST
PLAIN = (((1,), (0,)), ((), ()))
LAST = (((1,), (1,)), ((), ()))
LANES = 128
SIGNS = (-1.0, 1.0, -1.0, 1.0)


def odd(axis):
    return lax.axis_index(axis) % 2 == 1


def swapped(faces, odds):
    far, near = [], []
    for (low, high), is_odd in zip((faces[0:2], faces[2:4]), odds):
        far.append(jnp.where(is_odd, high, low))
        near.append(jnp.where(is_odd, low, high))
    return far + near


def exchange(faces):
    received = []
    for i, axis in enumerate(("sub", "grp", "sub", "grp")):
        peers = lax.axis_size(axis)
        if i < 2:
            pairs = [(j, (j + 2 * (j % 2) - 1) % peers) for j in range(peers)]
        else:
            pairs = [(j, j ^ 1) for j in range(peers)]
        received.append(lax.ppermute(faces[i], axis, pairs))
    return received


def sum_grp(values, beside=()):
    peers = lax.axis_size("grp")
    values = values + lax.ppermute(values, "grp", [(i, i ^ 1) for i in range(peers)])
    step = 2
    while step < peers:
        values = values + lax.ppermute(values, "grp", [(i, i ^ step) for i in range(1, peers, 2)])
        if step == 2 and beside:
            values, *beside = lax.optimization_barrier((values, *beside))
        step *= 2
    return values, *beside


def sum_sub(values):
    peers, width = lax.axis_size("sub"), lax.axis_size("grp")
    step = 1
    while step < peers:
        pairs = [
            (i * width + j, (i ^ step) * width + j)
            for i in range(peers)
            for j in range(1, width, 2)
        ]
        values = values + lax.ppermute(values, ("sub", "grp"), pairs)
        step *= 2
    return values, lax.ppermute(values, "grp", [(j, j - 1) for j in range(1, width, 2)])


def one_hot(match_ref, i):
    row = match_ref[i : i + 1, :]
    size = row.shape[1]
    nodes = lax.broadcasted_iota(jnp.int32, (size, size), 0)
    return jnp.where(nodes == row, 1.0, 0.0).astype(jnp.bfloat16)


def parts(x, count):
    out = []
    for _ in range(count):
        part = x.astype(jnp.bfloat16)
        out.append(part)
        x = x - part.astype(jnp.float32)
    return out


def mxu(x, y, dims=PLAIN):
    return lax.dot_general(x, y, dims, preferred_element_type=jnp.float32)


def exact(x, y, dims=PLAIN):
    return lax.dot_general(x, y, dims, precision=HIGHEST, preferred_element_type=jnp.float32)


def reorder(x, hot, dims):
    rows = x.shape[0]
    both = mxu(jnp.concatenate(parts(x, 3), axis=0), hot, dims)
    return both[:rows] + both[rows : 2 * rows] + both[2 * rows :]


def turn(x, hot):
    return reorder(x, hot, LAST)


def turn_back(x, hot):
    return reorder(x, hot, PLAIN)


def jump(received, own):
    return [
        received[0] - own[0],
        own[1] - received[1],
        received[2] - own[2],
        own[3] - received[3],
    ]


def odds():
    return odd("sub"), odd("grp")


def faces_in(values):
    out = []
    for far, near, is_odd in zip(values[0:2], values[2:4], odds()):
        out += [jnp.where(is_odd, near, far), jnp.where(is_odd, far, near)]
    return out


def faces_of(ref, size):
    return [ref[:, i * size : (i + 1) * size] for i in range(4)]


def store(ref, faces):
    size = faces[0].shape[1]
    for i in range(4):
        ref[:, i * size : (i + 1) * size] = faces[i]


def total(xs, ys):
    return sum(jnp.sum(x * y, axis=1, keepdims=True) for x, y in zip(xs, ys))


def blocks_of(interface):
    width = 256 if interface % 256 == 0 else interface
    return [slice(i, i + width) for i in range(0, interface, width)]


def product(matrix_ref, result_ref, left, groups):
    for block in blocks_of(matrix_ref.shape[1]):
        both = mxu(left, matrix_ref[:, block])
        at = 0
        for first, rows, count in groups:
            value = both[first : first + rows]
            for i in range(1, count):
                value = value + both[first + i * rows : first + (i + 1) * rows]
            result_ref[at : at + rows, block] = value
            at += rows


def local_order(faces, hots, count):
    split = [jnp.concatenate(parts(x, count), axis=0) for x in faces]
    split[0] = mxu(split[0], hots[0]).astype(jnp.bfloat16)
    split[2] = mxu(split[2], hots[2]).astype(jnp.bfloat16)
    return jnp.concatenate(split, axis=1)


def turned_result(result_ref, hots):
    size = result_ref.shape[1] // 4
    own = faces_of(result_ref, size)
    own[0] = turn(own[0], hots[0])
    own[2] = turn(own[2], hots[2])
    return own


def weighted(faces):
    return [(0.5 * s) * x for s, x in zip(SIGNS, faces)]


def hots_of(hots_ref):
    size = hots_ref.shape[1]
    return [hots_ref[i * size : (i + 1) * size, :] for i in range(4)]


def signed(faces):
    return [s * x for s, x in zip(SIGNS, faces)]


def lane_is(shape, lane):
    return lax.broadcasted_iota(jnp.int32, shape, 1) == lane


def pick(values, lane):
    return jnp.sum(jnp.where(lane_is(values.shape, lane), values, 0.0), axis=1, keepdims=True)


def numbering(extra, slots, width):
    numbers = extra[slots : slots + 1, :LANES]
    nodes = lax.broadcasted_iota(jnp.int32, (width, LANES), 0).astype(jnp.float32)
    return jnp.where(nodes == numbers, 1.0, 0.0)[:, : extra.shape[0]]


def partial_sums(forces, extra, slots, scalars, coarse_size, width):
    out = 0.0
    for x, rows in zip(forces, extra):
        out = out + exact(x, rows, LAST)
    out = exact(out, numbering(extra[0], slots, width), LAST)
    for i, value in enumerate(scalars):
        out = out + jnp.where(lane_is(out.shape, coarse_size + i), value, 0.0)
    return out


def coarse_solve(right, inverse):
    lowered = exact(right, inverse, LAST)
    return exact(lowered, inverse), jnp.sum(lowered * lowered, axis=1, keepdims=True)


def coarse_part(sums, coarse_size):
    lanes = lax.broadcasted_iota(jnp.int32, sums.shape, 1)
    return jnp.where(lanes < coarse_size, sums, 0.0)


def two_high(x):
    return jnp.concatenate(parts(x, 2), axis=0)


def two_wide(x):
    high, low = parts(x, 2)
    return jnp.concatenate(
        [jnp.concatenate([high, high], axis=1), jnp.concatenate([low, low], axis=1)], axis=0
    )


def coarse_times(coarse, image):
    rows = coarse.shape[0]
    both = mxu(two_wide(coarse), image)
    return both[:rows] + both[rows:]


def prepare_kernel(coupling_ref, corners_ref, loads_ref, match_ref, schur_ref,
                   loads_out, extra_out, hots_out, schur_out, match_held, sems):
    copies = [
        pltpu.make_async_copy(x, y, sems.at[i])
        for i, (x, y) in enumerate(
            ((match_ref, match_held), (loads_ref, loads_out), (schur_ref, schur_out))
        )
    ]
    for copy in copies:
        copy.start()
    size = loads_ref.shape[1] // 4
    slots = coupling_ref.shape[0]
    extra_out[slots:, :] = jnp.full((extra_out.shape[0] - slots, 4 * size), -1.0, jnp.float32)
    corners = corners_ref[...].astype(jnp.float32)
    for i in range(4):
        extra_out[slots : slots + 1, i * size : i * size + slots] = corners
    copies[0].wait()
    for i in range(4):
        hots_out[i * size : (i + 1) * size, :] = one_hot(match_held, i)
    coupling = faces_of(coupling_ref, size)
    for i in (0, 2):
        coupling[i] = turn(coupling[i], hots_out[i * size : (i + 1) * size, :])
    for i in range(4):
        extra_out[:slots, i * size : (i + 1) * size] = coupling[i]
    copies[1].wait()
    for i in (0, 2):
        block = slice(i * size, (i + 1) * size)
        loads_out[:, block] = turn(loads_out[:, block], hots_out[block, :])
    copies[2].wait()


def first_kernel(near0, near1, near2, near3, loads_ref, extra_ref, hots_ref, schur_ref,
                 residual_ref, send0, send1, send2, send3, result_ref):
    cases = loads_ref.shape[0]
    size = loads_ref.shape[1] // 4
    hots = hots_of(hots_ref)
    near = faces_in([x[...] for x in (near0, near1, near2, near3)])
    for i in (1, 3):
        near[i] = reorder(near[i], hots[i], PLAIN)
    residual = jump(near, faces_of(loads_ref, size))
    store(residual_ref, residual)
    product(schur_ref, result_ref, local_order(weighted(residual), hots, 1), [(0, cases, 1)])
    extra = faces_of(extra_ref, size)
    values = swapped(turned_result(result_ref, hots), odds())
    extra = swapped(extra, odds())
    for i, ref in enumerate((send0, send1, send2, send3)):
        ref[:cases, :] = values[i]
        ref[cases:, :] = extra[i]


def coarse_kernel(own_ref, near0, near1, near2, near3, residual_ref, hots_ref, schur_ref,
                  image_ref, response_ref, low_ref, result_ref):
    width = image_ref.shape[0] // 2
    cases = low_ref.shape[0]
    size = hots_ref.shape[1]
    slots = own_ref.shape[0] - 4
    hots = hots_of(hots_ref)
    own = faces_of(own_ref, size)
    near = faces_in([x[cases:, :] for x in (near0, near1, near2, near3)])
    own = [exact(numbering(x, slots, width), x) for x in own]
    near = [exact(numbering(x, slots, width), x) for x in near]
    image = jump(near, own)
    store(image_ref, [two_high(x) for x in image])
    left = local_order(weighted(image), hots, 2)
    rest = weighted(faces_of(residual_ref, size))
    rest = [x - x.astype(jnp.bfloat16).astype(jnp.float32) for x in rest]
    left = jnp.concatenate([left, local_order(rest, hots, 1)], axis=0)
    product(schur_ref, result_ref, left, [(0, width, 2), (2 * width, cases, 1)])
    response = turned_result(result_ref, hots)
    store(response_ref, [two_high(x[:width]) for x in response])
    store(low_ref, [x[width:] for x in response])


def direction_kernel(coarse_size, count, *refs):
    own = refs[0:4]
    near = refs[4:8]
    extra_ref, residual_ref, hots_ref, flex_ref = refs[8:12]
    n = 12
    if count > 1:
        before_ref = refs[12]
        before_free = refs[13:17]
        n = 17
    precond_ref, free0, free1, free2, free3, sums_ref, result_ref = refs[n:]
    size = own[0].shape[1]
    cases = residual_ref.shape[0]
    slots = extra_ref.shape[0] - 4
    hots = hots_of(hots_ref)
    precond = jump(
        faces_in([x[:cases, :] for x in near]), faces_in([x[:cases, :] for x in own])
    )
    precond = [0.5 * x for x in precond]
    store(precond_ref, precond)
    forces = signed(precond)
    product(flex_ref, result_ref, local_order(forces, hots, count), [(0, cases, count)])
    free = turned_result(result_ref, hots)
    for ref, value in zip((free0, free1, free2, free3), swapped(free, odds())):
        ref[...] = value
    scalars = [0.5 * total(faces_of(residual_ref, size), precond), total(forces, free)]
    if count > 1:
        before = signed(faces_of(before_ref, size))
        scalars.append(total(forces, faces_in([x[...] for x in before_free])) + total(before, free))
    sums_ref[...] = partial_sums(
        forces, faces_of(extra_ref, size), slots, scalars, coarse_size, sums_ref.shape[1]
    )


def image_kernel(own0, own1, own2, own3, near0, near1, near2, near3, hots_ref, schur_ref,
                 jump_ref, response_ref, result_ref):
    cases = own0.shape[0]
    hots = hots_of(hots_ref)
    moved = jump(
        faces_in([x[...] for x in (near0, near1, near2, near3)]),
        faces_in([x[...] for x in (own0, own1, own2, own3)]),
    )
    store(jump_ref, moved)
    product(schur_ref, result_ref, local_order(weighted(moved), hots, 2), [(0, cases, 2)])
    store(response_ref, turned_result(result_ref, hots))


def step_kernel(coarse_size, sums_ref, other_ref, inverse_ref, coarse_response_ref, image_response_ref,
                low_ref, own0, own1, own2, own3,
                total_ref, step_ref, coarse_ref, send0, send1, send2, send3):
    size = own0.shape[1]
    sums = jnp.where(odd("grp"), sums_ref[...], other_ref[...])
    total_ref[...] = sums
    coarse, energy = coarse_solve(coarse_part(sums, coarse_size), inverse_ref[...])
    step = pick(sums, coarse_size) / (pick(sums, coarse_size + 1) + energy)
    step_ref[...] = jnp.broadcast_to(step, step_ref.shape)
    coarse_ref[...] = coarse
    change = coarse_times(coarse, coarse_response_ref[...]) + image_response_ref[...]
    change = low_ref[...] - step * change
    change = swapped([change[:, i * size : (i + 1) * size] for i in range(4)], odds())
    for send, own, value in zip(
        (send0, send1, send2, send3), (own0, own1, own2, own3), change
    ):
        send[...] = own[: sums.shape[0], :] + value


def residual_kernel(residual_ref, jump_ref, image_ref, step_ref, coarse_ref, new_ref):
    image = jump_ref[...] + coarse_times(coarse_ref[...], image_ref[...])
    new_ref[...] = residual_ref[...] - step_ref[:, 0:1] * image


def home_kernel(residual_ref, before_ref, precond_ref, jump_ref, image_ref, hots_ref,
                own0, own1, own2, own3, near0, near1, near2, near3,
                residual_out, before_out, precond_out, jump_out, image_out, next_out):
    size = own0.shape[1]
    hots = hots_of(hots_ref)
    moved = jump(
        faces_in([x[...] for x in (near0, near1, near2, near3)]),
        faces_in([x[...] for x in (own0, own1, own2, own3)]),
    )
    fields = [faces_of(x, size) for x in (residual_ref, before_ref, precond_ref, jump_ref)]
    image = faces_of(image_ref, size)
    for i in (0, 2):
        image[i] = mxu(image[i], hots[i]).astype(jnp.bfloat16)
        for field in [*fields, moved]:
            field[i] = turn_back(field[i], hots[i])
    store(image_out, image)
    for ref, field in zip(
        (residual_out, before_out, precond_out, jump_out, next_out), [*fields, moved]
    ):
        store(ref, field)


def last_kernel(coarse_size, first_ref, sums_ref, other_ref, inverse_ref, step_ref, residual_ref, before_ref,
                precond_ref, jump_ref, image_ref, next_ref, multipliers_ref, out_ref):
    size = residual_ref.shape[1] // 4
    first = first_ref[...]
    sums = jnp.where(odd("grp"), sums_ref[...], other_ref[...])
    beta = pick(sums, coarse_size) / pick(first, coarse_size)
    right = coarse_part(sums, coarse_size) + beta * coarse_part(first, coarse_size)
    coarse, energy = coarse_solve(right, inverse_ref[...])
    local = pick(sums, coarse_size + 1) + beta * (
        pick(sums, coarse_size + 2) + beta * pick(first, coarse_size + 1)
    )
    step = pick(sums, coarse_size) / (local + energy)
    step_before = step_ref[:, 0:1]
    image = coarse_times(coarse, image_ref[...])
    for i in range(4):
        block = slice(i * size, (i + 1) * size)
        moved = next_ref[:, block] + beta * jump_ref[:, block] + image[:, block]
        out_ref[:, i, :] = residual_ref[:, block] - step * moved
        before = before_ref[:, block]
        direction = precond_ref[:, block] + beta * before
        multipliers_ref[:, i, :] = step_before * before + step * direction


VMEM = pl.BlockSpec(memory_space=pltpu.VMEM)
OUTSIDE = pl.BlockSpec(memory_space=pltpu.HBM)


def call(kernel, args, outs, scratch=(), outside=(), flops=0):
    specs = [OUTSIDE if i in outside else VMEM for i in range(len(args))]
    shapes = [(x, jnp.float32) if isinstance(x[0], int) else x for x in outs]
    return pl.pallas_call(
        kernel,
        in_specs=specs,
        out_specs=[VMEM] * len(outs),
        out_shape=[jax.ShapeDtypeStruct(*x) for x in shapes],
        scratch_shapes=list(scratch),
        compiler_params=pltpu.CompilerParams(vmem_limit_bytes=28 * 2**20),
        cost_estimate=pl.CostEstimate(flops=flops, bytes_accessed=2**22, transcendentals=0),
    )(*args)


def shards(
    applied_loads,
    flex_matrix,
    schur_matrix,
    corner_coupling,
    coarse_inverse,
    face_match,
    corner_map,
):
    loads = applied_loads[0, 0]
    flex = flex_matrix[0, 0]
    schur = schur_matrix[0, 0]
    match = face_match[0, 0]
    cases, interface = loads.shape
    size = interface // 4
    slots = corner_coupling.shape[2]
    coarse_size = coarse_inverse.shape[0]
    width = -(-(coarse_size + 3) // LANES) * LANES
    work = 2 * cases * interface * interface

    inverse = jnp.pad(coarse_inverse, ((0, width - coarse_size), (0, width - coarse_size)))
    field = (cases, interface)
    face = (cases, size)
    result = pltpu.VMEM(field, jnp.float32)
    both_parts = ((2 * width, interface), jnp.bfloat16)

    held = [pltpu.with_memory_space_constraint(x, pltpu.HBM) for x in (loads, match, schur)]
    near = exchange(
        swapped([loads[:, i * size : (i + 1) * size] for i in range(4)], (odd("sub"), odd("grp")))
    )
    loads, extra, hots, schur = call(
        prepare_kernel,
        [corner_coupling[0, 0], corner_map[0], *held],
        [
            field,
            (slots + 4, interface),
            ((4 * size, size), jnp.bfloat16),
            (schur.shape, jnp.bfloat16),
        ],
        [pltpu.VMEM(match.shape, jnp.int32), pltpu.SemaphoreType.DMA((3,))],
        outside=(2, 3, 4),
        flops=work,
    )
    residual, *own_first = call(
        first_kernel,
        [*near, loads, extra, hots, schur],
        [field] + [(cases + slots + 4, size)] * 4,
        [result],
        flops=work,
    )
    near_first = exchange(own_first)
    before, *own_free, sums = call(
        functools.partial(direction_kernel, coarse_size, 1),
        [*own_first, *near_first, extra, residual, hots, flex],
        [field] + [face] * 4 + [(cases, width)],
        [result],
        flops=work,
    )
    near = exchange(own_free)
    coarse_fields = call(
        coarse_kernel,
        [extra, *near_first, residual, hots, schur],
        [both_parts, both_parts, field],
        [pltpu.VMEM((cases + width, interface), jnp.float32)],
        flops=work,
    )
    sums, image, coarse_response, low = sum_grp(sums, coarse_fields)
    first_sums = sum_sub(sums)
    moved, response = call(
        image_kernel, [*own_free, *near, hots, schur], [field, field], [result], flops=work
    )
    first_sums, step, coarse, *own = call(
        functools.partial(step_kernel, coarse_size),
        [*first_sums, inverse, coarse_response, response, low, *own_first],
        [(cases, width), (cases, LANES), (cases, width)] + [face] * 4,
        flops=work // 4,
    )
    near = exchange(own)
    (residual,) = call(residual_kernel, [residual, moved, image, step, coarse], [field], flops=work // 4)
    precond, *own, sums = call(
        functools.partial(direction_kernel, coarse_size, 2),
        [*own, *near, extra, residual, hots, flex, before, *own_free],
        [field] + [face] * 4 + [(cases, width)],
        [result],
        flops=work,
    )
    near = exchange(own)
    sums = sum_sub(*sum_grp(sums))
    fields = call(
        home_kernel,
        [residual, before, precond, moved, image, hots, *own, *near],
        [field] * 4 + [both_parts, field],
        flops=work // 2,
    )
    layout = (cases, 4, size)
    multipliers, residual = call(
        functools.partial(last_kernel, coarse_size),
        [first_sums, *sums, inverse, step, *fields],
        [layout, layout],
        flops=work // 4,
    )
    return multipliers[None, None], residual[None, None]


def solution(mesh):
    return jax.shard_map(
        shards,
        mesh=mesh,
        in_specs=(
            P("sub", "grp", None, None),
            P("sub", "grp", None, None),
            P("sub", "grp", None, None),
            P("sub", "grp", None, None),
            P(),
            P("sub", "grp", None, None),
            P("sub", "grp", None),
        ),
        out_specs=(P("sub", "grp", None, None, None), P("sub", "grp", None, None, None)),
        check_vma=False,
    )
```

```python
import functools

import jax
import jax.numpy as jnp
from jax import lax
from jax.experimental import pallas as pl
from jax.experimental.pallas import tpu as pltpu
from jax.sharding import PartitionSpec as P

HIGHEST = lax.Precision.HIGHEST
PLAIN = (((1,), (0,)), ((), ()))
LAST = (((1,), (1,)), ((), ()))
LANES = 128
SIGNS = (-1.0, 1.0, -1.0, 1.0)


def odd(axis):
    return lax.axis_index(axis) % 2 == 1


def swapped(faces, odds):
    far, near = [], []
    for (low, high), is_odd in zip((faces[0:2], faces[2:4]), odds):
        far.append(jnp.where(is_odd, high, low))
        near.append(jnp.where(is_odd, low, high))
    return far + near


def swap(face, i):
    axis = ("sub", "grp", "sub", "grp")[i]
    peers = lax.axis_size(axis)
    if i < 2:
        pairs = [(j, (j + 2 * (j % 2) - 1) % peers) for j in range(peers)]
    else:
        pairs = [(j, j ^ 1) for j in range(peers)]
    return lax.ppermute(face, axis, pairs)


def exchange(faces):
    return [swap(face, i) for i, face in enumerate(faces)]


def sum_over(values, axis, first):
    peers = lax.axis_size(axis)
    step, count = 1, first
    while step < peers:
        if step * count > peers:
            count = 2
        others = [
            lax.ppermute(values, axis, [(i, i ^ (k * step)) for i in range(peers)])
            for k in range(1, count)
        ]
        values = values + others[0]
        if count == 4:
            values = values + (others[1] + others[2])
        step *= count
        count = 4
    return values


def sum_and_exchange(values, faces):
    far = [swap(face, i) for i, face in enumerate(faces[:2])]
    values = sum_over(values, "grp", 2)
    values, *faces = lax.optimization_barrier((values, *far, *faces[2:]))
    near = [swap(face, i) for i, face in enumerate(faces[2:], 2)]
    return sum_over(values, "sub", 4), faces[:2] + near


def one_hot(match_ref, i):
    row = match_ref[i : i + 1, :]
    size = row.shape[1]
    nodes = lax.broadcasted_iota(jnp.int32, (size, size), 0)
    return jnp.where(nodes == row, 1.0, 0.0).astype(jnp.bfloat16)


def parts(x, count):
    out = []
    for _ in range(count):
        part = x.astype(jnp.bfloat16)
        out.append(part)
        x = x - part.astype(jnp.float32)
    return out


def mxu(x, y, dims=PLAIN):
    return lax.dot_general(x, y, dims, preferred_element_type=jnp.float32)


def exact(x, y, dims=PLAIN):
    return lax.dot_general(x, y, dims, precision=HIGHEST, preferred_element_type=jnp.float32)


def reorder(x, hot, dims):
    rows = x.shape[0]
    both = mxu(jnp.concatenate(parts(x, 3), axis=0), hot, dims)
    return both[:rows] + both[rows : 2 * rows] + both[2 * rows :]


def turn(x, hot):
    return reorder(x, hot, LAST)


def turn_back(x, hot):
    return reorder(x, hot, PLAIN)


def jump(received, own):
    return [
        received[0] - own[0],
        own[1] - received[1],
        received[2] - own[2],
        own[3] - received[3],
    ]


def odds():
    return odd("sub"), odd("grp")


def faces_in(values):
    out = []
    for far, near, is_odd in zip(values[0:2], values[2:4], odds()):
        out += [jnp.where(is_odd, near, far), jnp.where(is_odd, far, near)]
    return out


def faces_of(ref, size):
    return [ref[:, i * size : (i + 1) * size] for i in range(4)]


def store(ref, faces):
    size = faces[0].shape[1]
    for i in range(4):
        ref[:, i * size : (i + 1) * size] = faces[i]


def total(xs, ys):
    return sum(jnp.sum(x * y, axis=1, keepdims=True) for x, y in zip(xs, ys))


def blocks_of(interface):
    width = 256 if interface % 256 == 0 else interface
    return [slice(i, i + width) for i in range(0, interface, width)]


def product(matrix_ref, result_ref, left, groups):
    for block in blocks_of(matrix_ref.shape[1]):
        both = mxu(left, matrix_ref[:, block])
        at = 0
        for first, rows, count in groups:
            value = both[first : first + rows]
            for i in range(1, count):
                value = value + both[first + i * rows : first + (i + 1) * rows]
            result_ref[at : at + rows, block] = value
            at += rows


def local_order(faces, hots, count):
    split = [jnp.concatenate(parts(x, count), axis=0) for x in faces]
    split[0] = mxu(split[0], hots[0]).astype(jnp.bfloat16)
    split[2] = mxu(split[2], hots[2]).astype(jnp.bfloat16)
    return jnp.concatenate(split, axis=1)


def turned_result(result_ref, hots):
    size = result_ref.shape[1] // 4
    own = faces_of(result_ref, size)
    own[0] = turn(own[0], hots[0])
    own[2] = turn(own[2], hots[2])
    return own


def weighted(faces):
    return [(0.5 * s) * x for s, x in zip(SIGNS, faces)]


def hots_of(hots_ref):
    size = hots_ref.shape[1]
    return [hots_ref[i * size : (i + 1) * size, :] for i in range(4)]


def signed(faces):
    return [s * x for s, x in zip(SIGNS, faces)]


def lane_is(shape, lane):
    return lax.broadcasted_iota(jnp.int32, shape, 1) == lane


def pick(values, lane):
    return jnp.sum(jnp.where(lane_is(values.shape, lane), values, 0.0), axis=1, keepdims=True)


def numbering(extra, slots, width):
    numbers = extra[slots : slots + 1, :LANES]
    nodes = lax.broadcasted_iota(jnp.int32, (width, LANES), 0).astype(jnp.float32)
    return jnp.where(nodes == numbers, 1.0, 0.0)[:, : extra.shape[0]]


def partial_sums(forces, extra, slots, scalars, coarse_size, width):
    out = 0.0
    for x, rows in zip(forces, extra):
        out = out + exact(x, rows, LAST)
    out = exact(out, numbering(extra[0], slots, width), LAST)
    for i, value in enumerate(scalars):
        out = out + jnp.where(lane_is(out.shape, coarse_size + i), value, 0.0)
    return out


def coarse_solve(right, inverse):
    lowered = exact(right, inverse, LAST)
    return exact(lowered, inverse), jnp.sum(lowered * lowered, axis=1, keepdims=True)


def coarse_part(sums, coarse_size):
    lanes = lax.broadcasted_iota(jnp.int32, sums.shape, 1)
    return jnp.where(lanes < coarse_size, sums, 0.0)


def two_high(x):
    return jnp.concatenate(parts(x, 2), axis=0)


def two_wide(x):
    high, low = parts(x, 2)
    return jnp.concatenate(
        [jnp.concatenate([high, high], axis=1), jnp.concatenate([low, low], axis=1)], axis=0
    )


def coarse_times(coarse, image):
    rows = coarse.shape[0]
    both = mxu(two_wide(coarse), image)
    return both[:rows] + both[rows:]


def prepare_kernel(loads_ref, match_ref, schur_ref,
                   loads_out, hots_out, schur_out, match_held, sems):
    copies = [
        pltpu.make_async_copy(x, y, sems.at[i])
        for i, (x, y) in enumerate(
            ((match_ref, match_held), (loads_ref, loads_out), (schur_ref, schur_out))
        )
    ]
    for copy in copies:
        copy.start()
    size = loads_ref.shape[1] // 4
    copies[0].wait()
    for i in range(4):
        hots_out[i * size : (i + 1) * size, :] = one_hot(match_held, i)
    copies[1].wait()
    for i in (0, 2):
        block = slice(i * size, (i + 1) * size)
        loads_out[:, block] = turn(loads_out[:, block], hots_out[block, :])
    copies[2].wait()


def extra_kernel(coupling_ref, corners_ref, hots_ref, extra_out):
    size = hots_ref.shape[1]
    slots = coupling_ref.shape[0]
    hots = hots_of(hots_ref)
    extra_out[slots:, :] = jnp.full((extra_out.shape[0] - slots, 4 * size), -1.0, jnp.float32)
    corners = corners_ref[...].astype(jnp.float32)
    coupling = faces_of(coupling_ref, size)
    for i in range(4):
        rows = turn(coupling[i], hots[i]) if i in (0, 2) else coupling[i]
        extra_out[:slots, i * size : (i + 1) * size] = rows
        extra_out[slots : slots + 1, i * size : i * size + slots] = corners


def first_kernel(near0, near1, near2, near3, loads_ref, hots_ref, schur_ref,
                 residual_ref, send0, send1, send2, send3, result_ref):
    cases = loads_ref.shape[0]
    size = loads_ref.shape[1] // 4
    hots = hots_of(hots_ref)
    near = faces_in([x[...] for x in (near0, near1, near2, near3)])
    for i in (1, 3):
        near[i] = reorder(near[i], hots[i], PLAIN)
    residual = jump(near, faces_of(loads_ref, size))
    store(residual_ref, residual)
    product(schur_ref, result_ref, local_order(weighted(residual), hots, 1), [(0, cases, 1)])
    for ref, value in zip(
        (send0, send1, send2, send3), swapped(turned_result(result_ref, hots), odds())
    ):
        ref[...] = value


def coarse_kernel(own_ref, near0, near1, near2, near3, image_ref):
    width = image_ref.shape[0] // 2
    size = near0.shape[1]
    slots = own_ref.shape[0] - 4
    cases = near0.shape[0] - own_ref.shape[0]
    own = faces_of(own_ref, size)
    near = faces_in([x[cases:, :] for x in (near0, near1, near2, near3)])
    own = [exact(numbering(x, slots, width), x) for x in own]
    near = [exact(numbering(x, slots, width), x) for x in near]
    store(image_ref, [two_high(x) for x in jump(near, own)])


def direction_kernel(coarse_size, count, *refs):
    own = refs[0:4]
    near = refs[4:8]
    extra_ref, residual_ref, hots_ref, flex_ref = refs[8:12]
    n = 12
    if count > 1:
        before_ref = refs[12]
        before_free = refs[13:17]
        n = 17
    precond_ref, free0, free1, free2, free3, sums_ref, result_ref = refs[n:]
    size = own[0].shape[1]
    cases = residual_ref.shape[0]
    slots = extra_ref.shape[0] - 4
    hots = hots_of(hots_ref)
    precond = jump(faces_in([x[...] for x in near]), faces_in([x[...] for x in own]))
    precond = [0.5 * x for x in precond]
    store(precond_ref, precond)
    forces = signed(precond)
    product(flex_ref, result_ref, local_order(forces, hots, count), [(0, cases, count)])
    free = turned_result(result_ref, hots)
    extra = faces_of(extra_ref, size)
    for ref, value, rows in zip(
        (free0, free1, free2, free3), swapped(free, odds()), swapped(extra, odds())
    ):
        ref[:cases, :] = value
        if count == 1:
            ref[cases:, :] = rows
    scalars = [0.5 * total(faces_of(residual_ref, size), precond), total(forces, free)]
    if count > 1:
        before = signed(faces_of(before_ref, size))
        scalars.append(total(forces, faces_in([x[:cases, :] for x in before_free])) + total(before, free))
    sums_ref[...] = partial_sums(
        forces, extra, slots, scalars, coarse_size, sums_ref.shape[1]
    )


def step_kernel(coarse_size, sums_ref, inverse_ref, image_ref, own0, own1, own2, own3,
                near0, near1, near2, near3, residual_ref, hots_ref, schur_ref,
                new_ref, jump_ref, step_ref, send0, send1, send2, send3, result_ref):
    size = own0.shape[1]
    cases = sums_ref.shape[0]
    hots = hots_of(hots_ref)
    moved = jump(
        faces_in([x[:cases, :] for x in (near0, near1, near2, near3)]),
        faces_in([x[:cases, :] for x in (own0, own1, own2, own3)]),
    )
    store(jump_ref, moved)
    sums = sums_ref[...]
    coarse, energy = coarse_solve(coarse_part(sums, coarse_size), inverse_ref[...])
    step = pick(sums, coarse_size) / (pick(sums, coarse_size + 1) + energy)
    step_ref[...] = jnp.broadcast_to(step, step_ref.shape)
    image = coarse_times(coarse, image_ref[...])
    residual = [
        residual_ref[:, i * size : (i + 1) * size]
        - step * (moved[i] + image[:, i * size : (i + 1) * size])
        for i in range(4)
    ]
    store(new_ref, residual)
    product(schur_ref, result_ref, local_order(weighted(residual), hots, 1), [(0, cases, 1)])
    for ref, value in zip(
        (send0, send1, send2, send3), swapped(turned_result(result_ref, hots), odds())
    ):
        ref[...] = value


def home_kernel(residual_ref, before_ref, precond_ref, jump_ref, image_ref, hots_ref,
                own0, own1, own2, own3, near0, near1, near2, near3,
                residual_out, before_out, precond_out, jump_out, image_out, next_out):
    size = own0.shape[1]
    hots = hots_of(hots_ref)
    moved = jump(
        faces_in([x[...] for x in (near0, near1, near2, near3)]),
        faces_in([x[...] for x in (own0, own1, own2, own3)]),
    )
    fields = [faces_of(x, size) for x in (residual_ref, before_ref, precond_ref, jump_ref)]
    image = faces_of(image_ref, size)
    for i in (0, 2):
        image[i] = mxu(image[i], hots[i]).astype(jnp.bfloat16)
        for field in [*fields, moved]:
            field[i] = turn_back(field[i], hots[i])
    store(image_out, image)
    for ref, field in zip(
        (residual_out, before_out, precond_out, jump_out, next_out), [*fields, moved]
    ):
        store(ref, field)


def last_kernel(coarse_size, first_ref, sums_ref, inverse_ref, step_ref, residual_ref, before_ref,
                precond_ref, jump_ref, image_ref, next_ref, multipliers_ref, out_ref):
    size = residual_ref.shape[1] // 4
    first = first_ref[...]
    sums = sums_ref[...]
    beta = pick(sums, coarse_size) / pick(first, coarse_size)
    right = coarse_part(sums, coarse_size) + beta * coarse_part(first, coarse_size)
    coarse, energy = coarse_solve(right, inverse_ref[...])
    local = pick(sums, coarse_size + 1) + beta * (
        pick(sums, coarse_size + 2) + beta * pick(first, coarse_size + 1)
    )
    step = pick(sums, coarse_size) / (local + energy)
    step_before = step_ref[:, 0:1]
    image = coarse_times(coarse, image_ref[...])
    for i in range(4):
        block = slice(i * size, (i + 1) * size)
        moved = next_ref[:, block] + beta * jump_ref[:, block] + image[:, block]
        out_ref[:, i, :] = residual_ref[:, block] - step * moved
        before = before_ref[:, block]
        direction = precond_ref[:, block] + beta * before
        multipliers_ref[:, i, :] = step_before * before + step * direction


VMEM = pl.BlockSpec(memory_space=pltpu.VMEM)
OUTSIDE = pl.BlockSpec(memory_space=pltpu.HBM)


def call(kernel, args, outs, scratch=(), outside=(), flops=0):
    specs = [OUTSIDE if i in outside else VMEM for i in range(len(args))]
    shapes = [(x, jnp.float32) if isinstance(x[0], int) else x for x in outs]
    return pl.pallas_call(
        kernel,
        in_specs=specs,
        out_specs=[VMEM] * len(outs),
        out_shape=[jax.ShapeDtypeStruct(*x) for x in shapes],
        scratch_shapes=list(scratch),
        compiler_params=pltpu.CompilerParams(vmem_limit_bytes=28 * 2**20),
        cost_estimate=pl.CostEstimate(flops=flops, bytes_accessed=2**22, transcendentals=0),
    )(*args)


def shards(
    applied_loads,
    flex_matrix,
    schur_matrix,
    corner_coupling,
    coarse_inverse,
    face_match,
    corner_map,
):
    loads = applied_loads[0, 0]
    flex = flex_matrix[0, 0]
    schur = schur_matrix[0, 0]
    match = face_match[0, 0]
    cases, interface = loads.shape
    size = interface // 4
    slots = corner_coupling.shape[2]
    coarse_size = coarse_inverse.shape[0]
    width = -(-(coarse_size + 3) // LANES) * LANES
    work = 2 * cases * interface * interface

    inverse = jnp.pad(coarse_inverse, ((0, width - coarse_size), (0, width - coarse_size)))
    field = (cases, interface)
    face = (cases, size)
    result = pltpu.VMEM(field, jnp.float32)
    both_parts = ((2 * width, interface), jnp.bfloat16)

    held = [pltpu.with_memory_space_constraint(x, pltpu.HBM) for x in (loads, match, schur)]
    near = exchange(
        swapped([loads[:, i * size : (i + 1) * size] for i in range(4)], (odd("sub"), odd("grp")))
    )
    loads, hots, schur = call(
        prepare_kernel,
        held,
        [field, ((4 * size, size), jnp.bfloat16), (schur.shape, jnp.bfloat16)],
        [pltpu.VMEM(match.shape, jnp.int32), pltpu.SemaphoreType.DMA((3,))],
        outside=(0, 1, 2),
        flops=work,
    )
    residual, *own_first = call(
        first_kernel, [*near, loads, hots, schur], [field] + [face] * 4, [result], flops=work
    )
    near = exchange(own_first)
    residual, coupling, corners = lax.optimization_barrier(
        (residual, corner_coupling[0, 0], corner_map[0])
    )
    (extra,) = call(extra_kernel, [coupling, corners, hots], [(slots + 4, interface)], flops=work // 4)
    before, *own_free, sums = call(
        functools.partial(direction_kernel, coarse_size, 1),
        [*own_first, *near, extra, residual, hots, flex],
        [field] + [(cases + slots + 4, size)] * 4 + [(cases, width)],
        [result],
        flops=work,
    )
    first_sums, near = sum_and_exchange(sums, own_free)
    (image,) = call(coarse_kernel, [extra, *near], [both_parts], flops=work // 4)
    residual, moved, step, *own = call(
        functools.partial(step_kernel, coarse_size),
        [first_sums, inverse, image, *own_free, *near, residual, hots, schur],
        [field, field, (cases, LANES)] + [face] * 4,
        [result],
        flops=work,
    )
    near = exchange(own)
    precond, *own, sums = call(
        functools.partial(direction_kernel, coarse_size, 2),
        [*own, *near, extra, residual, hots, flex, before, *own_free],
        [field] + [face] * 4 + [(cases, width)],
        [result],
        flops=work,
    )
    sums, near = sum_and_exchange(sums, own)
    fields = call(
        home_kernel,
        [residual, before, precond, moved, image, hots, *own, *near],
        [field] * 4 + [both_parts, field],
        flops=work // 2,
    )
    layout = (cases, 4, size)
    multipliers, residual = call(
        functools.partial(last_kernel, coarse_size),
        [first_sums, sums, inverse, step, *fields],
        [layout, layout],
        flops=work // 4,
    )
    return multipliers[None, None], residual[None, None]


def solution(mesh):
    return jax.shard_map(
        shards,
        mesh=mesh,
        in_specs=(
            P("sub", "grp", None, None),
            P("sub", "grp", None, None),
            P("sub", "grp", None, None),
            P("sub", "grp", None, None),
            P(),
            P("sub", "grp", None, None),
            P("sub", "grp", None),
        ),
        out_specs=(P("sub", "grp", None, None, None), P("sub", "grp", None, None, None)),
        check_vma=False,
    )
```

```python
import functools

import jax
import jax.numpy as jnp
from jax import lax
from jax.experimental import pallas as pl
from jax.experimental.pallas import tpu as pltpu
from jax.sharding import PartitionSpec as P

HIGHEST = lax.Precision.HIGHEST
PLAIN = (((1,), (0,)), ((), ()))
LAST = (((1,), (1,)), ((), ()))
LANES = 128
SIGNS = (-1.0, 1.0, -1.0, 1.0)


def odd(axis):
    return lax.axis_index(axis) % 2 == 1


def swapped(faces, odds):
    far, near = [], []
    for (low, high), is_odd in zip((faces[0:2], faces[2:4]), odds):
        far.append(jnp.where(is_odd, high, low))
        near.append(jnp.where(is_odd, low, high))
    return far + near


def swap(face, i):
    axis = ("sub", "grp", "sub", "grp")[i]
    peers = lax.axis_size(axis)
    if i < 2:
        pairs = [(j, (j + 2 * (j % 2) - 1) % peers) for j in range(peers)]
    else:
        pairs = [(j, j ^ 1) for j in range(peers)]
    return lax.ppermute(face, axis, pairs)


def exchange(faces):
    return [swap(face, i) for i, face in enumerate(faces)]


def pair_sum(values, axis):
    peers = lax.axis_size(axis)
    return values + lax.ppermute(values, axis, [(i, i ^ 1) for i in range(peers)])


def sum_over(values, axis, step, beside=()):
    peers = lax.axis_size(axis)
    while step < peers:
        count = 4 if 4 * step <= peers else 2
        others = [
            lax.ppermute(values, axis, [(i, i ^ (k * step)) for i in range(peers)])
            for k in range(1, count)
        ]
        if beside:
            beside, others = lax.optimization_barrier((beside, others))
            arrived, beside = beside, ()
        values = values + others[0]
        if count == 4:
            values = values + (others[1] + others[2])
        step *= count
    return (values, arrived)


def sum_and_exchange(values, faces):
    values = pair_sum(values, "grp")
    core = swap(faces[3], 3)
    core, values = lax.optimization_barrier((core, values))
    far = [swap(face, i) for i, face in enumerate(faces[:2])]
    values, far = sum_over(values, "grp", 2, far)
    far, last, values = lax.optimization_barrier((far, faces[2], values))
    values, last = sum_over(values, "sub", 1, [swap(last, 2)])
    return values, [*far, *last, core]


def one_hot(match_ref, i):
    row = match_ref[i : i + 1, :]
    size = row.shape[1]
    nodes = lax.broadcasted_iota(jnp.int32, (size, size), 0)
    return jnp.where(nodes == row, 1.0, 0.0).astype(jnp.bfloat16)


def parts(x, count):
    out = []
    for _ in range(count):
        part = x.astype(jnp.bfloat16)
        out.append(part)
        x = x - part.astype(jnp.float32)
    return out


def mxu(x, y, dims=PLAIN):
    return lax.dot_general(x, y, dims, preferred_element_type=jnp.float32)


def exact(x, y, dims=PLAIN):
    return lax.dot_general(x, y, dims, precision=HIGHEST, preferred_element_type=jnp.float32)


def reorder(x, hot, dims):
    rows = x.shape[0]
    both = mxu(jnp.concatenate(parts(x, 3), axis=0), hot, dims)
    return both[:rows] + both[rows : 2 * rows] + both[2 * rows :]


def turn(x, hot):
    return reorder(x, hot, LAST)


def turn_back(x, hot):
    return reorder(x, hot, PLAIN)


def jump(received, own):
    return [
        received[0] - own[0],
        own[1] - received[1],
        received[2] - own[2],
        own[3] - received[3],
    ]


def odds():
    return odd("sub"), odd("grp")


def faces_in(values):
    out = []
    for far, near, is_odd in zip(values[0:2], values[2:4], odds()):
        out += [jnp.where(is_odd, near, far), jnp.where(is_odd, far, near)]
    return out


def faces_of(ref, size):
    return [ref[:, i * size : (i + 1) * size] for i in range(4)]


def store(ref, faces):
    size = faces[0].shape[1]
    for i in range(4):
        ref[:, i * size : (i + 1) * size] = faces[i]


def total(xs, ys):
    return sum(jnp.sum(x * y, axis=1, keepdims=True) for x, y in zip(xs, ys))


def blocks_of(interface):
    width = 256 if interface % 256 == 0 else interface
    return [slice(i, i + width) for i in range(0, interface, width)]


def product(matrix_ref, result_ref, left, groups):
    for block in blocks_of(matrix_ref.shape[1]):
        both = mxu(left, matrix_ref[:, block])
        at = 0
        for first, rows, count in groups:
            value = both[first : first + rows]
            for i in range(1, count):
                value = value + both[first + i * rows : first + (i + 1) * rows]
            result_ref[at : at + rows, block] = value
            at += rows


def local_order(faces, hots, count):
    split = [jnp.concatenate(parts(x, count), axis=0) for x in faces]
    split[0] = mxu(split[0], hots[0]).astype(jnp.bfloat16)
    split[2] = mxu(split[2], hots[2]).astype(jnp.bfloat16)
    return jnp.concatenate(split, axis=1)


def turned_result(result_ref, hots):
    size = result_ref.shape[1] // 4
    own = faces_of(result_ref, size)
    own[0] = turn(own[0], hots[0])
    own[2] = turn(own[2], hots[2])
    return own


def weighted(faces):
    return [(0.5 * s) * x for s, x in zip(SIGNS, faces)]


def hots_of(hots_ref):
    size = hots_ref.shape[1]
    return [hots_ref[i * size : (i + 1) * size, :] for i in range(4)]


def signed(faces):
    return [s * x for s, x in zip(SIGNS, faces)]


def lane_is(shape, lane):
    return lax.broadcasted_iota(jnp.int32, shape, 1) == lane


def pick(values, lane):
    return jnp.sum(jnp.where(lane_is(values.shape, lane), values, 0.0), axis=1, keepdims=True)


def numbering(extra, slots, width):
    numbers = extra[slots : slots + 1, :LANES]
    nodes = lax.broadcasted_iota(jnp.int32, (width, LANES), 0).astype(jnp.float32)
    return jnp.where(nodes == numbers, 1.0, 0.0)[:, : extra.shape[0]]


def partial_sums(forces, extra, slots, scalars, coarse_size, width):
    out = 0.0
    for x, rows in zip(forces, extra):
        out = out + exact(x, rows, LAST)
    out = exact(out, numbering(extra[0], slots, width), LAST)
    for i, value in enumerate(scalars):
        out = out + jnp.where(lane_is(out.shape, coarse_size + i), value, 0.0)
    return out


def coarse_solve(right, inverse):
    lowered = exact(right, inverse, LAST)
    return exact(lowered, inverse), jnp.sum(lowered * lowered, axis=1, keepdims=True)


def coarse_part(sums, coarse_size):
    lanes = lax.broadcasted_iota(jnp.int32, sums.shape, 1)
    return jnp.where(lanes < coarse_size, sums, 0.0)


def two_high(x):
    return jnp.concatenate(parts(x, 2), axis=0)


def two_wide(x):
    high, low = parts(x, 2)
    return jnp.concatenate(
        [jnp.concatenate([high, high], axis=1), jnp.concatenate([low, low], axis=1)], axis=0
    )


def coarse_times(coarse, image):
    rows = coarse.shape[0]
    both = mxu(two_wide(coarse), image)
    return both[:rows] + both[rows:]


def prepare_kernel(loads_ref, match_ref, schur_ref,
                   loads_out, hots_out, schur_out, match_held, sems):
    copies = [
        pltpu.make_async_copy(x, y, sems.at[i])
        for i, (x, y) in enumerate(
            ((match_ref, match_held), (loads_ref, loads_out), (schur_ref, schur_out))
        )
    ]
    for copy in copies:
        copy.start()
    size = loads_ref.shape[1] // 4
    copies[0].wait()
    for i in range(4):
        hots_out[i * size : (i + 1) * size, :] = one_hot(match_held, i)
    copies[1].wait()
    for i in (0, 2):
        block = slice(i * size, (i + 1) * size)
        loads_out[:, block] = turn(loads_out[:, block], hots_out[block, :])
    copies[2].wait()


def extra_kernel(coupling_ref, corners_ref, hots_ref, extra_out, spread_out):
    size = hots_ref.shape[1]
    slots = coupling_ref.shape[0]
    hots = hots_of(hots_ref)
    extra_out[slots:, :] = jnp.full((extra_out.shape[0] - slots, 4 * size), -1.0, jnp.float32)
    corners = corners_ref[...].astype(jnp.float32)
    coupling = faces_of(coupling_ref, size)
    for i in range(4):
        rows = turn(coupling[i], hots[i]) if i in (0, 2) else coupling[i]
        extra_out[:slots, i * size : (i + 1) * size] = rows
        extra_out[slots : slots + 1, i * size : i * size + slots] = corners
    hot = numbering(extra_out[:, :size], slots, spread_out.shape[0])
    spread_out[...] = exact(hot, extra_out[...])


def first_kernel(near0, near1, near2, near3, loads_ref, hots_ref, schur_ref,
                 residual_ref, send0, send1, send2, send3, result_ref):
    cases = loads_ref.shape[0]
    size = loads_ref.shape[1] // 4
    hots = hots_of(hots_ref)
    near = faces_in([x[...] for x in (near0, near1, near2, near3)])
    for i in (1, 3):
        near[i] = reorder(near[i], hots[i], PLAIN)
    residual = jump(near, faces_of(loads_ref, size))
    store(residual_ref, residual)
    product(schur_ref, result_ref, local_order(weighted(residual), hots, 1), [(0, cases, 1)])
    for ref, value in zip(
        (send0, send1, send2, send3), swapped(turned_result(result_ref, hots), odds())
    ):
        ref[...] = value


def coarse_kernel(cases, spread_ref, near0, near1, near2, near3, image_ref):
    width, interface = spread_ref.shape
    slots = near0.shape[0] - cases - 4
    near = faces_in([x[cases:, :] for x in (near0, near1, near2, near3)])
    near = [exact(numbering(x, slots, width), x) for x in near]
    store(image_ref, [two_high(x) for x in jump(near, faces_of(spread_ref, interface // 4))])


def direction_kernel(coarse_size, count, *refs):
    own = refs[0:4]
    near = refs[4:8]
    extra_ref, residual_ref, hots_ref, flex_ref = refs[8:12]
    n = 12
    if count > 1:
        before_ref = refs[12]
        before_free = refs[13:17]
        n = 17
    precond_ref, free0, free1, free2, free3, sums_ref, result_ref = refs[n:]
    size = own[0].shape[1]
    cases = residual_ref.shape[0]
    slots = extra_ref.shape[0] - 4
    hots = hots_of(hots_ref)
    precond = jump(faces_in([x[...] for x in near]), faces_in([x[...] for x in own]))
    precond = [0.5 * x for x in precond]
    store(precond_ref, precond)
    forces = signed(precond)
    product(flex_ref, result_ref, local_order(forces, hots, count), [(0, cases, count)])
    free = turned_result(result_ref, hots)
    extra = faces_of(extra_ref, size)
    for ref, value, rows in zip(
        (free0, free1, free2, free3), swapped(free, odds()), swapped(extra, odds())
    ):
        ref[:cases, :] = value
        if count == 1:
            ref[cases:, :] = rows
    scalars = [0.5 * total(faces_of(residual_ref, size), precond), total(forces, free)]
    if count > 1:
        before = signed(faces_of(before_ref, size))
        scalars.append(total(forces, faces_in([x[:cases, :] for x in before_free])) + total(before, free))
    sums_ref[...] = partial_sums(
        forces, extra, slots, scalars, coarse_size, sums_ref.shape[1]
    )


def step_kernel(coarse_size, sums_ref, inverse_ref, image_ref, own0, own1, own2, own3,
                near0, near1, near2, near3, residual_ref, hots_ref, schur_ref,
                new_ref, jump_ref, step_ref, send0, send1, send2, send3, result_ref):
    size = own0.shape[1]
    cases = sums_ref.shape[0]
    hots = hots_of(hots_ref)
    moved = jump(
        faces_in([x[:cases, :] for x in (near0, near1, near2, near3)]),
        faces_in([x[:cases, :] for x in (own0, own1, own2, own3)]),
    )
    store(jump_ref, moved)
    sums = sums_ref[...]
    coarse, energy = coarse_solve(coarse_part(sums, coarse_size), inverse_ref[...])
    step = pick(sums, coarse_size) / (pick(sums, coarse_size + 1) + energy)
    step_ref[...] = jnp.broadcast_to(step, step_ref.shape)
    image = coarse_times(coarse, image_ref[...])
    residual = [
        residual_ref[:, i * size : (i + 1) * size]
        - step * (moved[i] + image[:, i * size : (i + 1) * size])
        for i in range(4)
    ]
    store(new_ref, residual)
    product(schur_ref, result_ref, local_order(weighted(residual), hots, 1), [(0, cases, 1)])
    for ref, value in zip(
        (send0, send1, send2, send3), swapped(turned_result(result_ref, hots), odds())
    ):
        ref[...] = value


def home_kernel(residual_ref, before_ref, precond_ref, jump_ref, image_ref, hots_ref,
                residual_out, before_out, precond_out, jump_out, image_out):
    size = hots_ref.shape[1]
    hots = hots_of(hots_ref)
    fields = [faces_of(x, size) for x in (residual_ref, before_ref, precond_ref, jump_ref)]
    image = faces_of(image_ref, size)
    for i in (0, 2):
        image[i] = mxu(image[i], hots[i]).astype(jnp.bfloat16)
        for field in fields:
            field[i] = turn_back(field[i], hots[i])
    store(image_out, image)
    for ref, field in zip((residual_out, before_out, precond_out, jump_out), fields):
        store(ref, field)


def last_kernel(coarse_size, first_ref, sums_ref, inverse_ref, step_ref, residual_ref, before_ref,
                precond_ref, jump_ref, image_ref, hots_ref, own0, own1, own2, own3,
                near0, near1, near2, near3, multipliers_ref, out_ref):
    size = hots_ref.shape[1]
    hots = hots_of(hots_ref)
    following = jump(
        faces_in([x[...] for x in (near0, near1, near2, near3)]),
        faces_in([x[...] for x in (own0, own1, own2, own3)]),
    )
    for i in (0, 2):
        following[i] = turn_back(following[i], hots[i])
    first = first_ref[...]
    sums = sums_ref[...]
    beta = pick(sums, coarse_size) / pick(first, coarse_size)
    right = coarse_part(sums, coarse_size) + beta * coarse_part(first, coarse_size)
    coarse, energy = coarse_solve(right, inverse_ref[...])
    local = pick(sums, coarse_size + 1) + beta * (
        pick(sums, coarse_size + 2) + beta * pick(first, coarse_size + 1)
    )
    step = pick(sums, coarse_size) / (local + energy)
    step_before = step_ref[:, 0:1]
    image = coarse_times(coarse, image_ref[...])
    for i in range(4):
        block = slice(i * size, (i + 1) * size)
        moved = following[i] + beta * jump_ref[:, block] + image[:, block]
        out_ref[:, i, :] = residual_ref[:, block] - step * moved
        before = before_ref[:, block]
        direction = precond_ref[:, block] + beta * before
        multipliers_ref[:, i, :] = step_before * before + step * direction


VMEM = pl.BlockSpec(memory_space=pltpu.VMEM)
OUTSIDE = pl.BlockSpec(memory_space=pltpu.HBM)


def call(kernel, args, outs, scratch=(), outside=(), flops=0):
    specs = [OUTSIDE if i in outside else VMEM for i in range(len(args))]
    shapes = [(x, jnp.float32) if isinstance(x[0], int) else x for x in outs]
    return pl.pallas_call(
        kernel,
        in_specs=specs,
        out_specs=[VMEM] * len(outs),
        out_shape=[jax.ShapeDtypeStruct(*x) for x in shapes],
        scratch_shapes=list(scratch),
        compiler_params=pltpu.CompilerParams(vmem_limit_bytes=28 * 2**20),
        cost_estimate=pl.CostEstimate(flops=flops, bytes_accessed=2**22, transcendentals=0),
    )(*args)


def shards(
    applied_loads,
    flex_matrix,
    schur_matrix,
    corner_coupling,
    coarse_inverse,
    face_match,
    corner_map,
):
    loads = applied_loads[0, 0]
    flex = flex_matrix[0, 0]
    schur = schur_matrix[0, 0]
    match = face_match[0, 0]
    cases, interface = loads.shape
    size = interface // 4
    slots = corner_coupling.shape[2]
    coarse_size = coarse_inverse.shape[0]
    width = -(-(coarse_size + 3) // LANES) * LANES
    work = 2 * cases * interface * interface

    inverse = jnp.pad(coarse_inverse, ((0, width - coarse_size), (0, width - coarse_size)))
    field = (cases, interface)
    face = (cases, size)
    result = pltpu.VMEM(field, jnp.float32)
    both_parts = ((2 * width, interface), jnp.bfloat16)

    held = [pltpu.with_memory_space_constraint(x, pltpu.HBM) for x in (loads, match, schur)]
    near = exchange(
        swapped([loads[:, i * size : (i + 1) * size] for i in range(4)], (odd("sub"), odd("grp")))
    )
    loads, hots, schur = call(
        prepare_kernel,
        held,
        [field, ((4 * size, size), jnp.bfloat16), (schur.shape, jnp.bfloat16)],
        [pltpu.VMEM(match.shape, jnp.int32), pltpu.SemaphoreType.DMA((3,))],
        outside=(0, 1, 2),
        flops=work,
    )
    residual, *own_first = call(
        first_kernel, [*near, loads, hots, schur], [field] + [face] * 4, [result], flops=work
    )
    near = exchange(own_first)
    residual, coupling, corners = lax.optimization_barrier(
        (residual, corner_coupling[0, 0], corner_map[0])
    )
    extra, spread = call(
        extra_kernel,
        [coupling, corners, hots],
        [(slots + 4, interface), (width, interface)],
        flops=work // 4,
    )
    before, *own_free, sums = call(
        functools.partial(direction_kernel, coarse_size, 1),
        [*own_first, *near, extra, residual, hots, flex],
        [field] + [(cases + slots + 4, size)] * 4 + [(cases, width)],
        [result],
        flops=work,
    )
    first_sums, near = sum_and_exchange(sums, own_free)
    (image,) = call(
        functools.partial(coarse_kernel, cases), [spread, *near], [both_parts], flops=work // 4
    )
    residual, moved, step, *own = call(
        functools.partial(step_kernel, coarse_size),
        [first_sums, inverse, image, *own_free, *near, residual, hots, schur],
        [field, field, (cases, LANES)] + [face] * 4,
        [result],
        flops=work,
    )
    near = exchange(own)
    precond, *own, sums = call(
        functools.partial(direction_kernel, coarse_size, 2),
        [*own, *near, extra, residual, hots, flex, before, *own_free],
        [field] + [face] * 4 + [(cases, width)],
        [result],
        flops=work,
    )
    fields = call(
        home_kernel,
        [residual, before, precond, moved, image, hots],
        [field] * 4 + [both_parts],
        flops=work // 2,
    )
    sums, near = sum_and_exchange(sums, own)
    layout = (cases, 4, size)
    multipliers, residual = call(
        functools.partial(last_kernel, coarse_size),
        [first_sums, sums, inverse, step, *fields, hots, *own, *near],
        [layout, layout],
        flops=work // 4,
    )
    return multipliers[None, None], residual[None, None]


def solution(mesh):
    return jax.shard_map(
        shards,
        mesh=mesh,
        in_specs=(
            P("sub", "grp", None, None),
            P("sub", "grp", None, None),
            P("sub", "grp", None, None),
            P("sub", "grp", None, None),
            P(),
            P("sub", "grp", None, None),
            P("sub", "grp", None),
        ),
        out_specs=(P("sub", "grp", None, None, None), P("sub", "grp", None, None, None)),
        check_vma=False,
    )
```

```python
import functools

import jax
import jax.numpy as jnp
from jax import lax
from jax.experimental import pallas as pl
from jax.experimental.pallas import tpu as pltpu
from jax.sharding import PartitionSpec as P

HIGHEST = lax.Precision.HIGHEST
PLAIN = (((1,), (0,)), ((), ()))
LAST = (((1,), (1,)), ((), ()))
LANES = 128
SIGNS = (-1.0, 1.0, -1.0, 1.0)


def odd(axis):
    return lax.axis_index(axis) % 2 == 1


def swapped(faces, odds):
    far, near = [], []
    for (low, high), is_odd in zip((faces[0:2], faces[2:4]), odds):
        far.append(jnp.where(is_odd, high, low))
        near.append(jnp.where(is_odd, low, high))
    return far + near


def swap(face, i):
    axis = ("sub", "grp", "sub", "grp")[i]
    peers = lax.axis_size(axis)
    if i < 2:
        pairs = [(j, (j + 2 * (j % 2) - 1) % peers) for j in range(peers)]
    else:
        pairs = [(j, j ^ 1) for j in range(peers)]
    return lax.ppermute(face, axis, pairs)


def exchange(faces):
    return lax.optimization_barrier([swap(face, i) for i, face in enumerate(faces)])


def sum_over(values, axis, step, beside=()):
    peers = lax.axis_size(axis)
    while step < peers:
        count = 4 if 4 * step <= peers else 2
        others = [
            lax.ppermute(values, axis, [(i, i ^ (k * step)) for i in range(peers)])
            for k in range(1, count)
        ]
        if beside:
            beside, others = lax.optimization_barrier((beside, others))
            arrived, beside = beside, ()
        values = values + others[0]
        if count == 4:
            values = values + (others[1] + others[2])
        step *= count
    return (values, arrived)


def sum_and_exchange(faces, cases):
    far, high, near, core = faces
    size = near.shape[1]
    other = swap(core, 3)
    values = core[:cases, size:] + other[:cases, size:]
    subs = [swap(far, 0), swap(near, 2)]
    values, subs = sum_over(values, "grp", 2, subs)
    subs, high, values = lax.optimization_barrier((subs, high, values))
    values, high = sum_over(values, "sub", 1, [swap(high, 1)])
    return values, [subs[0], *high, subs[1], other]


def one_hot(match_ref, i):
    row = match_ref[i : i + 1, :]
    size = row.shape[1]
    nodes = lax.broadcasted_iota(jnp.int32, (size, size), 0)
    return jnp.where(nodes == row, 1.0, 0.0).astype(jnp.bfloat16)


def parts(x, count):
    out = []
    for _ in range(count):
        part = x.astype(jnp.bfloat16)
        out.append(part)
        x = x - part.astype(jnp.float32)
    return out


def mxu(x, y, dims=PLAIN):
    return lax.dot_general(x, y, dims, preferred_element_type=jnp.float32)


def exact(x, y, dims=PLAIN):
    return lax.dot_general(x, y, dims, precision=HIGHEST, preferred_element_type=jnp.float32)


def reorder(x, hot, dims):
    rows = x.shape[0]
    both = mxu(jnp.concatenate(parts(x, 3), axis=0), hot, dims)
    return both[:rows] + both[rows : 2 * rows] + both[2 * rows :]


def turn(x, hot):
    return reorder(x, hot, LAST)


def turn_back(x, hot):
    return reorder(x, hot, PLAIN)


def jump(received, own):
    return [
        received[0] - own[0],
        own[1] - received[1],
        received[2] - own[2],
        own[3] - received[3],
    ]


def odds():
    return odd("sub"), odd("grp")


def faces_in(values):
    out = []
    for far, near, is_odd in zip(values[0:2], values[2:4], odds()):
        out += [jnp.where(is_odd, near, far), jnp.where(is_odd, far, near)]
    return out


def faces_of(ref, size):
    return [ref[:, i * size : (i + 1) * size] for i in range(4)]


def store(ref, faces):
    size = faces[0].shape[1]
    for i in range(4):
        ref[:, i * size : (i + 1) * size] = faces[i]


def total(xs, ys):
    return sum(jnp.sum(x * y, axis=1, keepdims=True) for x, y in zip(xs, ys))


def blocks_of(interface):
    width = 256 if interface % 256 == 0 else interface
    return [slice(i, i + width) for i in range(0, interface, width)]


def product(matrix_ref, result_ref, left, groups):
    for block in blocks_of(matrix_ref.shape[1]):
        both = mxu(left, matrix_ref[:, block])
        at = 0
        for first, rows, count in groups:
            value = both[first : first + rows]
            for i in range(1, count):
                value = value + both[first + i * rows : first + (i + 1) * rows]
            result_ref[at : at + rows, block] = value
            at += rows


def local_order(faces, hots, count):
    split = [jnp.concatenate(parts(x, count), axis=0) for x in faces]
    split[0] = mxu(split[0], hots[0]).astype(jnp.bfloat16)
    split[2] = mxu(split[2], hots[2]).astype(jnp.bfloat16)
    return jnp.concatenate(split, axis=1)


def turned_result(result_ref, hots):
    size = result_ref.shape[1] // 4
    own = faces_of(result_ref, size)
    own[0] = turn(own[0], hots[0])
    own[2] = turn(own[2], hots[2])
    return own


def weighted(faces):
    return [(0.5 * s) * x for s, x in zip(SIGNS, faces)]


def hots_of(hots_ref):
    size = hots_ref.shape[1]
    return [hots_ref[i * size : (i + 1) * size, :] for i in range(4)]


def signed(faces):
    return [s * x for s, x in zip(SIGNS, faces)]


def lane_is(shape, lane):
    return lax.broadcasted_iota(jnp.int32, shape, 1) == lane


def pick(values, lane):
    return jnp.sum(jnp.where(lane_is(values.shape, lane), values, 0.0), axis=1, keepdims=True)


def numbering(extra, slots, width):
    numbers = extra[slots : slots + 1, :LANES]
    nodes = lax.broadcasted_iota(jnp.int32, (width, LANES), 0).astype(jnp.float32)
    return jnp.where(nodes == numbers, 1.0, 0.0)[:, : extra.shape[0]]


def partial_sums(forces, extra, slots, scalars, coarse_size, width):
    out = 0.0
    for x, rows in zip(forces, extra):
        out = out + exact(x, rows, LAST)
    out = exact(out, numbering(extra[0], slots, width), LAST)
    for i, value in enumerate(scalars):
        out = out + jnp.where(lane_is(out.shape, coarse_size + i), value, 0.0)
    return out


def coarse_solve(right, inverse):
    lowered = exact(right, inverse, LAST)
    return exact(lowered, inverse), jnp.sum(lowered * lowered, axis=1, keepdims=True)


def coarse_part(sums, coarse_size):
    lanes = lax.broadcasted_iota(jnp.int32, sums.shape, 1)
    return jnp.where(lanes < coarse_size, sums, 0.0)


def two_high(x):
    return jnp.concatenate(parts(x, 2), axis=0)


def two_wide(x):
    high, low = parts(x, 2)
    return jnp.concatenate(
        [jnp.concatenate([high, high], axis=1), jnp.concatenate([low, low], axis=1)], axis=0
    )


def coarse_times(coarse, image):
    rows = coarse.shape[0]
    both = mxu(two_wide(coarse), image)
    return both[:rows] + both[rows:]


def prepare_kernel(loads_ref, match_ref, schur_ref,
                   loads_out, hots_out, schur_out, match_held, sems):
    copies = [
        pltpu.make_async_copy(x, y, sems.at[i])
        for i, (x, y) in enumerate(
            ((match_ref, match_held), (loads_ref, loads_out), (schur_ref, schur_out))
        )
    ]
    for copy in copies:
        copy.start()
    size = loads_ref.shape[1] // 4
    copies[0].wait()
    for i in range(4):
        hots_out[i * size : (i + 1) * size, :] = one_hot(match_held, i)
    copies[1].wait()
    for i in (0, 2):
        block = slice(i * size, (i + 1) * size)
        loads_out[:, block] = turn(loads_out[:, block], hots_out[block, :])
    copies[2].wait()


def extra_kernel(coupling_ref, corners_ref, hots_ref, extra_out, spread_out):
    size = hots_ref.shape[1]
    slots = coupling_ref.shape[0]
    hots = hots_of(hots_ref)
    extra_out[slots:, :] = jnp.full((extra_out.shape[0] - slots, 4 * size), -1.0, jnp.float32)
    corners = corners_ref[...].astype(jnp.float32)
    coupling = faces_of(coupling_ref, size)
    for i in range(4):
        rows = turn(coupling[i], hots[i]) if i in (0, 2) else coupling[i]
        extra_out[:slots, i * size : (i + 1) * size] = rows
        extra_out[slots : slots + 1, i * size : i * size + slots] = corners
    hot = numbering(extra_out[:, :size], slots, spread_out.shape[0])
    spread_out[...] = exact(hot, extra_out[...])


def first_kernel(near0, near1, near2, near3, loads_ref, hots_ref, schur_ref,
                 residual_ref, send0, send1, send2, send3, result_ref):
    cases = loads_ref.shape[0]
    size = loads_ref.shape[1] // 4
    hots = hots_of(hots_ref)
    near = faces_in([x[...] for x in (near0, near1, near2, near3)])
    for i in (1, 3):
        near[i] = reorder(near[i], hots[i], PLAIN)
    residual = jump(near, faces_of(loads_ref, size))
    store(residual_ref, residual)
    product(schur_ref, result_ref, local_order(weighted(residual), hots, 1), [(0, cases, 1)])
    for ref, value in zip(
        (send0, send1, send2, send3), swapped(turned_result(result_ref, hots), odds())
    ):
        ref[...] = value


def coarse_kernel(cases, spread_ref, near0, near1, near2, near3, image_ref):
    width, interface = spread_ref.shape
    slots = near0.shape[0] - cases - 4
    size = interface // 4
    near = faces_in([x[cases:, :size] for x in (near0, near1, near2, near3)])
    near = [exact(numbering(x, slots, width), x) for x in near]
    store(image_ref, [two_high(x) for x in jump(near, faces_of(spread_ref, size))])


def direction_kernel(coarse_size, count, *refs):
    own = refs[0:4]
    near = refs[4:8]
    extra_ref, residual_ref, hots_ref, flex_ref = refs[8:12]
    n = 12
    if count > 1:
        before_ref = refs[12]
        before_free = refs[13:17]
        n = 17
    precond_ref, free0, free1, free2, free3, result_ref = refs[n:]
    size = own[0].shape[1]
    cases = residual_ref.shape[0]
    slots = extra_ref.shape[0] - 4
    hots = hots_of(hots_ref)
    precond = jump(faces_in([x[...] for x in near]), faces_in([x[...] for x in own]))
    precond = [0.5 * x for x in precond]
    store(precond_ref, precond)
    forces = signed(precond)
    product(flex_ref, result_ref, local_order(forces, hots, count), [(0, cases, count)])
    free = turned_result(result_ref, hots)
    extra = faces_of(extra_ref, size)
    for ref, value, rows in zip(
        (free0, free1, free2, free3), swapped(free, odds()), swapped(extra, odds())
    ):
        ref[:cases, :size] = value
        if count == 1:
            ref[cases:, :size] = rows
    scalars = [0.5 * total(faces_of(residual_ref, size), precond), total(forces, free)]
    if count > 1:
        before = signed(faces_of(before_ref, size))
        scalars.append(total(forces, faces_in([x[:cases, :size] for x in before_free])) + total(before, free))
    width = free3.shape[1] - size
    free3[:cases, size:] = partial_sums(forces, extra, slots, scalars, coarse_size, width)
    if count == 1:
        free3[cases:, size:] = jnp.zeros((free3.shape[0] - cases, width), jnp.float32)


def step_kernel(coarse_size, sums_ref, inverse_ref, image_ref, own0, own1, own2, own3,
                near0, near1, near2, near3, residual_ref, hots_ref, schur_ref,
                new_ref, jump_ref, step_ref, send0, send1, send2, send3, result_ref):
    size = own0.shape[1]
    cases = sums_ref.shape[0]
    hots = hots_of(hots_ref)
    moved = jump(
        faces_in([x[:cases, :size] for x in (near0, near1, near2, near3)]),
        faces_in([x[:cases, :size] for x in (own0, own1, own2, own3)]),
    )
    store(jump_ref, moved)
    sums = sums_ref[...]
    coarse, energy = coarse_solve(coarse_part(sums, coarse_size), inverse_ref[...])
    step = pick(sums, coarse_size) / (pick(sums, coarse_size + 1) + energy)
    step_ref[...] = jnp.broadcast_to(step, step_ref.shape)
    image = coarse_times(coarse, image_ref[...])
    residual = [
        residual_ref[:, i * size : (i + 1) * size]
        - step * (moved[i] + image[:, i * size : (i + 1) * size])
        for i in range(4)
    ]
    store(new_ref, residual)
    product(schur_ref, result_ref, local_order(weighted(residual), hots, 1), [(0, cases, 1)])
    for ref, value in zip(
        (send0, send1, send2, send3), swapped(turned_result(result_ref, hots), odds())
    ):
        ref[...] = value


def home_kernel(residual_ref, before_ref, precond_ref, jump_ref, image_ref, hots_ref,
                residual_out, before_out, precond_out, jump_out, image_out):
    size = hots_ref.shape[1]
    hots = hots_of(hots_ref)
    fields = [faces_of(x, size) for x in (residual_ref, before_ref, precond_ref, jump_ref)]
    image = faces_of(image_ref, size)
    for i in (0, 2):
        image[i] = mxu(image[i], hots[i]).astype(jnp.bfloat16)
        for field in fields:
            field[i] = turn_back(field[i], hots[i])
    store(image_out, image)
    for ref, field in zip((residual_out, before_out, precond_out, jump_out), fields):
        store(ref, field)


def last_kernel(coarse_size, first_ref, sums_ref, inverse_ref, step_ref, residual_ref, before_ref,
                precond_ref, jump_ref, image_ref, hots_ref, own0, own1, own2, own3,
                near0, near1, near2, near3, multipliers_ref, out_ref):
    size = hots_ref.shape[1]
    hots = hots_of(hots_ref)
    following = jump(
        faces_in([x[:, :size] for x in (near0, near1, near2, near3)]),
        faces_in([x[:, :size] for x in (own0, own1, own2, own3)]),
    )
    for i in (0, 2):
        following[i] = turn_back(following[i], hots[i])
    first = first_ref[...]
    sums = sums_ref[...]
    beta = pick(sums, coarse_size) / pick(first, coarse_size)
    right = coarse_part(sums, coarse_size) + beta * coarse_part(first, coarse_size)
    coarse, energy = coarse_solve(right, inverse_ref[...])
    local = pick(sums, coarse_size + 1) + beta * (
        pick(sums, coarse_size + 2) + beta * pick(first, coarse_size + 1)
    )
    step = pick(sums, coarse_size) / (local + energy)
    step_before = step_ref[:, 0:1]
    image = coarse_times(coarse, image_ref[...])
    for i in range(4):
        block = slice(i * size, (i + 1) * size)
        moved = following[i] + beta * jump_ref[:, block] + image[:, block]
        out_ref[:, i, :] = residual_ref[:, block] - step * moved
        before = before_ref[:, block]
        direction = precond_ref[:, block] + beta * before
        multipliers_ref[:, i, :] = step_before * before + step * direction


VMEM = pl.BlockSpec(memory_space=pltpu.VMEM)
OUTSIDE = pl.BlockSpec(memory_space=pltpu.HBM)


def call(kernel, args, outs, scratch=(), outside=(), flops=0):
    specs = [OUTSIDE if i in outside else VMEM for i in range(len(args))]
    shapes = [(x, jnp.float32) if isinstance(x[0], int) else x for x in outs]
    return pl.pallas_call(
        kernel,
        in_specs=specs,
        out_specs=[VMEM] * len(outs),
        out_shape=[jax.ShapeDtypeStruct(*x) for x in shapes],
        scratch_shapes=list(scratch),
        compiler_params=pltpu.CompilerParams(vmem_limit_bytes=28 * 2**20),
        cost_estimate=pl.CostEstimate(flops=flops, bytes_accessed=2**22, transcendentals=0),
    )(*args)


def shards(
    applied_loads,
    flex_matrix,
    schur_matrix,
    corner_coupling,
    coarse_inverse,
    face_match,
    corner_map,
):
    loads = applied_loads[0, 0]
    flex = flex_matrix[0, 0]
    schur = schur_matrix[0, 0]
    match = face_match[0, 0]
    cases, interface = loads.shape
    size = interface // 4
    slots = corner_coupling.shape[2]
    coarse_size = coarse_inverse.shape[0]
    width = -(-(coarse_size + 3) // LANES) * LANES
    work = 2 * cases * interface * interface

    inverse = jnp.pad(coarse_inverse, ((0, width - coarse_size), (0, width - coarse_size)))
    field = (cases, interface)
    face = (cases, size)
    result = pltpu.VMEM(field, jnp.float32)
    both_parts = ((2 * width, interface), jnp.bfloat16)

    held = [pltpu.with_memory_space_constraint(x, pltpu.HBM) for x in (loads, match, schur)]
    near = exchange(
        swapped([loads[:, i * size : (i + 1) * size] for i in range(4)], (odd("sub"), odd("grp")))
    )
    loads, hots, schur = call(
        prepare_kernel,
        held,
        [field, ((4 * size, size), jnp.bfloat16), (schur.shape, jnp.bfloat16)],
        [pltpu.VMEM(match.shape, jnp.int32), pltpu.SemaphoreType.DMA((3,))],
        outside=(0, 1, 2),
        flops=work,
    )
    residual, *own_first = call(
        first_kernel, [*near, loads, hots, schur], [field] + [face] * 4, [result], flops=work
    )
    near = exchange(own_first)
    residual, coupling, corners = lax.optimization_barrier(
        (residual, corner_coupling[0, 0], corner_map[0])
    )
    extra, spread = call(
        extra_kernel,
        [coupling, corners, hots],
        [(slots + 4, interface), (width, interface)],
        flops=work // 4,
    )
    before, *own_free = call(
        functools.partial(direction_kernel, coarse_size, 1),
        [*own_first, *near, extra, residual, hots, flex],
        [field] + [(cases + slots + 4, size)] * 3 + [(cases + slots + 4, size + width)],
        [result],
        flops=work,
    )
    first_sums, near = sum_and_exchange(own_free, cases)
    (image,) = call(
        functools.partial(coarse_kernel, cases), [spread, *near], [both_parts], flops=work // 4
    )
    residual, moved, step, *own = call(
        functools.partial(step_kernel, coarse_size),
        [first_sums, inverse, image, *own_free, *near, residual, hots, schur],
        [field, field, (cases, LANES)] + [face] * 4,
        [result],
        flops=work,
    )
    near = exchange(own)
    precond, *own = call(
        functools.partial(direction_kernel, coarse_size, 2),
        [*own, *near, extra, residual, hots, flex, before, *own_free],
        [field] + [face] * 3 + [(cases, size + width)],
        [result],
        flops=work,
    )
    fields = call(
        home_kernel,
        [residual, before, precond, moved, image, hots],
        [field] * 4 + [both_parts],
        flops=work // 2,
    )
    sums, near = sum_and_exchange(own, cases)
    layout = (cases, 4, size)
    multipliers, residual = call(
        functools.partial(last_kernel, coarse_size),
        [first_sums, sums, inverse, step, *fields, hots, *own, *near],
        [layout, layout],
        flops=work // 4,
    )
    return multipliers[None, None], residual[None, None]


def solution(mesh):
    return jax.shard_map(
        shards,
        mesh=mesh,
        in_specs=(
            P("sub", "grp", None, None),
            P("sub", "grp", None, None),
            P("sub", "grp", None, None),
            P("sub", "grp", None, None),
            P(),
            P("sub", "grp", None, None),
            P("sub", "grp", None),
        ),
        out_specs=(P("sub", "grp", None, None, None), P("sub", "grp", None, None, None)),
        check_vma=False,
    )
```

```python
import functools

import jax
import jax.numpy as jnp
from jax import lax
from jax.experimental import pallas as pl
from jax.experimental.pallas import tpu as pltpu
from jax.sharding import PartitionSpec as P

HIGHEST = lax.Precision.HIGHEST
PLAIN = (((1,), (0,)), ((), ()))
LAST = (((1,), (1,)), ((), ()))
LANES = 128
SIGNS = (-1.0, 1.0, -1.0, 1.0)


def odd(axis):
    return lax.axis_index(axis) % 2 == 1


def swapped(faces, odds):
    far, near = [], []
    for (low, high), is_odd in zip((faces[0:2], faces[2:4]), odds):
        far.append(jnp.where(is_odd, high, low))
        near.append(jnp.where(is_odd, low, high))
    return far + near


def swap(face, i):
    axis = ("sub", "grp", "sub", "grp")[i]
    peers = lax.axis_size(axis)
    if i < 2:
        pairs = [(j, (j + 2 * (j % 2) - 1) % peers) for j in range(peers)]
    else:
        pairs = [(j, j ^ 1) for j in range(peers)]
    return lax.ppermute(face, axis, pairs)


def exchange(faces):
    return lax.optimization_barrier([swap(face, i) for i, face in enumerate(faces)])


def sum_over(values, axis, step, before=(), after=()):
    peers = lax.axis_size(axis)
    first = True
    while step < peers:
        count = 4 if 4 * step <= peers else 2
        others = [
            lax.ppermute(values, axis, [(i, i ^ (k * step)) for i in range(peers)])
            for k in range(1, count)
        ]
        if first:
            before, others, after = lax.optimization_barrier((before, others, after))
            first = False
        values = values + others[0]
        if count == 4:
            values = values + (others[1] + others[2])
        step *= count
    return values, before, after


def sum_and_exchange(faces, cases):
    far, high, near, core = faces
    size = near.shape[1]
    other = swap(core, 3)
    values = core[:cases, size:] + other[:cases, size:]
    near, values = lax.optimization_barrier((near, values))
    values, far, near = sum_over(values, "grp", 2, [swap(far, 0)], [swap(near, 2)])
    far, near, high, values = lax.optimization_barrier((far, near, high, values))
    values, high, _ = sum_over(values, "sub", 1, [swap(high, 1)])
    return values, [*far, *high, *near, other]


def one_hot(match_ref, i):
    row = match_ref[i : i + 1, :]
    size = row.shape[1]
    nodes = lax.broadcasted_iota(jnp.int32, (size, size), 0)
    return jnp.where(nodes == row, 1.0, 0.0).astype(jnp.bfloat16)


def parts(x, count):
    out = []
    for _ in range(count):
        part = x.astype(jnp.bfloat16)
        out.append(part)
        x = x - part.astype(jnp.float32)
    return out


def mxu(x, y, dims=PLAIN):
    return lax.dot_general(x, y, dims, preferred_element_type=jnp.float32)


def exact(x, y, dims=PLAIN):
    return lax.dot_general(x, y, dims, precision=HIGHEST, preferred_element_type=jnp.float32)


def reorder(x, hot, dims):
    rows = x.shape[0]
    both = mxu(jnp.concatenate(parts(x, 3), axis=0), hot, dims)
    return both[:rows] + both[rows : 2 * rows] + both[2 * rows :]


def turn(x, hot):
    return reorder(x, hot, LAST)


def turn_back(x, hot):
    return reorder(x, hot, PLAIN)


def jump(received, own):
    return [
        received[0] - own[0],
        own[1] - received[1],
        received[2] - own[2],
        own[3] - received[3],
    ]


def odds():
    return odd("sub"), odd("grp")


def faces_in(values):
    out = []
    for far, near, is_odd in zip(values[0:2], values[2:4], odds()):
        out += [jnp.where(is_odd, near, far), jnp.where(is_odd, far, near)]
    return out


def faces_of(ref, size):
    return [ref[:, i * size : (i + 1) * size] for i in range(4)]


def store(ref, faces):
    size = faces[0].shape[1]
    for i in range(4):
        ref[:, i * size : (i + 1) * size] = faces[i]


def store_some(ref, faces):
    size = faces[0].shape[1]
    for i, face in enumerate(faces):
        ref[:, i * size : (i + 1) * size] = face


def total(xs, ys):
    return sum(jnp.sum(x * y, axis=1, keepdims=True) for x, y in zip(xs, ys))


def blocks_of(interface):
    width = 256 if interface % 256 == 0 else interface
    return [slice(i, i + width) for i in range(0, interface, width)]


def product(matrix_ref, result_ref, left, groups):
    for block in blocks_of(matrix_ref.shape[1]):
        both = mxu(left, matrix_ref[:, block])
        at = 0
        for first, rows, count in groups:
            value = both[first : first + rows]
            for i in range(1, count):
                value = value + both[first + i * rows : first + (i + 1) * rows]
            result_ref[at : at + rows, block] = value
            at += rows


def local_order(faces, hots, count):
    split = [jnp.concatenate(parts(x, count), axis=0) for x in faces]
    split[0] = mxu(split[0], hots[0]).astype(jnp.bfloat16)
    split[2] = mxu(split[2], hots[2]).astype(jnp.bfloat16)
    return jnp.concatenate(split, axis=1)


def turned_result(result_ref, hots):
    size = result_ref.shape[1] // 4
    own = faces_of(result_ref, size)
    own[0] = turn(own[0], hots[0])
    own[2] = turn(own[2], hots[2])
    return own


def weighted(faces):
    return [(0.5 * s) * x for s, x in zip(SIGNS, faces)]


def hots_of(hots_ref):
    size = hots_ref.shape[1]
    return [hots_ref[i * size : (i + 1) * size, :] for i in range(4)]


def signed(faces):
    return [s * x for s, x in zip(SIGNS, faces)]


def lane_is(shape, lane):
    return lax.broadcasted_iota(jnp.int32, shape, 1) == lane


def pick(values, lane):
    return jnp.sum(jnp.where(lane_is(values.shape, lane), values, 0.0), axis=1, keepdims=True)


def numbering(extra, slots, width):
    numbers = extra[slots : slots + 1, :LANES]
    nodes = lax.broadcasted_iota(jnp.int32, (width, LANES), 0).astype(jnp.float32)
    hot = jnp.where(nodes == numbers, 1.0, 0.0)
    return hot[:, : 3 * extra.shape[0]].astype(jnp.bfloat16)


def spread(extra, slots, width):
    return mxu(numbering(extra, slots, width), jnp.concatenate(parts(extra, 3), axis=0))


def partial_sums(left, coupling, extra, slots, scalars, coarse_size, width):
    out = reorder(mxu(left, coupling, LAST), numbering(extra, slots, width), LAST)
    rows = out.shape[0] // 2
    out = out[:rows] + out[rows:]
    for i, value in enumerate(scalars):
        out = out + jnp.where(lane_is(out.shape, coarse_size + i), value, 0.0)
    return out


def by_parts(x, matrix, dims):
    rows = x.shape[0]
    both = mxu(jnp.concatenate(parts(x, 3), axis=0), matrix, dims)
    both = both[:rows] + (both[rows : 2 * rows] + both[2 * rows :])
    width = both.shape[1] // 3
    return both[:, :width] + (both[:, width : 2 * width] + both[:, 2 * width :])


def coarse_solve(right, down_ref, up_ref):
    lowered = by_parts(right, down_ref[...], LAST)
    return by_parts(lowered, up_ref[...], PLAIN), jnp.sum(lowered * lowered, axis=1, keepdims=True)


def coarse_part(sums, coarse_size):
    lanes = lax.broadcasted_iota(jnp.int32, sums.shape, 1)
    return jnp.where(lanes < coarse_size, sums, 0.0)


def two_high(x):
    return jnp.concatenate(parts(x, 2), axis=0)


def two_wide(x):
    high, low = parts(x, 2)
    return jnp.concatenate(
        [jnp.concatenate([high, high], axis=1), jnp.concatenate([low, low], axis=1)], axis=0
    )


def coarse_times(coarse, *image_refs):
    rows = coarse.shape[0]
    left = two_wide(coarse)
    both = [mxu(left, image[...]) for image in image_refs]
    return jnp.concatenate([x[:rows] + x[rows:] for x in both], axis=1)


def prepare_kernel(loads_ref, match_ref, schur_ref,
                   loads_out, hots_out, schur_out, match_held, sems):
    copies = [
        pltpu.make_async_copy(x, y, sems.at[i])
        for i, (x, y) in enumerate(
            ((match_ref, match_held), (loads_ref, loads_out), (schur_ref, schur_out))
        )
    ]
    for copy in copies:
        copy.start()
    size = loads_ref.shape[1] // 4
    copies[0].wait()
    for i in range(4):
        hots_out[i * size : (i + 1) * size, :] = one_hot(match_held, i)
    copies[1].wait()
    for i in (0, 2):
        block = slice(i * size, (i + 1) * size)
        loads_out[:, block] = turn(loads_out[:, block], hots_out[block, :])
    copies[2].wait()


def extra_kernel(coupling_ref, corners_ref, inverse_ref, hots_ref,
                 extra_out, spread_out, coupling_out, down_out, up_out):
    size = hots_ref.shape[1]
    slots = coupling_ref.shape[0]
    rows = extra_out.shape[0]
    hots = hots_of(hots_ref)
    extra_out[...] = jnp.full(extra_out.shape, -1.0, jnp.float32)
    corners = corners_ref[...].astype(jnp.float32)
    for i in range(4):
        extra_out[:slots, i * size : (i + 1) * size] = coupling_ref[:, i * size : (i + 1) * size]
        for k in range(3):
            at = i * size + k * rows
            extra_out[slots : slots + 1, at : at + slots] = corners
    coupling_out[...] = jnp.concatenate(parts(extra_out[...], 3), axis=0)
    for i in (0, 2):
        block = slice(i * size, (i + 1) * size)
        extra_out[:slots, block] = turn(coupling_ref[:, block], hots[i])
    spread_out[...] = spread(extra_out[...], slots, spread_out.shape[0])
    inverse = parts(inverse_ref[...], 3)
    down_out[...] = jnp.concatenate(inverse, axis=0)
    up_out[...] = jnp.concatenate(inverse, axis=1)


def first_kernel(near0, near1, near2, near3, loads_ref, hots_ref, schur_ref,
                 residual_ref, send0, send1, send2, send3, result_ref):
    cases = loads_ref.shape[0]
    size = loads_ref.shape[1] // 4
    hots = hots_of(hots_ref)
    near = faces_in([x[...] for x in (near0, near1, near2, near3)])
    for i in (1, 3):
        near[i] = reorder(near[i], hots[i], PLAIN)
    residual = jump(near, faces_of(loads_ref, size))
    store(residual_ref, residual)
    product(schur_ref, result_ref, local_order(weighted(residual), hots, 1), [(0, cases, 1)])
    for ref, value in zip(
        (send0, send1, send2, send3), swapped(turned_result(result_ref, hots), odds())
    ):
        ref[...] = value


def coarse_kernel(cases, spread_ref, far_ref, near_ref, core_ref, image_ref, rest_ref):
    width, interface = spread_ref.shape
    size = interface // 4
    slots = near_ref.shape[0] - cases - 4
    own = faces_of(spread_ref, size)
    far, near, core = [
        spread(x[cases:, :size], slots, width) for x in (far_ref, near_ref, core_ref)
    ]
    zero = jnp.zeros_like(core)
    image = jump(faces_in([far, zero, near, core]), own)
    store_some(image_ref, [two_high(x) for x in image[:2]])
    store_some(rest_ref, image[2:])


def coarse_rest_kernel(cases, rest_ref, high_ref, image_ref):
    size = rest_ref.shape[1] // 2
    width = rest_ref.shape[0]
    slots = high_ref.shape[0] - cases - 4
    share = spread(high_ref[cases:, :size], slots, width)
    zero = jnp.zeros_like(share)
    low, high = faces_in([zero, share, zero, zero])[2:]
    store_some(image_ref, [two_high(rest_ref[:, :size] + low), two_high(rest_ref[:, size:] - high)])


def direction_kernel(coarse_size, count, *refs):
    own = refs[0:4]
    near = refs[4:8]
    extra_ref, coupling_ref, residual_ref, hots_ref, flex_ref = refs[8:13]
    n = 13
    if count > 1:
        before_ref = refs[13]
        before_free = refs[14:18]
        n = 18
    precond_ref, free0, free1, free2, free3, result_ref = refs[n:]
    size = own[0].shape[1]
    cases = residual_ref.shape[0]
    slots = extra_ref.shape[0] - 4
    hots = hots_of(hots_ref)
    precond = jump(faces_in([x[...] for x in near]), faces_in([x[...] for x in own]))
    precond = [0.5 * x for x in precond]
    store(precond_ref, precond)
    forces = signed(precond)
    left = local_order(forces, hots, 2)
    product(flex_ref, result_ref, left[: count * cases], [(0, cases, count)])
    free = turned_result(result_ref, hots)
    extra = faces_of(extra_ref, size)
    for ref, value, rows in zip(
        (free0, free1, free2, free3), swapped(free, odds()), swapped(extra, odds())
    ):
        ref[:cases, :size] = value
        if count == 1:
            ref[cases:, :size] = rows
    scalars = [0.5 * total(faces_of(residual_ref, size), precond), total(forces, free)]
    if count > 1:
        before = signed(faces_of(before_ref, size))
        scalars.append(total(forces, faces_in([x[:cases, :size] for x in before_free])) + total(before, free))
    width = free3.shape[1] - size
    free3[:cases, size:] = partial_sums(
        left, coupling_ref[...], extra[0], slots, scalars, coarse_size, width
    )
    if count == 1:
        free3[cases:, size:] = jnp.zeros((free3.shape[0] - cases, width), jnp.float32)


def step_kernel(coarse_size, sums_ref, down_ref, up_ref, image_ref, rest_ref, own0, own1, own2, own3,
                near0, near1, near2, near3, residual_ref, hots_ref, schur_ref,
                new_ref, jump_ref, step_ref, send0, send1, send2, send3, result_ref):
    size = own0.shape[1]
    cases = sums_ref.shape[0]
    hots = hots_of(hots_ref)
    moved = jump(
        faces_in([x[:cases, :size] for x in (near0, near1, near2, near3)]),
        faces_in([x[:cases, :size] for x in (own0, own1, own2, own3)]),
    )
    store(jump_ref, moved)
    sums = sums_ref[...]
    coarse, energy = coarse_solve(coarse_part(sums, coarse_size), down_ref, up_ref)
    step = pick(sums, coarse_size) / (pick(sums, coarse_size + 1) + energy)
    step_ref[...] = jnp.broadcast_to(step, step_ref.shape)
    image = coarse_times(coarse, image_ref, rest_ref)
    residual = [
        residual_ref[:, i * size : (i + 1) * size]
        - step * (moved[i] + image[:, i * size : (i + 1) * size])
        for i in range(4)
    ]
    store(new_ref, residual)
    product(schur_ref, result_ref, local_order(weighted(residual), hots, 1), [(0, cases, 1)])
    for ref, value in zip(
        (send0, send1, send2, send3), swapped(turned_result(result_ref, hots), odds())
    ):
        ref[...] = value


def home_kernel(residual_ref, before_ref, precond_ref, jump_ref, image_ref, rest_ref, hots_ref,
                residual_out, before_out, precond_out, jump_out, image_out):
    size = hots_ref.shape[1]
    hots = hots_of(hots_ref)
    fields = [faces_of(x, size) for x in (residual_ref, before_ref, precond_ref, jump_ref)]
    image = [
        ref[:, block] for ref in (image_ref, rest_ref) for block in (slice(size), slice(size, None))
    ]
    for i in (0, 2):
        image[i] = mxu(image[i], hots[i]).astype(jnp.bfloat16)
        for field in fields:
            field[i] = turn_back(field[i], hots[i])
    store(image_out, image)
    for ref, field in zip((residual_out, before_out, precond_out, jump_out), fields):
        store(ref, field)


def last_kernel(coarse_size, first_ref, sums_ref, down_ref, up_ref, step_ref, residual_ref, before_ref,
                precond_ref, jump_ref, image_ref, hots_ref, own0, own1, own2, own3,
                near0, near1, near2, near3, multipliers_ref, out_ref):
    size = hots_ref.shape[1]
    hots = hots_of(hots_ref)
    following = jump(
        faces_in([x[:, :size] for x in (near0, near1, near2, near3)]),
        faces_in([x[:, :size] for x in (own0, own1, own2, own3)]),
    )
    for i in (0, 2):
        following[i] = turn_back(following[i], hots[i])
    first = first_ref[...]
    sums = sums_ref[...]
    beta = pick(sums, coarse_size) / pick(first, coarse_size)
    right = coarse_part(sums, coarse_size) + beta * coarse_part(first, coarse_size)
    coarse, energy = coarse_solve(right, down_ref, up_ref)
    local = pick(sums, coarse_size + 1) + beta * (
        pick(sums, coarse_size + 2) + beta * pick(first, coarse_size + 1)
    )
    step = pick(sums, coarse_size) / (local + energy)
    step_before = step_ref[:, 0:1]
    image = coarse_times(coarse, image_ref)
    for i in range(4):
        block = slice(i * size, (i + 1) * size)
        moved = following[i] + beta * jump_ref[:, block] + image[:, block]
        out_ref[:, i, :] = residual_ref[:, block] - step * moved
        before = before_ref[:, block]
        direction = precond_ref[:, block] + beta * before
        multipliers_ref[:, i, :] = step_before * before + step * direction


VMEM = pl.BlockSpec(memory_space=pltpu.VMEM)
OUTSIDE = pl.BlockSpec(memory_space=pltpu.HBM)


def call(kernel, args, outs, scratch=(), outside=(), flops=0):
    specs = [OUTSIDE if i in outside else VMEM for i in range(len(args))]
    shapes = [(x, jnp.float32) if isinstance(x[0], int) else x for x in outs]
    return pl.pallas_call(
        kernel,
        in_specs=specs,
        out_specs=[VMEM] * len(outs),
        out_shape=[jax.ShapeDtypeStruct(*x) for x in shapes],
        scratch_shapes=list(scratch),
        compiler_params=pltpu.CompilerParams(vmem_limit_bytes=28 * 2**20),
        cost_estimate=pl.CostEstimate(flops=flops, bytes_accessed=2**22, transcendentals=0),
    )(*args)


def shards(
    applied_loads,
    flex_matrix,
    schur_matrix,
    corner_coupling,
    coarse_inverse,
    face_match,
    corner_map,
):
    loads = applied_loads[0, 0]
    flex = flex_matrix[0, 0]
    schur = schur_matrix[0, 0]
    match = face_match[0, 0]
    cases, interface = loads.shape
    size = interface // 4
    slots = corner_coupling.shape[2]
    coarse_size = coarse_inverse.shape[0]
    width = -(-(coarse_size + 3) // LANES) * LANES
    work = 2 * cases * interface * interface

    inverse = jnp.pad(coarse_inverse, ((0, width - coarse_size), (0, width - coarse_size)))
    field = (cases, interface)
    face = (cases, size)
    result = pltpu.VMEM(field, jnp.float32)
    both_parts = ((2 * width, interface), jnp.bfloat16)

    held = [pltpu.with_memory_space_constraint(x, pltpu.HBM) for x in (loads, match, schur)]
    near = exchange(
        swapped([loads[:, i * size : (i + 1) * size] for i in range(4)], (odd("sub"), odd("grp")))
    )
    loads, hots, schur = call(
        prepare_kernel,
        held,
        [field, ((4 * size, size), jnp.bfloat16), (schur.shape, jnp.bfloat16)],
        [pltpu.VMEM(match.shape, jnp.int32), pltpu.SemaphoreType.DMA((3,))],
        outside=(0, 1, 2),
        flops=work,
    )
    residual, *own_first = call(
        first_kernel, [*near, loads, hots, schur], [field] + [face] * 4, [result], flops=work
    )
    near = exchange(own_first)
    residual, coupling, corners = lax.optimization_barrier(
        (residual, corner_coupling[0, 0], corner_map[0])
    )
    extra, own_spread, coupling, down, up = call(
        extra_kernel,
        [coupling, corners, inverse, hots],
        [
            (slots + 4, interface),
            (width, interface),
            ((3 * (slots + 4), interface), jnp.bfloat16),
            ((3 * width, width), jnp.bfloat16),
            ((width, 3 * width), jnp.bfloat16),
        ],
        flops=work // 4,
    )
    before, *own_free = call(
        functools.partial(direction_kernel, coarse_size, 1),
        [*own_first, *near, extra, coupling, residual, hots, flex],
        [field] + [(cases + slots + 4, size)] * 3 + [(cases + slots + 4, size + width)],
        [result],
        flops=work,
    )
    first_sums, near = sum_and_exchange(own_free, cases)
    half = ((2 * width, interface // 2), jnp.bfloat16)
    image, rest = call(
        functools.partial(coarse_kernel, cases),
        [own_spread, near[0], near[2], near[3]],
        [half, (width, interface // 2)],
        flops=work // 4,
    )
    (rest,) = call(
        functools.partial(coarse_rest_kernel, cases), [rest, near[1]], [half], flops=work // 8
    )
    residual, moved, step, *own = call(
        functools.partial(step_kernel, coarse_size),
        [first_sums, down, up, image, rest, *own_free, *near, residual, hots, schur],
        [field, field, (cases, LANES)] + [face] * 4,
        [result],
        flops=work,
    )
    near = exchange(own)
    precond, *own = call(
        functools.partial(direction_kernel, coarse_size, 2),
        [*own, *near, extra, coupling, residual, hots, flex, before, *own_free],
        [field] + [face] * 3 + [(cases, size + width)],
        [result],
        flops=work,
    )
    fields = call(
        home_kernel,
        [residual, before, precond, moved, image, rest, hots],
        [field] * 4 + [both_parts],
        flops=work // 2,
    )
    sums, near = sum_and_exchange(own, cases)
    layout = (cases, 4, size)
    multipliers, residual = call(
        functools.partial(last_kernel, coarse_size),
        [first_sums, sums, down, up, step, *fields, hots, *own, *near],
        [layout, layout],
        flops=work // 4,
    )
    return multipliers[None, None], residual[None, None]


def solution(mesh):
    return jax.shard_map(
        shards,
        mesh=mesh,
        in_specs=(
            P("sub", "grp", None, None),
            P("sub", "grp", None, None),
            P("sub", "grp", None, None),
            P("sub", "grp", None, None),
            P(),
            P("sub", "grp", None, None),
            P("sub", "grp", None),
        ),
        out_specs=(P("sub", "grp", None, None, None), P("sub", "grp", None, None, None)),
        check_vma=False,
    )
```

```python
import functools

import jax
import jax.numpy as jnp
from jax import lax
from jax.experimental import pallas as pl
from jax.experimental.pallas import tpu as pltpu
from jax.sharding import PartitionSpec as P

HIGHEST = lax.Precision.HIGHEST
PLAIN = (((1,), (0,)), ((), ()))
LAST = (((1,), (1,)), ((), ()))
LANES = 128
SIGNS = (-1.0, 1.0, -1.0, 1.0)


def odd(axis):
    return lax.axis_index(axis) % 2 == 1


def swapped(faces, odds):
    far, near = [], []
    for (low, high), is_odd in zip((faces[0:2], faces[2:4]), odds):
        far.append(jnp.where(is_odd, high, low))
        near.append(jnp.where(is_odd, low, high))
    return far[::-1] + near


def swap(face, i):
    axis = ("grp", "sub", "sub", "grp")[i]
    peers = lax.axis_size(axis)
    if i < 2:
        pairs = [(j, (j + 2 * (j % 2) - 1) % peers) for j in range(peers)]
    else:
        pairs = [(j, j ^ 1) for j in range(peers)]
    return lax.ppermute(face, axis, pairs)


def exchange(faces):
    return [swap(face, i) for i, face in enumerate(faces)]


def sum_over(values, axis, step, before=(), after=()):
    peers = lax.axis_size(axis)
    first = True
    while step < peers:
        count = 4 if 4 * step <= peers else 2
        others = [
            lax.ppermute(values, axis, [(i, i ^ (k * step)) for i in range(peers)])
            for k in ((2, 1, 3) if count == 4 else (1,))
        ]
        if first:
            before, others, after = lax.optimization_barrier((before, others, after))
            first = False
        if count == 4:
            values = (values + others[1]) + (others[0] + others[2])
        else:
            values = values + others[0]
        step *= count
    return values, before, after


def sum_and_exchange(faces, cases):
    high, far, near, core = faces
    size = near.shape[1]
    other = swap(core, 3)
    values = core[:cases, size:] + other[:cases, size:]
    near, values = lax.optimization_barrier((near, values))
    values, far, near = sum_over(values, "grp", 2, [swap(far, 1)], [swap(near, 2)])
    far, near, high, values = lax.optimization_barrier((far, near, high, values))
    values, high, _ = sum_over(values, "sub", 1, [swap(high, 0)])
    return values, [*high, *far, *near, other]


def one_hot(match_ref, i):
    row = match_ref[i : i + 1, :]
    size = row.shape[1]
    nodes = lax.broadcasted_iota(jnp.int32, (size, size), 0)
    return jnp.where(nodes == row, 1.0, 0.0).astype(jnp.bfloat16)


def parts(x, count):
    out = []
    for _ in range(count):
        part = x.astype(jnp.bfloat16)
        out.append(part)
        x = x - part.astype(jnp.float32)
    return out


def mxu(x, y, dims=PLAIN):
    return lax.dot_general(x, y, dims, preferred_element_type=jnp.float32)


def exact(x, y, dims=PLAIN):
    return lax.dot_general(x, y, dims, precision=HIGHEST, preferred_element_type=jnp.float32)


def reorder(x, hot, dims):
    rows = x.shape[0]
    both = mxu(jnp.concatenate(parts(x, 3), axis=0), hot, dims)
    return both[:rows] + both[rows : 2 * rows] + both[2 * rows :]


def turn(x, hot):
    return reorder(x, hot, LAST)


def turn_back(x, hot):
    return reorder(x, hot, PLAIN)


def jump(received, own):
    return [
        received[0] - own[0],
        own[1] - received[1],
        received[2] - own[2],
        own[3] - received[3],
    ]


def odds():
    return odd("sub"), odd("grp")


def faces_in(values):
    out = []
    for far, near, is_odd in zip(values[1::-1], values[2:4], odds()):
        out += [jnp.where(is_odd, near, far), jnp.where(is_odd, far, near)]
    return out


def faces_of(ref, size):
    return [ref[:, i * size : (i + 1) * size] for i in range(4)]


def store(ref, faces):
    size = faces[0].shape[1]
    for i in range(4):
        ref[:, i * size : (i + 1) * size] = faces[i]


def store_some(ref, faces):
    size = faces[0].shape[1]
    for i, face in enumerate(faces):
        ref[:, i * size : (i + 1) * size] = face


def total(xs, ys):
    return sum(jnp.sum(x * y, axis=1, keepdims=True) for x, y in zip(xs, ys))


def blocks_of(interface):
    width = 256 if interface % 256 == 0 else interface
    return [slice(i, i + width) for i in range(0, interface, width)]


def product(matrix_ref, result_ref, left, groups):
    for block in blocks_of(matrix_ref.shape[1]):
        both = mxu(left, matrix_ref[:, block])
        at = 0
        for first, rows, count in groups:
            value = both[first : first + rows]
            for i in range(1, count):
                value = value + both[first + i * rows : first + (i + 1) * rows]
            result_ref[at : at + rows, block] = value
            at += rows


def local_order(faces, hots, count):
    split = [jnp.concatenate(parts(x, count), axis=0) for x in faces]
    split[0] = mxu(split[0], hots[0]).astype(jnp.bfloat16)
    split[2] = mxu(split[2], hots[2]).astype(jnp.bfloat16)
    return jnp.concatenate(split, axis=1)


def turned_result(result_ref, hots):
    size = result_ref.shape[1] // 4
    own = faces_of(result_ref, size)
    own[0] = turn(own[0], hots[0])
    own[2] = turn(own[2], hots[2])
    return own


def weighted(faces):
    return [(0.5 * s) * x for s, x in zip(SIGNS, faces)]


def hots_of(hots_ref):
    size = hots_ref.shape[1]
    return [hots_ref[i * size : (i + 1) * size, :] for i in range(4)]


def signed(faces):
    return [s * x for s, x in zip(SIGNS, faces)]


def lane_is(shape, lane):
    return lax.broadcasted_iota(jnp.int32, shape, 1) == lane


def pick(values, lane):
    return jnp.sum(jnp.where(lane_is(values.shape, lane), values, 0.0), axis=1, keepdims=True)


def numbering(extra, slots, width):
    numbers = extra[slots : slots + 1, :LANES]
    nodes = lax.broadcasted_iota(jnp.int32, (width, LANES), 0).astype(jnp.float32)
    hot = jnp.where(nodes == numbers, 1.0, 0.0)
    return hot[:, : 3 * extra.shape[0]].astype(jnp.bfloat16)


def spread(extra, slots, width):
    return mxu(numbering(extra, slots, width), jnp.concatenate(parts(extra, 3), axis=0))


def partial_sums(left, coupling, extra, slots, scalars, coarse_size, width):
    out = reorder(mxu(left, coupling, LAST), numbering(extra, slots, width), LAST)
    rows = out.shape[0] // 2
    out = out[:rows] + out[rows:]
    for i, value in enumerate(scalars):
        out = out + jnp.where(lane_is(out.shape, coarse_size + i), value, 0.0)
    return out


def by_parts(x, matrix, dims):
    rows = x.shape[0]
    both = mxu(jnp.concatenate(parts(x, 3), axis=0), matrix, dims)
    both = both[:rows] + (both[rows : 2 * rows] + both[2 * rows :])
    width = both.shape[1] // 3
    return both[:, :width] + (both[:, width : 2 * width] + both[:, 2 * width :])


def coarse_solve(right, down_ref, up_ref):
    lowered = by_parts(right, down_ref[...], LAST)
    return by_parts(lowered, up_ref[...], PLAIN), jnp.sum(lowered * lowered, axis=1, keepdims=True)


def coarse_part(sums, coarse_size):
    lanes = lax.broadcasted_iota(jnp.int32, sums.shape, 1)
    return jnp.where(lanes < coarse_size, sums, 0.0)


def two_high(x):
    return jnp.concatenate(parts(x, 2), axis=0)


def two_wide(x):
    high, low = parts(x, 2)
    return jnp.concatenate(
        [jnp.concatenate([high, high], axis=1), jnp.concatenate([low, low], axis=1)], axis=0
    )


def coarse_times(coarse, *image_refs):
    rows = coarse.shape[0]
    left = two_wide(coarse)
    both = [mxu(left, image[...]) for image in image_refs]
    return jnp.concatenate([x[:rows] + x[rows:] for x in both], axis=1)


def prepare_kernel(loads_ref, match_ref, schur_ref,
                   loads_out, hots_out, schur_out, match_held, sems):
    copies = [
        pltpu.make_async_copy(x, y, sems.at[i])
        for i, (x, y) in enumerate(
            ((match_ref, match_held), (loads_ref, loads_out), (schur_ref, schur_out))
        )
    ]
    for copy in copies:
        copy.start()
    size = loads_ref.shape[1] // 4
    copies[0].wait()
    for i in range(4):
        hots_out[i * size : (i + 1) * size, :] = one_hot(match_held, i)
    copies[1].wait()
    for i in (0, 2):
        block = slice(i * size, (i + 1) * size)
        loads_out[:, block] = turn(loads_out[:, block], hots_out[block, :])
    copies[2].wait()


def extra_kernel(coupling_ref, corners_ref, inverse_ref, hots_ref,
                 extra_out, spread_out, coupling_out, down_out, up_out):
    size = hots_ref.shape[1]
    slots = coupling_ref.shape[0]
    rows = extra_out.shape[0]
    hots = hots_of(hots_ref)
    extra_out[...] = jnp.full(extra_out.shape, -1.0, jnp.float32)
    corners = corners_ref[...].astype(jnp.float32)
    for i in range(4):
        extra_out[:slots, i * size : (i + 1) * size] = coupling_ref[:, i * size : (i + 1) * size]
        for k in range(3):
            at = i * size + k * rows
            extra_out[slots : slots + 1, at : at + slots] = corners
    coupling_out[...] = jnp.concatenate(parts(extra_out[...], 3), axis=0)
    for i in (0, 2):
        block = slice(i * size, (i + 1) * size)
        extra_out[:slots, block] = turn(coupling_ref[:, block], hots[i])
    spread_out[...] = spread(extra_out[...], slots, spread_out.shape[0])
    inverse = parts(inverse_ref[...], 3)
    down_out[...] = jnp.concatenate(inverse, axis=0)
    up_out[...] = jnp.concatenate(inverse, axis=1)


def first_kernel(near0, near1, near2, near3, loads_ref, hots_ref, schur_ref,
                 residual_ref, send0, send1, send2, send3, result_ref):
    cases = loads_ref.shape[0]
    size = loads_ref.shape[1] // 4
    hots = hots_of(hots_ref)
    near = faces_in([x[...] for x in (near0, near1, near2, near3)])
    for i in (1, 3):
        near[i] = reorder(near[i], hots[i], PLAIN)
    residual = jump(near, faces_of(loads_ref, size))
    store(residual_ref, residual)
    product(schur_ref, result_ref, local_order(weighted(residual), hots, 1), [(0, cases, 1)])
    for ref, value in zip(
        (send0, send1, send2, send3), swapped(turned_result(result_ref, hots), odds())
    ):
        ref[...] = value


def coarse_kernel(cases, spread_ref, far_ref, near_ref, core_ref, image_ref, rest_ref):
    width, interface = spread_ref.shape
    size = interface // 4
    slots = near_ref.shape[0] - cases - 4
    own = faces_of(spread_ref, size)
    far, near, core = [
        spread(x[cases:, :size], slots, width) for x in (far_ref, near_ref, core_ref)
    ]
    zero = jnp.zeros_like(core)
    image = jump(faces_in([zero, far, near, core]), own)
    store_some(image_ref, [two_high(x) for x in image[:2]])
    store_some(rest_ref, image[2:])


def coarse_rest_kernel(cases, rest_ref, high_ref, image_ref):
    size = rest_ref.shape[1] // 2
    width = rest_ref.shape[0]
    slots = high_ref.shape[0] - cases - 4
    share = spread(high_ref[cases:, :size], slots, width)
    zero = jnp.zeros_like(share)
    low, high = faces_in([share, zero, zero, zero])[2:]
    store_some(image_ref, [two_high(rest_ref[:, :size] + low), two_high(rest_ref[:, size:] - high)])


def direction_kernel(coarse_size, count, *refs):
    own = refs[0:4]
    near = refs[4:8]
    extra_ref, coupling_ref, residual_ref, hots_ref, flex_ref = refs[8:13]
    n = 13
    if count > 1:
        before_ref = refs[13]
        before_free = refs[14:18]
        n = 18
    precond_ref, free0, free1, free2, free3, result_ref = refs[n:]
    size = own[0].shape[1]
    cases = residual_ref.shape[0]
    slots = extra_ref.shape[0] - 4
    hots = hots_of(hots_ref)
    precond = jump(faces_in([x[...] for x in near]), faces_in([x[...] for x in own]))
    precond = [0.5 * x for x in precond]
    store(precond_ref, precond)
    forces = signed(precond)
    left = local_order(forces, hots, 2)
    product(flex_ref, result_ref, left[: count * cases], [(0, cases, count)])
    free = turned_result(result_ref, hots)
    extra = faces_of(extra_ref, size)
    for ref, value, rows in zip(
        (free0, free1, free2, free3), swapped(free, odds()), swapped(extra, odds())
    ):
        ref[:cases, :size] = value
        if count == 1:
            ref[cases:, :size] = rows
    scalars = [0.5 * total(faces_of(residual_ref, size), precond), total(forces, free)]
    if count > 1:
        before = signed(faces_of(before_ref, size))
        scalars.append(total(forces, faces_in([x[:cases, :size] for x in before_free])) + total(before, free))
    width = free3.shape[1] - size
    free3[:cases, size:] = partial_sums(
        left, coupling_ref[...], extra[0], slots, scalars, coarse_size, width
    )
    if count == 1:
        free3[cases:, size:] = jnp.zeros((free3.shape[0] - cases, width), jnp.float32)


def step_kernel(coarse_size, sums_ref, down_ref, up_ref, image_ref, rest_ref, own0, own1, own2, own3,
                near0, near1, near2, near3, residual_ref, hots_ref, schur_ref,
                new_ref, jump_ref, step_ref, send0, send1, send2, send3, result_ref):
    size = own0.shape[1]
    cases = sums_ref.shape[0]
    hots = hots_of(hots_ref)
    moved = jump(
        faces_in([x[:cases, :size] for x in (near0, near1, near2, near3)]),
        faces_in([x[:cases, :size] for x in (own0, own1, own2, own3)]),
    )
    store(jump_ref, moved)
    sums = sums_ref[...]
    coarse, energy = coarse_solve(coarse_part(sums, coarse_size), down_ref, up_ref)
    step = pick(sums, coarse_size) / (pick(sums, coarse_size + 1) + energy)
    step_ref[...] = jnp.broadcast_to(step, step_ref.shape)
    image = coarse_times(coarse, image_ref, rest_ref)
    residual = [
        residual_ref[:, i * size : (i + 1) * size]
        - step * (moved[i] + image[:, i * size : (i + 1) * size])
        for i in range(4)
    ]
    store(new_ref, residual)
    product(schur_ref, result_ref, local_order(weighted(residual), hots, 1), [(0, cases, 1)])
    for ref, value in zip(
        (send0, send1, send2, send3), swapped(turned_result(result_ref, hots), odds())
    ):
        ref[...] = value


def home_kernel(residual_ref, before_ref, precond_ref, jump_ref, image_ref, rest_ref, hots_ref,
                residual_out, before_out, precond_out, jump_out, image_out):
    size = hots_ref.shape[1]
    hots = hots_of(hots_ref)
    fields = [faces_of(x, size) for x in (residual_ref, before_ref, precond_ref, jump_ref)]
    image = [
        ref[:, block] for ref in (image_ref, rest_ref) for block in (slice(size), slice(size, None))
    ]
    for i in (0, 2):
        image[i] = mxu(image[i], hots[i]).astype(jnp.bfloat16)
        for field in fields:
            field[i] = turn_back(field[i], hots[i])
    store(image_out, image)
    for ref, field in zip((residual_out, before_out, precond_out, jump_out), fields):
        store(ref, field)


def last_kernel(coarse_size, first_ref, sums_ref, down_ref, up_ref, step_ref, residual_ref, before_ref,
                precond_ref, jump_ref, image_ref, hots_ref, own0, own1, own2, own3,
                near0, near1, near2, near3, multipliers_ref, out_ref):
    size = hots_ref.shape[1]
    hots = hots_of(hots_ref)
    following = jump(
        faces_in([x[:, :size] for x in (near0, near1, near2, near3)]),
        faces_in([x[:, :size] for x in (own0, own1, own2, own3)]),
    )
    for i in (0, 2):
        following[i] = turn_back(following[i], hots[i])
    first = first_ref[...]
    sums = sums_ref[...]
    beta = pick(sums, coarse_size) / pick(first, coarse_size)
    right = coarse_part(sums, coarse_size) + beta * coarse_part(first, coarse_size)
    coarse, energy = coarse_solve(right, down_ref, up_ref)
    local = pick(sums, coarse_size + 1) + beta * (
        pick(sums, coarse_size + 2) + beta * pick(first, coarse_size + 1)
    )
    step = pick(sums, coarse_size) / (local + energy)
    step_before = step_ref[:, 0:1]
    image = coarse_times(coarse, image_ref)
    for i in range(4):
        block = slice(i * size, (i + 1) * size)
        moved = following[i] + beta * jump_ref[:, block] + image[:, block]
        out_ref[:, i, :] = residual_ref[:, block] - step * moved
        before = before_ref[:, block]
        direction = precond_ref[:, block] + beta * before
        multipliers_ref[:, i, :] = step_before * before + step * direction


VMEM = pl.BlockSpec(memory_space=pltpu.VMEM)
OUTSIDE = pl.BlockSpec(memory_space=pltpu.HBM)


def call(kernel, args, outs, scratch=(), outside=(), flops=0):
    specs = [OUTSIDE if i in outside else VMEM for i in range(len(args))]
    shapes = [(x, jnp.float32) if isinstance(x[0], int) else x for x in outs]
    return pl.pallas_call(
        kernel,
        in_specs=specs,
        out_specs=[VMEM] * len(outs),
        out_shape=[jax.ShapeDtypeStruct(*x) for x in shapes],
        scratch_shapes=list(scratch),
        compiler_params=pltpu.CompilerParams(vmem_limit_bytes=28 * 2**20),
        cost_estimate=pl.CostEstimate(flops=flops, bytes_accessed=2**22, transcendentals=0),
    )(*args)


def shards(
    applied_loads,
    flex_matrix,
    schur_matrix,
    corner_coupling,
    coarse_inverse,
    face_match,
    corner_map,
):
    loads = applied_loads[0, 0]
    flex = flex_matrix[0, 0]
    schur = schur_matrix[0, 0]
    match = face_match[0, 0]
    cases, interface = loads.shape
    size = interface // 4
    slots = corner_coupling.shape[2]
    coarse_size = coarse_inverse.shape[0]
    width = -(-(coarse_size + 3) // LANES) * LANES
    work = 2 * cases * interface * interface

    inverse = jnp.pad(coarse_inverse, ((0, width - coarse_size), (0, width - coarse_size)))
    field = (cases, interface)
    face = (cases, size)
    result = pltpu.VMEM(field, jnp.float32)
    both_parts = ((2 * width, interface), jnp.bfloat16)

    held = [pltpu.with_memory_space_constraint(x, pltpu.HBM) for x in (loads, match, schur)]
    near = exchange(
        swapped([loads[:, i * size : (i + 1) * size] for i in range(4)], (odd("sub"), odd("grp")))
    )
    loads, hots, schur = call(
        prepare_kernel,
        held,
        [field, ((4 * size, size), jnp.bfloat16), (schur.shape, jnp.bfloat16)],
        [pltpu.VMEM(match.shape, jnp.int32), pltpu.SemaphoreType.DMA((3,))],
        outside=(0, 1, 2),
        flops=work,
    )
    residual, *own_first = call(
        first_kernel, [*near, loads, hots, schur], [field] + [face] * 4, [result], flops=work
    )
    near = exchange(own_first)
    residual, coupling, corners = lax.optimization_barrier(
        (residual, corner_coupling[0, 0], corner_map[0])
    )
    extra, own_spread, coupling, down, up = call(
        extra_kernel,
        [coupling, corners, inverse, hots],
        [
            (slots + 4, interface),
            (width, interface),
            ((3 * (slots + 4), interface), jnp.bfloat16),
            ((3 * width, width), jnp.bfloat16),
            ((width, 3 * width), jnp.bfloat16),
        ],
        flops=work // 4,
    )
    before, *own_free = call(
        functools.partial(direction_kernel, coarse_size, 1),
        [*own_first, *near, extra, coupling, residual, hots, flex],
        [field] + [(cases + slots + 4, size)] * 3 + [(cases + slots + 4, size + width)],
        [result],
        flops=work,
    )
    first_sums, near = sum_and_exchange(own_free, cases)
    half = ((2 * width, interface // 2), jnp.bfloat16)
    image, rest = call(
        functools.partial(coarse_kernel, cases),
        [own_spread, *near[1:]],
        [half, (width, interface // 2)],
        flops=work // 4,
    )
    (rest,) = call(
        functools.partial(coarse_rest_kernel, cases), [rest, near[0]], [half], flops=work // 8
    )
    residual, moved, step, *own = call(
        functools.partial(step_kernel, coarse_size),
        [first_sums, down, up, image, rest, *own_free, *near, residual, hots, schur],
        [field, field, (cases, LANES)] + [face] * 4,
        [result],
        flops=work,
    )
    near = exchange(own)
    precond, *own = call(
        functools.partial(direction_kernel, coarse_size, 2),
        [*own, *near, extra, coupling, residual, hots, flex, before, *own_free],
        [field] + [face] * 3 + [(cases, size + width)],
        [result],
        flops=work,
    )
    fields = call(
        home_kernel,
        [residual, before, precond, moved, image, rest, hots],
        [field] * 4 + [both_parts],
        flops=work // 2,
    )
    sums, near = sum_and_exchange(own, cases)
    layout = (cases, 4, size)
    multipliers, residual = call(
        functools.partial(last_kernel, coarse_size),
        [first_sums, sums, down, up, step, *fields, hots, *own, *near],
        [layout, layout],
        flops=work // 4,
    )
    return multipliers[None, None], residual[None, None]


def solution(mesh):
    return jax.shard_map(
        shards,
        mesh=mesh,
        in_specs=(
            P("sub", "grp", None, None),
            P("sub", "grp", None, None),
            P("sub", "grp", None, None),
            P("sub", "grp", None, None),
            P(),
            P("sub", "grp", None, None),
            P("sub", "grp", None),
        ),
        out_specs=(P("sub", "grp", None, None, None), P("sub", "grp", None, None, None)),
        check_vma=False,
    )
```

```python
import functools

import jax
import jax.numpy as jnp
from jax import lax
from jax.experimental import pallas as pl
from jax.experimental.pallas import tpu as pltpu
from jax.sharding import PartitionSpec as P

HIGHEST = lax.Precision.HIGHEST
PLAIN = (((1,), (0,)), ((), ()))
LAST = (((1,), (1,)), ((), ()))
LANES = 128
SIGNS = (-1.0, 1.0, -1.0, 1.0)


def odd(axis):
    return lax.axis_index(axis) % 2 == 1


def swapped(faces, odds):
    far, near = [], []
    for (low, high), is_odd in zip((faces[0:2], faces[2:4]), odds):
        far.append(jnp.where(is_odd, high, low))
        near.append(jnp.where(is_odd, low, high))
    return far + near


def swap(face, i):
    axis = ("sub", "grp", "sub", "grp")[i]
    peers = lax.axis_size(axis)
    if i < 2:
        pairs = [(j, (j + 2 * (j % 2) - 1) % peers) for j in range(peers)]
    else:
        pairs = [(j, j ^ 1) for j in range(peers)]
    return lax.ppermute(face, axis, pairs)


def exchange(faces):
    grp_far, far, near, core = lax.optimization_barrier([swap(faces[i], i) for i in (1, 0, 2, 3)])
    return [far, grp_far, near, core]


def sum_over(values, axis, step, before=(), after=()):
    peers, width = lax.axis_size("sub"), lax.axis_size("grp")

    def target(i, j, far):
        if j % 2 == 0:
            return i * width + j
        return (i ^ far) * width + j if axis == "sub" else i * width + (j ^ far)

    first = True
    while step < lax.axis_size(axis):
        count = 4 if 4 * step <= lax.axis_size(axis) else 2
        others = [
            lax.ppermute(
                values,
                ("sub", "grp"),
                [
                    (i * width + j, target(i, j, k * step))
                    for i in range(peers)
                    for j in range(width)
                ],
            )
            for k in ((2, 1, 3) if count == 4 else (1,))
        ]
        if first:
            before, others, after = lax.optimization_barrier((before, others, after))
            first = False
        if count == 4:
            values = (values + others[1]) + (others[0] + others[2])
        else:
            values = values + others[0]
        step *= count
    return values, before, after


def sum_and_exchange(faces, cases):
    far, high, near, core = faces
    size = near.shape[1]
    other = swap(core, 3)
    values = core[:cases, size:] + other[:cases, size:]
    near, values = lax.optimization_barrier((near, values))
    values, far, near = sum_over(values, "grp", 2, [swap(far, 0)], [swap(near, 2)])
    far, near, high, values = lax.optimization_barrier((far, near, high, values))
    values, high, _ = sum_over(values, "sub", 1, [swap(high, 1)])
    return [values, swap(values, 3)], [*far, *high, *near, other]


def one_hot(match_ref, i):
    row = match_ref[i : i + 1, :]
    size = row.shape[1]
    nodes = lax.broadcasted_iota(jnp.int32, (size, size), 0)
    return jnp.where(nodes == row, 1.0, 0.0).astype(jnp.bfloat16)


def parts(x, count):
    out = []
    for _ in range(count):
        part = x.astype(jnp.bfloat16)
        out.append(part)
        x = x - part.astype(jnp.float32)
    return out


def mxu(x, y, dims=PLAIN):
    return lax.dot_general(x, y, dims, preferred_element_type=jnp.float32)


def exact(x, y, dims=PLAIN):
    return lax.dot_general(x, y, dims, precision=HIGHEST, preferred_element_type=jnp.float32)


def reorder(x, hot, dims):
    rows = x.shape[0]
    both = mxu(jnp.concatenate(parts(x, 3), axis=0), hot, dims)
    return both[:rows] + both[rows : 2 * rows] + both[2 * rows :]


def turn(x, hot):
    return reorder(x, hot, LAST)


def turn_back(x, hot):
    return reorder(x, hot, PLAIN)


def jump(received, own):
    return [
        received[0] - own[0],
        own[1] - received[1],
        received[2] - own[2],
        own[3] - received[3],
    ]


def odds():
    return odd("sub"), odd("grp")


def faces_in(values):
    out = []
    for far, near, is_odd in zip(values[0:2], values[2:4], odds()):
        out += [jnp.where(is_odd, near, far), jnp.where(is_odd, far, near)]
    return out


def faces_of(ref, size):
    return [ref[:, i * size : (i + 1) * size] for i in range(4)]


def store(ref, faces):
    size = faces[0].shape[1]
    for i in range(4):
        ref[:, i * size : (i + 1) * size] = faces[i]


def store_some(ref, faces):
    size = faces[0].shape[1]
    for i, face in enumerate(faces):
        ref[:, i * size : (i + 1) * size] = face


def total(xs, ys):
    return sum(jnp.sum(x * y, axis=1, keepdims=True) for x, y in zip(xs, ys))


def blocks_of(interface):
    width = 256 if interface % 256 == 0 else interface
    return [slice(i, i + width) for i in range(0, interface, width)]


def product(matrix_ref, result_ref, left, groups):
    for block in blocks_of(matrix_ref.shape[1]):
        both = mxu(left, matrix_ref[:, block])
        at = 0
        for first, rows, count in groups:
            value = both[first : first + rows]
            for i in range(1, count):
                value = value + both[first + i * rows : first + (i + 1) * rows]
            result_ref[at : at + rows, block] = value
            at += rows


def local_order(faces, hots, count):
    split = [jnp.concatenate(parts(x, count), axis=0) for x in faces]
    split[0] = mxu(split[0], hots[0]).astype(jnp.bfloat16)
    split[2] = mxu(split[2], hots[2]).astype(jnp.bfloat16)
    return jnp.concatenate(split, axis=1)


def turned_result(result_ref, hots):
    size = result_ref.shape[1] // 4
    own = faces_of(result_ref, size)
    own[0] = turn(own[0], hots[0])
    own[2] = turn(own[2], hots[2])
    return own


def weighted(faces):
    return [(0.5 * s) * x for s, x in zip(SIGNS, faces)]


def hots_of(hots_ref):
    size = hots_ref.shape[1]
    return [hots_ref[i * size : (i + 1) * size, :] for i in range(4)]


def signed(faces):
    return [s * x for s, x in zip(SIGNS, faces)]


def lane_is(shape, lane):
    return lax.broadcasted_iota(jnp.int32, shape, 1) == lane


def pick(values, lane):
    return jnp.sum(jnp.where(lane_is(values.shape, lane), values, 0.0), axis=1, keepdims=True)


def numbering(extra, slots, width):
    numbers = extra[slots : slots + 1, :LANES]
    nodes = lax.broadcasted_iota(jnp.int32, (width, LANES), 0).astype(jnp.float32)
    hot = jnp.where(nodes == numbers, 1.0, 0.0)
    return hot[:, : 3 * extra.shape[0]].astype(jnp.bfloat16)


def spread(extra, slots, width):
    return mxu(numbering(extra, slots, width), jnp.concatenate(parts(extra, 3), axis=0))


def partial_sums(left, coupling, extra, slots, scalars, coarse_size, width):
    out = reorder(mxu(left, coupling, LAST), numbering(extra, slots, width), LAST)
    rows = out.shape[0] // 2
    out = out[:rows] + out[rows:]
    for i, value in enumerate(scalars):
        out = out + jnp.where(lane_is(out.shape, coarse_size + i), value, 0.0)
    return out


def by_parts(x, matrix, dims):
    rows = x.shape[0]
    both = mxu(jnp.concatenate(parts(x, 3), axis=0), matrix, dims)
    both = both[:rows] + (both[rows : 2 * rows] + both[2 * rows :])
    width = both.shape[1] // 3
    return both[:, :width] + (both[:, width : 2 * width] + both[:, 2 * width :])


def coarse_solve(right, down_ref, up_ref):
    lowered = by_parts(right, down_ref[...], LAST)
    return by_parts(lowered, up_ref[...], PLAIN), jnp.sum(lowered * lowered, axis=1, keepdims=True)


def coarse_part(sums, coarse_size):
    lanes = lax.broadcasted_iota(jnp.int32, sums.shape, 1)
    return jnp.where(lanes < coarse_size, sums, 0.0)


def two_high(x):
    return jnp.concatenate(parts(x, 2), axis=0)


def two_wide(x):
    high, low = parts(x, 2)
    return jnp.concatenate(
        [jnp.concatenate([high, high], axis=1), jnp.concatenate([low, low], axis=1)], axis=0
    )


def coarse_times(coarse, *image_refs):
    rows = coarse.shape[0]
    left = two_wide(coarse)
    both = [mxu(left, image[...]) for image in image_refs]
    return jnp.concatenate([x[:rows] + x[rows:] for x in both], axis=1)


def prepare_kernel(loads_ref, match_ref, schur_ref,
                   loads_out, hots_out, schur_out, match_held, sems):
    copies = [
        pltpu.make_async_copy(x, y, sems.at[i])
        for i, (x, y) in enumerate(
            ((match_ref, match_held), (loads_ref, loads_out), (schur_ref, schur_out))
        )
    ]
    for copy in copies:
        copy.start()
    size = loads_ref.shape[1] // 4
    copies[0].wait()
    for i in range(4):
        hots_out[i * size : (i + 1) * size, :] = one_hot(match_held, i)
    copies[1].wait()
    for i in (0, 2):
        block = slice(i * size, (i + 1) * size)
        loads_out[:, block] = turn(loads_out[:, block], hots_out[block, :])
    copies[2].wait()


def extra_kernel(coupling_ref, corners_ref, inverse_ref, hots_ref,
                 extra_out, spread_out, coupling_out, down_out, up_out):
    size = hots_ref.shape[1]
    slots = coupling_ref.shape[0]
    rows = extra_out.shape[0]
    hots = hots_of(hots_ref)
    extra_out[...] = jnp.full(extra_out.shape, -1.0, jnp.float32)
    corners = corners_ref[...].astype(jnp.float32)
    for i in range(4):
        extra_out[:slots, i * size : (i + 1) * size] = coupling_ref[:, i * size : (i + 1) * size]
        for k in range(3):
            at = i * size + k * rows
            extra_out[slots : slots + 1, at : at + slots] = corners
    coupling_out[...] = jnp.concatenate(parts(extra_out[...], 3), axis=0)
    for i in (0, 2):
        block = slice(i * size, (i + 1) * size)
        extra_out[:slots, block] = turn(coupling_ref[:, block], hots[i])
    spread_out[...] = spread(extra_out[...], slots, spread_out.shape[0])
    inverse = parts(inverse_ref[...], 3)
    down_out[...] = jnp.concatenate(inverse, axis=0)
    up_out[...] = jnp.concatenate(inverse, axis=1)


def first_kernel(near0, near1, near2, near3, loads_ref, hots_ref, schur_ref,
                 residual_ref, send0, send1, send2, send3, result_ref):
    cases = loads_ref.shape[0]
    size = loads_ref.shape[1] // 4
    hots = hots_of(hots_ref)
    near = faces_in([x[...] for x in (near0, near1, near2, near3)])
    for i in (1, 3):
        near[i] = reorder(near[i], hots[i], PLAIN)
    residual = jump(near, faces_of(loads_ref, size))
    store(residual_ref, residual)
    product(schur_ref, result_ref, local_order(weighted(residual), hots, 1), [(0, cases, 1)])
    for ref, value in zip(
        (send0, send1, send2, send3), swapped(turned_result(result_ref, hots), odds())
    ):
        ref[...] = value


def coarse_kernel(cases, spread_ref, far_ref, near_ref, core_ref, image_ref, rest_ref):
    width, interface = spread_ref.shape
    size = interface // 4
    slots = near_ref.shape[0] - cases - 4
    own = faces_of(spread_ref, size)
    far, near, core = [
        spread(x[cases:, :size], slots, width) for x in (far_ref, near_ref, core_ref)
    ]
    zero = jnp.zeros_like(core)
    image = jump(faces_in([far, zero, near, core]), own)
    store_some(image_ref, [two_high(x) for x in image[:2]])
    store_some(rest_ref, image[2:])


def coarse_rest_kernel(cases, rest_ref, high_ref, image_ref):
    size = rest_ref.shape[1] // 2
    width = rest_ref.shape[0]
    slots = high_ref.shape[0] - cases - 4
    share = spread(high_ref[cases:, :size], slots, width)
    zero = jnp.zeros_like(share)
    low, high = faces_in([zero, share, zero, zero])[2:]
    store_some(image_ref, [two_high(rest_ref[:, :size] + low), two_high(rest_ref[:, size:] - high)])


def direction_kernel(coarse_size, count, *refs):
    own = refs[0:4]
    near = refs[4:8]
    extra_ref, coupling_ref, residual_ref, hots_ref, flex_ref = refs[8:13]
    n = 13
    if count > 1:
        before_ref = refs[13]
        before_free = refs[14:18]
        n = 18
    precond_ref, free0, free1, free2, free3, result_ref = refs[n:]
    size = own[0].shape[1]
    cases = residual_ref.shape[0]
    slots = extra_ref.shape[0] - 4
    hots = hots_of(hots_ref)
    precond = jump(faces_in([x[...] for x in near]), faces_in([x[...] for x in own]))
    precond = [0.5 * x for x in precond]
    store(precond_ref, precond)
    forces = signed(precond)
    left = local_order(forces, hots, 2)
    product(flex_ref, result_ref, left[: count * cases], [(0, cases, count)])
    free = turned_result(result_ref, hots)
    extra = faces_of(extra_ref, size)
    for ref, value, rows in zip(
        (free0, free1, free2, free3), swapped(free, odds()), swapped(extra, odds())
    ):
        ref[:cases, :size] = value
        if count == 1:
            ref[cases:, :size] = rows
    scalars = [0.5 * total(faces_of(residual_ref, size), precond), total(forces, free)]
    if count > 1:
        before = signed(faces_of(before_ref, size))
        scalars.append(total(forces, faces_in([x[:cases, :size] for x in before_free])) + total(before, free))
    width = free3.shape[1] - size
    free3[:cases, size:] = partial_sums(
        left, coupling_ref[...], extra[0], slots, scalars, coarse_size, width
    )
    if count == 1:
        free3[cases:, size:] = jnp.zeros((free3.shape[0] - cases, width), jnp.float32)


def step_kernel(coarse_size, sums_ref, other_ref, down_ref, up_ref, image_ref, rest_ref, own0, own1, own2, own3,
                near0, near1, near2, near3, residual_ref, hots_ref, schur_ref,
                total_ref, new_ref, jump_ref, step_ref, send0, send1, send2, send3, result_ref):
    size = own0.shape[1]
    cases = sums_ref.shape[0]
    hots = hots_of(hots_ref)
    moved = jump(
        faces_in([x[:cases, :size] for x in (near0, near1, near2, near3)]),
        faces_in([x[:cases, :size] for x in (own0, own1, own2, own3)]),
    )
    store(jump_ref, moved)
    sums = jnp.where(odd("grp"), sums_ref[...], other_ref[...])
    total_ref[...] = sums
    coarse, energy = coarse_solve(coarse_part(sums, coarse_size), down_ref, up_ref)
    step = pick(sums, coarse_size) / (pick(sums, coarse_size + 1) + energy)
    step_ref[...] = jnp.broadcast_to(step, step_ref.shape)
    image = coarse_times(coarse, image_ref, rest_ref)
    residual = [
        residual_ref[:, i * size : (i + 1) * size]
        - step * (moved[i] + image[:, i * size : (i + 1) * size])
        for i in range(4)
    ]
    store(new_ref, residual)
    product(schur_ref, result_ref, local_order(weighted(residual), hots, 1), [(0, cases, 1)])
    for ref, value in zip(
        (send0, send1, send2, send3), swapped(turned_result(result_ref, hots), odds())
    ):
        ref[...] = value


def home_kernel(residual_ref, before_ref, precond_ref, jump_ref, image_ref, rest_ref, hots_ref,
                residual_out, before_out, precond_out, jump_out, image_out):
    size = hots_ref.shape[1]
    hots = hots_of(hots_ref)
    fields = [faces_of(x, size) for x in (residual_ref, before_ref, precond_ref, jump_ref)]
    image = [
        ref[:, block] for ref in (image_ref, rest_ref) for block in (slice(size), slice(size, None))
    ]
    for i in (0, 2):
        image[i] = mxu(image[i], hots[i]).astype(jnp.bfloat16)
        for field in fields:
            field[i] = turn_back(field[i], hots[i])
    store(image_out, image)
    for ref, field in zip((residual_out, before_out, precond_out, jump_out), fields):
        store(ref, field)


def last_kernel(coarse_size, first_ref, sums_ref, other_ref, down_ref, up_ref, step_ref, residual_ref, before_ref,
                precond_ref, jump_ref, image_ref, hots_ref, own0, own1, own2, own3,
                near0, near1, near2, near3, multipliers_ref, out_ref):
    size = hots_ref.shape[1]
    hots = hots_of(hots_ref)
    following = jump(
        faces_in([x[:, :size] for x in (near0, near1, near2, near3)]),
        faces_in([x[:, :size] for x in (own0, own1, own2, own3)]),
    )
    for i in (0, 2):
        following[i] = turn_back(following[i], hots[i])
    first = first_ref[...]
    sums = jnp.where(odd("grp"), sums_ref[...], other_ref[...])
    beta = pick(sums, coarse_size) / pick(first, coarse_size)
    right = coarse_part(sums, coarse_size) + beta * coarse_part(first, coarse_size)
    coarse, energy = coarse_solve(right, down_ref, up_ref)
    local = pick(sums, coarse_size + 1) + beta * (
        pick(sums, coarse_size + 2) + beta * pick(first, coarse_size + 1)
    )
    step = pick(sums, coarse_size) / (local + energy)
    step_before = step_ref[:, 0:1]
    image = coarse_times(coarse, image_ref)
    for i in range(4):
        block = slice(i * size, (i + 1) * size)
        moved = following[i] + beta * jump_ref[:, block] + image[:, block]
        out_ref[:, i, :] = residual_ref[:, block] - step * moved
        before = before_ref[:, block]
        direction = precond_ref[:, block] + beta * before
        multipliers_ref[:, i, :] = step_before * before + step * direction


VMEM = pl.BlockSpec(memory_space=pltpu.VMEM)
OUTSIDE = pl.BlockSpec(memory_space=pltpu.HBM)


def call(kernel, args, outs, scratch=(), outside=(), flops=0):
    specs = [OUTSIDE if i in outside else VMEM for i in range(len(args))]
    shapes = [(x, jnp.float32) if isinstance(x[0], int) else x for x in outs]
    return pl.pallas_call(
        kernel,
        in_specs=specs,
        out_specs=[VMEM] * len(outs),
        out_shape=[jax.ShapeDtypeStruct(*x) for x in shapes],
        scratch_shapes=list(scratch),
        compiler_params=pltpu.CompilerParams(vmem_limit_bytes=28 * 2**20),
        cost_estimate=pl.CostEstimate(flops=flops, bytes_accessed=2**22, transcendentals=0),
    )(*args)


def shards(
    applied_loads,
    flex_matrix,
    schur_matrix,
    corner_coupling,
    coarse_inverse,
    face_match,
    corner_map,
):
    loads = applied_loads[0, 0]
    flex = flex_matrix[0, 0]
    schur = schur_matrix[0, 0]
    match = face_match[0, 0]
    cases, interface = loads.shape
    size = interface // 4
    slots = corner_coupling.shape[2]
    coarse_size = coarse_inverse.shape[0]
    width = -(-(coarse_size + 3) // LANES) * LANES
    work = 2 * cases * interface * interface

    inverse = jnp.pad(coarse_inverse, ((0, width - coarse_size), (0, width - coarse_size)))
    field = (cases, interface)
    face = (cases, size)
    result = pltpu.VMEM(field, jnp.float32)
    both_parts = ((2 * width, interface), jnp.bfloat16)

    held = [pltpu.with_memory_space_constraint(x, pltpu.HBM) for x in (loads, match, schur)]
    near = exchange(
        swapped([loads[:, i * size : (i + 1) * size] for i in range(4)], (odd("sub"), odd("grp")))
    )
    loads, hots, schur = call(
        prepare_kernel,
        held,
        [field, ((4 * size, size), jnp.bfloat16), (schur.shape, jnp.bfloat16)],
        [pltpu.VMEM(match.shape, jnp.int32), pltpu.SemaphoreType.DMA((3,))],
        outside=(0, 1, 2),
        flops=work,
    )
    residual, *own_first = call(
        first_kernel, [*near, loads, hots, schur], [field] + [face] * 4, [result], flops=work
    )
    near = exchange(own_first)
    residual, coupling, corners = lax.optimization_barrier(
        (residual, corner_coupling[0, 0], corner_map[0])
    )
    extra, own_spread, coupling, down, up = call(
        extra_kernel,
        [coupling, corners, inverse, hots],
        [
            (slots + 4, interface),
            (width, interface),
            ((3 * (slots + 4), interface), jnp.bfloat16),
            ((3 * width, width), jnp.bfloat16),
            ((width, 3 * width), jnp.bfloat16),
        ],
        flops=work // 4,
    )
    before, *own_free = call(
        functools.partial(direction_kernel, coarse_size, 1),
        [*own_first, *near, extra, coupling, residual, hots, flex],
        [field] + [(cases + slots + 4, size)] * 3 + [(cases + slots + 4, size + width)],
        [result],
        flops=work,
    )
    first_sums, near = sum_and_exchange(own_free, cases)
    half = ((2 * width, interface // 2), jnp.bfloat16)
    image, rest = call(
        functools.partial(coarse_kernel, cases),
        [own_spread, near[0], near[2], near[3]],
        [half, (width, interface // 2)],
        flops=work // 4,
    )
    (rest,) = call(
        functools.partial(coarse_rest_kernel, cases), [rest, near[1]], [half], flops=work // 8
    )
    first_sums, residual, moved, step, *own = call(
        functools.partial(step_kernel, coarse_size),
        [*first_sums, down, up, image, rest, *own_free, *near, residual, hots, schur],
        [(cases, width), field, field, (cases, LANES)] + [face] * 4,
        [result],
        flops=work,
    )
    near = exchange(own)
    precond, *own = call(
        functools.partial(direction_kernel, coarse_size, 2),
        [*own, *near, extra, coupling, residual, hots, flex, before, *own_free],
        [field] + [face] * 3 + [(cases, size + width)],
        [result],
        flops=work,
    )
    fields = call(
        home_kernel,
        [residual, before, precond, moved, image, rest, hots],
        [field] * 4 + [both_parts],
        flops=work // 2,
    )
    sums, near = sum_and_exchange(own, cases)
    layout = (cases, 4, size)
    multipliers, residual = call(
        functools.partial(last_kernel, coarse_size),
        [first_sums, *sums, down, up, step, *fields, hots, *own, *near],
        [layout, layout],
        flops=work // 4,
    )
    return multipliers[None, None], residual[None, None]


def solution(mesh):
    return jax.shard_map(
        shards,
        mesh=mesh,
        in_specs=(
            P("sub", "grp", None, None),
            P("sub", "grp", None, None),
            P("sub", "grp", None, None),
            P("sub", "grp", None, None),
            P(),
            P("sub", "grp", None, None),
            P("sub", "grp", None),
        ),
        out_specs=(P("sub", "grp", None, None, None), P("sub", "grp", None, None, None)),
        check_vma=False,
    )
```

```python
import functools

import jax
import jax.numpy as jnp
from jax import lax
from jax.experimental import pallas as pl
from jax.experimental.pallas import tpu as pltpu
from jax.sharding import PartitionSpec as P

HIGHEST = lax.Precision.HIGHEST
PLAIN = (((1,), (0,)), ((), ()))
LAST = (((1,), (1,)), ((), ()))
LANES = 128
SIGNS = (-1.0, 1.0, -1.0, 1.0)


def odd(axis):
    return lax.axis_index(axis) % 2 == 1


def swapped(faces, odds):
    far, near = [], []
    for (low, high), is_odd in zip((faces[0:2], faces[2:4]), odds):
        far.append(jnp.where(is_odd, high, low))
        near.append(jnp.where(is_odd, low, high))
    return far + near


def swap(face, i):
    axis = ("sub", "grp", "sub", "grp")[i]
    peers = lax.axis_size(axis)
    if i < 2:
        pairs = [(j, (j + 2 * (j % 2) - 1) % peers) for j in range(peers)]
    else:
        pairs = [(j, j ^ 1) for j in range(peers)]
    return lax.ppermute(face, axis, pairs)


def exchange(faces):
    grp_far, far, near, core = lax.optimization_barrier([swap(faces[i], i) for i in (1, 0, 2, 3)])
    return [far, grp_far, near, core]


def sum_over(values, axis, step, before=(), after=()):
    peers = lax.axis_size(axis)
    first = True
    while step < peers:
        count = 4 if 4 * step <= peers else 2
        others = [
            lax.ppermute(values, axis, [(i, i ^ (k * step)) for i in range(peers)])
            for k in ((2, 1, 3) if count == 4 else (1,))
        ]
        if first:
            before, others, after = lax.optimization_barrier((before, others, after))
            first = False
        if count == 4:
            values = (values + others[1]) + (others[0] + others[2])
        else:
            values = values + others[0]
        step *= count
    return values, before, after


def sum_and_exchange(faces, cases):
    far, high, near, core = faces
    size = near.shape[1]
    other = swap(core, 3)
    values = core[:cases, size:] + other[:cases, size:]
    near, values = lax.optimization_barrier((near, values))
    values, far, near = sum_over(values, "grp", 2, [swap(far, 0)], [swap(near, 2)])
    far, near, high, values = lax.optimization_barrier((far, near, high, values))
    values, high, _ = sum_over(values, "sub", 1, [swap(high, 1)])
    return values, [*far, *high, *near, other]


def one_hot(match_ref, i):
    row = match_ref[i : i + 1, :]
    size = row.shape[1]
    nodes = lax.broadcasted_iota(jnp.int32, (size, size), 0)
    return jnp.where(nodes == row, 1.0, 0.0).astype(jnp.bfloat16)


def parts(x, count):
    out = []
    for _ in range(count):
        part = x.astype(jnp.bfloat16)
        out.append(part)
        x = x - part.astype(jnp.float32)
    return out


def mxu(x, y, dims=PLAIN):
    return lax.dot_general(x, y, dims, preferred_element_type=jnp.float32)


def exact(x, y, dims=PLAIN):
    return lax.dot_general(x, y, dims, precision=HIGHEST, preferred_element_type=jnp.float32)


def reorder(x, hot, dims):
    rows = x.shape[0]
    both = mxu(jnp.concatenate(parts(x, 3), axis=0), hot, dims)
    return both[:rows] + both[rows : 2 * rows] + both[2 * rows :]


def turn(x, hot):
    return reorder(x, hot, LAST)


def turn_back(x, hot):
    return reorder(x, hot, PLAIN)


def jump(received, own):
    return [
        received[0] - own[0],
        own[1] - received[1],
        received[2] - own[2],
        own[3] - received[3],
    ]


def odds():
    return odd("sub"), odd("grp")


def faces_in(values):
    out = []
    for far, near, is_odd in zip(values[0:2], values[2:4], odds()):
        out += [jnp.where(is_odd, near, far), jnp.where(is_odd, far, near)]
    return out


def faces_of(ref, size):
    return [ref[:, i * size : (i + 1) * size] for i in range(4)]


def store(ref, faces):
    size = faces[0].shape[1]
    for i in range(4):
        ref[:, i * size : (i + 1) * size] = faces[i]


def store_some(ref, faces):
    size = faces[0].shape[1]
    for i, face in enumerate(faces):
        ref[:, i * size : (i + 1) * size] = face


def total(xs, ys):
    return sum(jnp.sum(x * y, axis=1, keepdims=True) for x, y in zip(xs, ys))


def blocks_of(interface):
    width = 256 if interface % 256 == 0 else interface
    return [slice(i, i + width) for i in range(0, interface, width)]


def product(matrix_ref, result_ref, left, groups):
    for block in blocks_of(matrix_ref.shape[1]):
        both = mxu(left, matrix_ref[:, block])
        at = 0
        for first, rows, count in groups:
            value = both[first : first + rows]
            for i in range(1, count):
                value = value + both[first + i * rows : first + (i + 1) * rows]
            result_ref[at : at + rows, block] = value
            at += rows


def local_order(faces, hots, count):
    split = [jnp.concatenate(parts(x, count), axis=0) for x in faces]
    split[0] = mxu(split[0], hots[0]).astype(jnp.bfloat16)
    split[2] = mxu(split[2], hots[2]).astype(jnp.bfloat16)
    return jnp.concatenate(split, axis=1)


def turned_result(result_ref, hots):
    size = result_ref.shape[1] // 4
    own = faces_of(result_ref, size)
    own[0] = turn(own[0], hots[0])
    own[2] = turn(own[2], hots[2])
    return own


def weighted(faces):
    return [(0.5 * s) * x for s, x in zip(SIGNS, faces)]


def hots_of(hots_ref):
    size = hots_ref.shape[1]
    return [hots_ref[i * size : (i + 1) * size, :] for i in range(4)]


def signed(faces):
    return [s * x for s, x in zip(SIGNS, faces)]


def lane_is(shape, lane):
    return lax.broadcasted_iota(jnp.int32, shape, 1) == lane


def pick(values, lane):
    return jnp.sum(jnp.where(lane_is(values.shape, lane), values, 0.0), axis=1, keepdims=True)


def numbering(extra, slots, width):
    numbers = extra[slots : slots + 1, :LANES]
    nodes = lax.broadcasted_iota(jnp.int32, (width, LANES), 0).astype(jnp.float32)
    hot = jnp.where(nodes == numbers, 1.0, 0.0)
    return hot[:, : 3 * extra.shape[0]].astype(jnp.bfloat16)


def spread(extra, slots, width):
    return mxu(numbering(extra, slots, width), jnp.concatenate(parts(extra, 3), axis=0))


def partial_sums(left, coupling, extra, slots, scalars, coarse_size, width):
    out = reorder(mxu(left, coupling, LAST), numbering(extra, slots, width), LAST)
    rows = out.shape[0] // 2
    out = out[:rows] + out[rows:]
    for i, value in enumerate(scalars):
        out = out + jnp.where(lane_is(out.shape, coarse_size + i), value, 0.0)
    return out


def by_parts(x, matrix, dims):
    rows = x.shape[0]
    both = mxu(jnp.concatenate(parts(x, 3), axis=0), matrix, dims)
    both = both[:rows] + (both[rows : 2 * rows] + both[2 * rows :])
    width = both.shape[1] // 3
    return both[:, :width] + (both[:, width : 2 * width] + both[:, 2 * width :])


def coarse_solve(right, down_ref, up_ref):
    lowered = by_parts(right, down_ref[...], LAST)
    return by_parts(lowered, up_ref[...], PLAIN), jnp.sum(lowered * lowered, axis=1, keepdims=True)


def coarse_part(sums, coarse_size):
    lanes = lax.broadcasted_iota(jnp.int32, sums.shape, 1)
    return jnp.where(lanes < coarse_size, sums, 0.0)


def two_high(x):
    return jnp.concatenate(parts(x, 2), axis=0)


def two_wide(x):
    high, low = parts(x, 2)
    return jnp.concatenate(
        [jnp.concatenate([high, high], axis=1), jnp.concatenate([low, low], axis=1)], axis=0
    )


def coarse_times(coarse, *image_refs):
    rows = coarse.shape[0]
    left = two_wide(coarse)
    both = [mxu(left, image[...]) for image in image_refs]
    return jnp.concatenate([x[:rows] + x[rows:] for x in both], axis=1)


def prepare_kernel(loads_ref, match_ref, schur_ref,
                   loads_out, hots_out, schur_out, match_held, sems):
    copies = [
        pltpu.make_async_copy(x, y, sems.at[i])
        for i, (x, y) in enumerate(
            ((match_ref, match_held), (loads_ref, loads_out), (schur_ref, schur_out))
        )
    ]
    for copy in copies:
        copy.start()
    size = loads_ref.shape[1] // 4
    copies[0].wait()
    for i in range(4):
        hots_out[i * size : (i + 1) * size, :] = one_hot(match_held, i)
    copies[1].wait()
    for i in (0, 2):
        block = slice(i * size, (i + 1) * size)
        loads_out[:, block] = turn(loads_out[:, block], hots_out[block, :])
    copies[2].wait()


def extra_kernel(coupling_ref, corners_ref, inverse_ref, hots_ref,
                 extra_out, spread_out, coupling_out, down_out, up_out):
    size = hots_ref.shape[1]
    slots = coupling_ref.shape[0]
    rows = extra_out.shape[0]
    hots = hots_of(hots_ref)
    extra_out[...] = jnp.full(extra_out.shape, -1.0, jnp.float32)
    corners = corners_ref[...].astype(jnp.float32)
    for i in range(4):
        extra_out[:slots, i * size : (i + 1) * size] = coupling_ref[:, i * size : (i + 1) * size]
        for k in range(3):
            at = i * size + k * rows
            extra_out[slots : slots + 1, at : at + slots] = corners
    coupling_out[...] = jnp.concatenate(parts(extra_out[...], 3), axis=0)
    for i in (0, 2):
        block = slice(i * size, (i + 1) * size)
        extra_out[:slots, block] = turn(coupling_ref[:, block], hots[i])
    spread_out[...] = spread(extra_out[...], slots, spread_out.shape[0])
    inverse = parts(inverse_ref[...], 3)
    down_out[...] = jnp.concatenate(inverse, axis=0)
    up_out[...] = jnp.concatenate(inverse, axis=1)


def first_kernel(near0, near1, near2, near3, loads_ref, hots_ref, schur_ref,
                 residual_ref, send0, send1, send2, send3, result_ref):
    cases = loads_ref.shape[0]
    size = loads_ref.shape[1] // 4
    hots = hots_of(hots_ref)
    near = faces_in([x[...] for x in (near0, near1, near2, near3)])
    for i in (1, 3):
        near[i] = reorder(near[i], hots[i], PLAIN)
    residual = jump(near, faces_of(loads_ref, size))
    store(residual_ref, residual)
    product(schur_ref, result_ref, local_order(weighted(residual), hots, 1), [(0, cases, 1)])
    for ref, value in zip(
        (send0, send1, send2, send3), swapped(turned_result(result_ref, hots), odds())
    ):
        ref[...] = value


def coarse_kernel(cases, spread_ref, far_ref, near_ref, core_ref, image_ref, rest_ref):
    width, interface = spread_ref.shape
    size = interface // 4
    slots = near_ref.shape[0] - cases - 4
    own = faces_of(spread_ref, size)
    far, near, core = [
        spread(x[cases:, :size], slots, width) for x in (far_ref, near_ref, core_ref)
    ]
    zero = jnp.zeros_like(core)
    image = jump(faces_in([far, zero, near, core]), own)
    store_some(image_ref, [two_high(x) for x in image[:2]])
    store_some(rest_ref, image[2:])


def coarse_rest_kernel(cases, rest_ref, high_ref, image_ref):
    size = rest_ref.shape[1] // 2
    width = rest_ref.shape[0]
    slots = high_ref.shape[0] - cases - 4
    share = spread(high_ref[cases:, :size], slots, width)
    zero = jnp.zeros_like(share)
    low, high = faces_in([zero, share, zero, zero])[2:]
    store_some(image_ref, [two_high(rest_ref[:, :size] + low), two_high(rest_ref[:, size:] - high)])


def direction_kernel(coarse_size, count, *refs):
    own = refs[0:4]
    near = refs[4:8]
    extra_ref, coupling_ref, residual_ref, hots_ref, flex_ref = refs[8:13]
    n = 13
    if count > 1:
        before_ref = refs[13]
        before_free = refs[14:18]
        n = 18
    precond_ref, free0, free1, free2, free3, result_ref = refs[n:]
    size = own[0].shape[1]
    cases = residual_ref.shape[0]
    slots = extra_ref.shape[0] - 4
    hots = hots_of(hots_ref)
    precond = jump(faces_in([x[...] for x in near]), faces_in([x[...] for x in own]))
    precond = [0.5 * x for x in precond]
    store(precond_ref, precond)
    forces = signed(precond)
    left = local_order(forces, hots, 2)
    product(flex_ref, result_ref, left[: count * cases], [(0, cases, count)])
    free = turned_result(result_ref, hots)
    extra = faces_of(extra_ref, size)
    for ref, value, rows in zip(
        (free0, free1, free2, free3), swapped(free, odds()), swapped(extra, odds())
    ):
        ref[:cases, :size] = value
        if count == 1:
            ref[cases:, :size] = rows
    scalars = [0.5 * total(faces_of(residual_ref, size), precond), total(forces, free)]
    if count > 1:
        before = signed(faces_of(before_ref, size))
        scalars.append(total(forces, faces_in([x[:cases, :size] for x in before_free])) + total(before, free))
    width = free3.shape[1] - size
    free3[:cases, size:] = partial_sums(
        left, coupling_ref[...], extra[0], slots, scalars, coarse_size, width
    )
    if count == 1:
        free3[cases:, size:] = jnp.zeros((free3.shape[0] - cases, width), jnp.float32)


def step_kernel(coarse_size, sums_ref, down_ref, up_ref, image_ref, rest_ref, own0, own1, own2, own3,
                near0, near1, near2, near3, residual_ref, hots_ref, schur_ref,
                new_ref, jump_ref, step_ref, send0, send1, send2, send3, result_ref):
    size = own0.shape[1]
    cases = sums_ref.shape[0]
    hots = hots_of(hots_ref)
    moved = jump(
        faces_in([x[:cases, :size] for x in (near0, near1, near2, near3)]),
        faces_in([x[:cases, :size] for x in (own0, own1, own2, own3)]),
    )
    store(jump_ref, moved)
    sums = sums_ref[...]
    coarse, energy = coarse_solve(coarse_part(sums, coarse_size), down_ref, up_ref)
    step = pick(sums, coarse_size) / (pick(sums, coarse_size + 1) + energy)
    step_ref[...] = jnp.broadcast_to(step, step_ref.shape)
    image = coarse_times(coarse, image_ref, rest_ref)
    residual = [
        residual_ref[:, i * size : (i + 1) * size]
        - step * (moved[i] + image[:, i * size : (i + 1) * size])
        for i in range(4)
    ]
    store(new_ref, residual)
    product(schur_ref, result_ref, local_order(weighted(residual), hots, 1), [(0, cases, 1)])
    for ref, value in zip(
        (send0, send1, send2, send3), swapped(turned_result(result_ref, hots), odds())
    ):
        ref[...] = value


def home_kernel(residual_ref, before_ref, precond_ref, jump_ref, image_ref, rest_ref, hots_ref,
                residual_out, before_out, precond_out, jump_out, image_out):
    size = hots_ref.shape[1]
    hots = hots_of(hots_ref)
    fields = [faces_of(x, size) for x in (residual_ref, before_ref, precond_ref, jump_ref)]
    image = [
        ref[:, block] for ref in (image_ref, rest_ref) for block in (slice(size), slice(size, None))
    ]
    for i in (0, 2):
        image[i] = mxu(image[i], hots[i]).astype(jnp.bfloat16)
        for field in fields:
            field[i] = turn_back(field[i], hots[i])
    store(image_out, image)
    for ref, field in zip((residual_out, before_out, precond_out, jump_out), fields):
        store(ref, field)


def interleave(faces, held_ref, out_ref):
    cases, size = faces[0].shape
    for at in range(0, size, LANES):
        held = held_ref.at[at // LANES]
        for i in range(4):
            held[pl.ds(i, cases, stride=4), :] = faces[i][:, at : at + LANES]
        out_ref[:, :, at : at + LANES] = held[...].reshape(cases, 4, LANES)


def last_kernel(coarse_size, first_ref, sums_ref, down_ref, up_ref, step_ref, residual_ref, before_ref,
                precond_ref, jump_ref, image_ref, hots_ref, own0, own1, own2, own3,
                near0, near1, near2, near3, multipliers_ref, out_ref, held_ref):
    size = hots_ref.shape[1]
    hots = hots_of(hots_ref)
    following = jump(
        faces_in([x[:, :size] for x in (near0, near1, near2, near3)]),
        faces_in([x[:, :size] for x in (own0, own1, own2, own3)]),
    )
    for i in (0, 2):
        following[i] = turn_back(following[i], hots[i])
    first = first_ref[...]
    sums = sums_ref[...]
    beta = pick(sums, coarse_size) / pick(first, coarse_size)
    right = coarse_part(sums, coarse_size) + beta * coarse_part(first, coarse_size)
    coarse, energy = coarse_solve(right, down_ref, up_ref)
    local = pick(sums, coarse_size + 1) + beta * (
        pick(sums, coarse_size + 2) + beta * pick(first, coarse_size + 1)
    )
    step = pick(sums, coarse_size) / (local + energy)
    step_before = step_ref[:, 0:1]
    image = coarse_times(coarse, image_ref)
    residual, multipliers = [], []
    for i in range(4):
        block = slice(i * size, (i + 1) * size)
        moved = following[i] + beta * jump_ref[:, block] + image[:, block]
        residual.append(residual_ref[:, block] - step * moved)
        before = before_ref[:, block]
        direction = precond_ref[:, block] + beta * before
        multipliers.append(step_before * before + step * direction)
    interleave(residual, held_ref.at[0], out_ref)
    interleave(multipliers, held_ref.at[1], multipliers_ref)


VMEM = pl.BlockSpec(memory_space=pltpu.VMEM)
OUTSIDE = pl.BlockSpec(memory_space=pltpu.HBM)


def call(kernel, args, outs, scratch=(), outside=(), flops=0):
    specs = [OUTSIDE if i in outside else VMEM for i in range(len(args))]
    shapes = [(x, jnp.float32) if isinstance(x[0], int) else x for x in outs]
    return pl.pallas_call(
        kernel,
        in_specs=specs,
        out_specs=[VMEM] * len(outs),
        out_shape=[jax.ShapeDtypeStruct(*x) for x in shapes],
        scratch_shapes=list(scratch),
        compiler_params=pltpu.CompilerParams(vmem_limit_bytes=28 * 2**20),
        cost_estimate=pl.CostEstimate(flops=flops, bytes_accessed=2**22, transcendentals=0),
    )(*args)


def shards(
    applied_loads,
    flex_matrix,
    schur_matrix,
    corner_coupling,
    coarse_inverse,
    face_match,
    corner_map,
):
    loads = applied_loads[0, 0]
    flex = flex_matrix[0, 0]
    schur = schur_matrix[0, 0]
    match = face_match[0, 0]
    cases, interface = loads.shape
    size = interface // 4
    slots = corner_coupling.shape[2]
    coarse_size = coarse_inverse.shape[0]
    width = -(-(coarse_size + 3) // LANES) * LANES
    work = 2 * cases * interface * interface

    inverse = jnp.pad(coarse_inverse, ((0, width - coarse_size), (0, width - coarse_size)))
    field = (cases, interface)
    face = (cases, size)
    result = pltpu.VMEM(field, jnp.float32)
    both_parts = ((2 * width, interface), jnp.bfloat16)

    held = [pltpu.with_memory_space_constraint(x, pltpu.HBM) for x in (loads, match, schur)]
    cut = [loads[:, i * size : (i + 1) * size] for i in range(4)]
    far, _, close, _ = swapped(cut, (odd("sub"), odd("grp")))
    far, close, later = lax.optimization_barrier((far, close, loads))
    cut = [later[:, i * size : (i + 1) * size] for i in range(4)]
    _, high, _, core = swapped(cut, (odd("sub"), odd("grp")))
    near = exchange([far, high, close, core])
    loads, hots, schur = call(
        prepare_kernel,
        held,
        [field, ((4 * size, size), jnp.bfloat16), (schur.shape, jnp.bfloat16)],
        [pltpu.VMEM(match.shape, jnp.int32), pltpu.SemaphoreType.DMA((3,))],
        outside=(0, 1, 2),
        flops=work,
    )
    residual, *own_first = call(
        first_kernel, [*near, loads, hots, schur], [field] + [face] * 4, [result], flops=work
    )
    near = exchange(own_first)
    residual, coupling, corners = lax.optimization_barrier(
        (residual, corner_coupling[0, 0], corner_map[0])
    )
    extra, own_spread, coupling, down, up = call(
        extra_kernel,
        [coupling, corners, inverse, hots],
        [
            (slots + 4, interface),
            (width, interface),
            ((3 * (slots + 4), interface), jnp.bfloat16),
            ((3 * width, width), jnp.bfloat16),
            ((width, 3 * width), jnp.bfloat16),
        ],
        flops=work // 4,
    )
    before, *own_free = call(
        functools.partial(direction_kernel, coarse_size, 1),
        [*own_first, *near, extra, coupling, residual, hots, flex],
        [field] + [(cases + slots + 4, size)] * 3 + [(cases + slots + 4, size + width)],
        [result],
        flops=work,
    )
    first_sums, near = sum_and_exchange(own_free, cases)
    half = ((2 * width, interface // 2), jnp.bfloat16)
    image, rest = call(
        functools.partial(coarse_kernel, cases),
        [own_spread, near[0], near[2], near[3]],
        [half, (width, interface // 2)],
        flops=work // 4,
    )
    (rest,) = call(
        functools.partial(coarse_rest_kernel, cases), [rest, near[1]], [half], flops=work // 8
    )
    residual, moved, step, *own = call(
        functools.partial(step_kernel, coarse_size),
        [first_sums, down, up, image, rest, *own_free, *near, residual, hots, schur],
        [field, field, (cases, LANES)] + [face] * 4,
        [result],
        flops=work,
    )
    near = exchange(own)
    precond, *own = call(
        functools.partial(direction_kernel, coarse_size, 2),
        [*own, *near, extra, coupling, residual, hots, flex, before, *own_free],
        [field] + [face] * 3 + [(cases, size + width)],
        [result],
        flops=work,
    )
    fields = call(
        home_kernel,
        [residual, before, precond, moved, image, rest, hots],
        [field] * 4 + [both_parts],
        flops=work // 2,
    )
    sums, near = sum_and_exchange(own, cases)
    layout = (cases, 4, size)
    multipliers, residual = call(
        functools.partial(last_kernel, coarse_size),
        [first_sums, sums, down, up, step, *fields, hots, *own, *near],
        [layout, layout],
        [pltpu.VMEM((2, size // LANES, 4 * cases, LANES), jnp.float32)],
        flops=work // 4,
    )
    return multipliers[None, None], residual[None, None]


def solution(mesh):
    return jax.shard_map(
        shards,
        mesh=mesh,
        in_specs=(
            P("sub", "grp", None, None),
            P("sub", "grp", None, None),
            P("sub", "grp", None, None),
            P("sub", "grp", None, None),
            P(),
            P("sub", "grp", None, None),
            P("sub", "grp", None),
        ),
        out_specs=(P("sub", "grp", None, None, None), P("sub", "grp", None, None, None)),
        check_vma=False,
    )
```

```python
import functools

import jax
import jax.numpy as jnp
from jax import lax
from jax.experimental import pallas as pl
from jax.experimental.pallas import tpu as pltpu
from jax.sharding import PartitionSpec as P

HIGHEST = lax.Precision.HIGHEST
PLAIN = (((1,), (0,)), ((), ()))
LAST = (((1,), (1,)), ((), ()))
LANES = 128
SIGNS = (-1.0, 1.0, -1.0, 1.0)


def odd(axis):
    return lax.axis_index(axis) % 2 == 1


def swapped(faces, odds):
    far, near = [], []
    for (low, high), is_odd in zip((faces[0:2], faces[2:4]), odds):
        far.append(jnp.where(is_odd, high, low))
        near.append(jnp.where(is_odd, low, high))
    return far + near


def swap(face, i):
    axis = ("sub", "grp", "sub", "grp")[i]
    peers = lax.axis_size(axis)
    if i < 2:
        pairs = [(j, (j + 2 * (j % 2) - 1) % peers) for j in range(peers)]
    else:
        pairs = [(j, j ^ 1) for j in range(peers)]
    return lax.ppermute(face, axis, pairs)


def exchange(faces):
    return lax.optimization_barrier([swap(face, i) for i, face in enumerate(faces)])


def sum_over(values, axis, step, before=(), after=()):
    peers = lax.axis_size(axis)
    first = True
    while step < peers:
        count = 4 if 4 * step <= peers else 2
        others = [
            lax.ppermute(values, axis, [(i, i ^ (k * step)) for i in range(peers)])
            for k in range(1, count)
        ]
        if first:
            before, others, after = lax.optimization_barrier((before, others, after))
            first = False
        values = values + others[0]
        if count == 4:
            values = values + (others[1] + others[2])
        step *= count
    return values, before, after


def sum_and_exchange(faces, cases, later=()):
    far, high, near, core = faces
    size = near.shape[1]
    other = swap(core, 3)
    values = core[:cases, size:] + other[:cases, size:]
    near, values = lax.optimization_barrier((near, values))
    values, far, near = sum_over(values, "grp", 2, [swap(far, 0)], [swap(near, 2)])
    far, near, high, values, later = lax.optimization_barrier((far, near, high, values, later))
    values, high, _ = sum_over(values, "sub", 1, [swap(high, 1)])
    return values, [*far, *high, *near, other], later


def one_hot(match_ref, i):
    row = match_ref[i : i + 1, :]
    size = row.shape[1]
    nodes = lax.broadcasted_iota(jnp.int32, (size, size), 0)
    return jnp.where(nodes == row, 1.0, 0.0).astype(jnp.bfloat16)


def parts(x, count):
    out = []
    for _ in range(count):
        part = x.astype(jnp.bfloat16)
        out.append(part)
        x = x - part.astype(jnp.float32)
    return out


def mxu(x, y, dims=PLAIN):
    return lax.dot_general(x, y, dims, preferred_element_type=jnp.float32)


def exact(x, y, dims=PLAIN):
    return lax.dot_general(x, y, dims, precision=HIGHEST, preferred_element_type=jnp.float32)


def reorder(x, hot, dims):
    rows = x.shape[0]
    both = mxu(jnp.concatenate(parts(x, 3), axis=0), hot, dims)
    return both[:rows] + both[rows : 2 * rows] + both[2 * rows :]


def turn(x, hot):
    return reorder(x, hot, LAST)


def turn_back(x, hot):
    return reorder(x, hot, PLAIN)


def jump(received, own):
    return [
        received[0] - own[0],
        own[1] - received[1],
        received[2] - own[2],
        own[3] - received[3],
    ]


def odds():
    return odd("sub"), odd("grp")


def faces_in(values):
    out = []
    for far, near, is_odd in zip(values[0:2], values[2:4], odds()):
        out += [jnp.where(is_odd, near, far), jnp.where(is_odd, far, near)]
    return out


def faces_of(ref, size):
    return [ref[:, i * size : (i + 1) * size] for i in range(4)]


def store(ref, faces):
    size = faces[0].shape[1]
    for i in range(4):
        ref[:, i * size : (i + 1) * size] = faces[i]


def store_some(ref, faces):
    size = faces[0].shape[1]
    for i, face in enumerate(faces):
        ref[:, i * size : (i + 1) * size] = face


def total(xs, ys):
    return sum(jnp.sum(x * y, axis=1, keepdims=True) for x, y in zip(xs, ys))


def blocks_of(interface):
    width = 256 if interface % 256 == 0 else interface
    return [slice(i, i + width) for i in range(0, interface, width)]


def product(matrix_ref, result_ref, left, groups):
    for block in blocks_of(matrix_ref.shape[1]):
        both = mxu(left, matrix_ref[:, block])
        at = 0
        for first, rows, count in groups:
            value = both[first : first + rows]
            for i in range(1, count):
                value = value + both[first + i * rows : first + (i + 1) * rows]
            result_ref[at : at + rows, block] = value
            at += rows


def local_order(faces, hots, count):
    split = [jnp.concatenate(parts(x, count), axis=0) for x in faces]
    split[0] = mxu(split[0], hots[0]).astype(jnp.bfloat16)
    split[2] = mxu(split[2], hots[2]).astype(jnp.bfloat16)
    return jnp.concatenate(split, axis=1)


def face_parts(faces, count):
    return jnp.concatenate(
        [jnp.concatenate(parts(x, count), axis=0) for x in faces], axis=1
    )


def turned_result(result_ref, hots):
    size = result_ref.shape[1] // 4
    own = faces_of(result_ref, size)
    own[0] = turn(own[0], hots[0])
    own[2] = turn(own[2], hots[2])
    return own


def weighted(faces):
    return [(0.5 * s) * x for s, x in zip(SIGNS, faces)]


def hots_of(hots_ref):
    size = hots_ref.shape[1]
    return [hots_ref[i * size : (i + 1) * size, :] for i in range(4)]


def signed(faces):
    return [s * x for s, x in zip(SIGNS, faces)]


def lane_is(shape, lane):
    return lax.broadcasted_iota(jnp.int32, shape, 1) == lane


def pick(values, lane):
    return jnp.sum(jnp.where(lane_is(values.shape, lane), values, 0.0), axis=1, keepdims=True)


def numbering(extra, slots, width):
    numbers = extra[slots : slots + 1, :LANES]
    nodes = lax.broadcasted_iota(jnp.int32, (width, LANES), 0).astype(jnp.float32)
    hot = jnp.where(nodes == numbers, 1.0, 0.0)
    return hot[:, : 3 * extra.shape[0]].astype(jnp.bfloat16)


def spread(extra, slots, width):
    return mxu(numbering(extra, slots, width), jnp.concatenate(parts(extra, 3), axis=0))


def partial_sums(left, coupling, extra, slots, scalars, coarse_size, width):
    out = reorder(mxu(left, coupling, LAST), numbering(extra, slots, width), LAST)
    rows = out.shape[0] // 2
    out = out[:rows] + out[rows:]
    for i, value in enumerate(scalars):
        out = out + jnp.where(lane_is(out.shape, coarse_size + i), value, 0.0)
    return out


def by_parts(x, matrix, dims):
    rows = x.shape[0]
    both = mxu(jnp.concatenate(parts(x, 3), axis=0), matrix, dims)
    both = both[:rows] + (both[rows : 2 * rows] + both[2 * rows :])
    width = both.shape[1] // 3
    return both[:, :width] + (both[:, width : 2 * width] + both[:, 2 * width :])


def coarse_solve(right, down_ref, up_ref):
    lowered = by_parts(right, down_ref[...], LAST)
    return by_parts(lowered, up_ref[...], PLAIN), jnp.sum(lowered * lowered, axis=1, keepdims=True)


def coarse_part(sums, coarse_size):
    lanes = lax.broadcasted_iota(jnp.int32, sums.shape, 1)
    return jnp.where(lanes < coarse_size, sums, 0.0)


def two_high(x):
    return jnp.concatenate(parts(x, 2), axis=0)


def two_wide(x):
    high, low = parts(x, 2)
    return jnp.concatenate(
        [jnp.concatenate([high, high], axis=1), jnp.concatenate([low, low], axis=1)], axis=0
    )


def coarse_times(coarse, *image_refs):
    rows = coarse.shape[0]
    left = two_wide(coarse)
    both = [mxu(left, image[...]) for image in image_refs]
    return jnp.concatenate([x[:rows] + x[rows:] for x in both], axis=1)


def prepare_kernel(loads_ref, match_ref, schur_ref,
                   loads_out, hots_out, schur_out, match_held, sems):
    copies = [
        pltpu.make_async_copy(x, y, sems.at[i])
        for i, (x, y) in enumerate(
            ((match_ref, match_held), (loads_ref, loads_out), (schur_ref, schur_out))
        )
    ]
    for copy in copies:
        copy.start()
    size = loads_ref.shape[1] // 4
    copies[0].wait()
    for i in range(4):
        hots_out[i * size : (i + 1) * size, :] = one_hot(match_held, i)
    copies[1].wait()
    for i in (0, 2):
        block = slice(i * size, (i + 1) * size)
        loads_out[:, block] = turn(loads_out[:, block], hots_out[block, :])
    copies[2].wait()


def extra_kernel(coupling_ref, corners_ref, inverse_ref, hots_ref,
                 extra_out, spread_out, coupling_out, down_out, up_out):
    size = hots_ref.shape[1]
    slots = coupling_ref.shape[0]
    rows = extra_out.shape[0]
    hots = hots_of(hots_ref)
    extra_out[...] = jnp.full(extra_out.shape, -1.0, jnp.float32)
    corners = corners_ref[...].astype(jnp.float32)
    for i in range(4):
        extra_out[:slots, i * size : (i + 1) * size] = coupling_ref[:, i * size : (i + 1) * size]
        for k in range(3):
            at = i * size + k * rows
            extra_out[slots : slots + 1, at : at + slots] = corners
    for i in (0, 2):
        block = slice(i * size, (i + 1) * size)
        extra_out[:slots, block] = turn(coupling_ref[:, block], hots[i])
    coupling_out[...] = jnp.concatenate(parts(extra_out[...], 3), axis=0)
    spread_out[...] = spread(extra_out[...], slots, spread_out.shape[0])
    inverse = parts(inverse_ref[...], 3)
    down_out[...] = jnp.concatenate(inverse, axis=0)
    up_out[...] = jnp.concatenate(inverse, axis=1)


def turn_matrix_kernel(matrix_ref, hots_ref, out_ref):
    size = hots_ref.shape[1]
    hots = hots_of(hots_ref)
    for i in range(4):
        rows = slice(i * size, (i + 1) * size)
        block = faces_of(matrix_ref.at[rows, :], size)
        for j in (0, 2):
            block[j] = mxu(block[j], hots[j], LAST).astype(jnp.bfloat16)
        for j in range(4):
            if i in (0, 2):
                block[j] = mxu(hots[i], block[j]).astype(jnp.bfloat16)
            out_ref[rows, j * size : (j + 1) * size] = block[j]


def first_kernel(near0, near1, near2, near3, loads_ref, hots_ref, schur_ref,
                 residual_ref, send0, send1, send2, send3, result_ref):
    cases = loads_ref.shape[0]
    size = loads_ref.shape[1] // 4
    hots = hots_of(hots_ref)
    near = faces_in([x[...] for x in (near0, near1, near2, near3)])
    for i in (1, 3):
        near[i] = reorder(near[i], hots[i], PLAIN)
    residual = jump(near, faces_of(loads_ref, size))
    store(residual_ref, residual)
    product(schur_ref, result_ref, local_order(weighted(residual), hots, 1), [(0, cases, 1)])
    for ref, value in zip(
        (send0, send1, send2, send3), swapped(turned_result(result_ref, hots), odds())
    ):
        ref[...] = value


def coarse_kernel(cases, spread_ref, far_ref, near_ref, core_ref, image_ref, rest_ref):
    width, interface = spread_ref.shape
    size = interface // 4
    slots = near_ref.shape[0] - cases - 4
    own = faces_of(spread_ref, size)
    far, near, core = [
        spread(x[cases:, :size], slots, width) for x in (far_ref, near_ref, core_ref)
    ]
    zero = jnp.zeros_like(core)
    image = jump(faces_in([far, zero, near, core]), own)
    store_some(image_ref, [two_high(x) for x in image[:2]])
    store_some(rest_ref, image[2:])


def coarse_rest_kernel(cases, rest_ref, high_ref, image_ref):
    size = rest_ref.shape[1] // 2
    width = rest_ref.shape[0]
    slots = high_ref.shape[0] - cases - 4
    share = spread(high_ref[cases:, :size], slots, width)
    zero = jnp.zeros_like(share)
    low, high = faces_in([zero, share, zero, zero])[2:]
    store_some(image_ref, [two_high(rest_ref[:, :size] + low), two_high(rest_ref[:, size:] - high)])


def direction_kernel(coarse_size, count, *refs):
    own = refs[0:4]
    near = refs[4:8]
    extra_ref, coupling_ref, residual_ref, flex_ref = refs[8:12]
    n = 12
    if count > 1:
        before_ref = refs[12]
        before_free = refs[13:17]
        n = 17
    precond_ref, free0, free1, free2, free3, result_ref = refs[n:]
    size = own[0].shape[1]
    cases = residual_ref.shape[0]
    slots = extra_ref.shape[0] - 4
    precond = jump(faces_in([x[...] for x in near]), faces_in([x[...] for x in own]))
    precond = [0.5 * x for x in precond]
    store(precond_ref, precond)
    forces = signed(precond)
    left = face_parts(forces, 2)
    product(flex_ref, result_ref, left[: count * cases], [(0, cases, count)])
    free = faces_of(result_ref, size)
    extra = faces_of(extra_ref, size)
    for ref, value, rows in zip(
        (free0, free1, free2, free3), swapped(free, odds()), swapped(extra, odds())
    ):
        ref[:cases, :size] = value
        if count == 1:
            ref[cases:, :size] = rows
    scalars = [0.5 * total(faces_of(residual_ref, size), precond), total(forces, free)]
    if count > 1:
        before = signed(faces_of(before_ref, size))
        scalars.append(total(forces, faces_in([x[:cases, :size] for x in before_free])) + total(before, free))
    width = free3.shape[1] - size
    free3[:cases, size:] = partial_sums(
        left, coupling_ref[...], extra[0], slots, scalars, coarse_size, width
    )
    if count == 1:
        free3[cases:, size:] = jnp.zeros((free3.shape[0] - cases, width), jnp.float32)


def step_kernel(coarse_size, sums_ref, down_ref, up_ref, image_ref, rest_ref, own0, own1, own2, own3,
                near0, near1, near2, near3, residual_ref, schur_ref,
                new_ref, jump_ref, step_ref, send0, send1, send2, send3, result_ref):
    size = own0.shape[1]
    cases = sums_ref.shape[0]
    moved = jump(
        faces_in([x[:cases, :size] for x in (near0, near1, near2, near3)]),
        faces_in([x[:cases, :size] for x in (own0, own1, own2, own3)]),
    )
    store(jump_ref, moved)
    sums = sums_ref[...]
    coarse, energy = coarse_solve(coarse_part(sums, coarse_size), down_ref, up_ref)
    step = pick(sums, coarse_size) / (pick(sums, coarse_size + 1) + energy)
    step_ref[...] = jnp.broadcast_to(step, step_ref.shape)
    image = coarse_times(coarse, image_ref, rest_ref)
    residual = [
        residual_ref[:, i * size : (i + 1) * size]
        - step * (moved[i] + image[:, i * size : (i + 1) * size])
        for i in range(4)
    ]
    store(new_ref, residual)
    product(schur_ref, result_ref, face_parts(weighted(residual), 1), [(0, cases, 1)])
    for ref, value in zip(
        (send0, send1, send2, send3), swapped(faces_of(result_ref, size), odds())
    ):
        ref[...] = value


def home_kernel(residual_ref, before_ref, precond_ref, jump_ref, image_ref, rest_ref, hots_ref,
                residual_out, before_out, precond_out, jump_out, image_out):
    size = hots_ref.shape[1]
    hots = hots_of(hots_ref)
    fields = [faces_of(x, size) for x in (residual_ref, before_ref, precond_ref, jump_ref)]
    image = [
        ref[:, block] for ref in (image_ref, rest_ref) for block in (slice(size), slice(size, None))
    ]
    for i in (0, 2):
        image[i] = mxu(image[i], hots[i]).astype(jnp.bfloat16)
        for field in fields:
            field[i] = turn_back(field[i], hots[i])
    store(image_out, image)
    for ref, field in zip((residual_out, before_out, precond_out, jump_out), fields):
        store(ref, field)


def last_kernel(coarse_size, first_ref, sums_ref, down_ref, up_ref, step_ref, residual_ref, before_ref,
                precond_ref, jump_ref, image_ref, hots_ref, own0, own1, own2, own3,
                near0, near1, near2, near3, multipliers_ref, out_ref):
    size = hots_ref.shape[1]
    hots = hots_of(hots_ref)
    following = jump(
        faces_in([x[:, :size] for x in (near0, near1, near2, near3)]),
        faces_in([x[:, :size] for x in (own0, own1, own2, own3)]),
    )
    for i in (0, 2):
        following[i] = turn_back(following[i], hots[i])
    first = first_ref[...]
    sums = sums_ref[...]
    beta = pick(sums, coarse_size) / pick(first, coarse_size)
    right = coarse_part(sums, coarse_size) + beta * coarse_part(first, coarse_size)
    coarse, energy = coarse_solve(right, down_ref, up_ref)
    local = pick(sums, coarse_size + 1) + beta * (
        pick(sums, coarse_size + 2) + beta * pick(first, coarse_size + 1)
    )
    step = pick(sums, coarse_size) / (local + energy)
    step_before = step_ref[:, 0:1]
    image = coarse_times(coarse, image_ref)
    for i in range(4):
        block = slice(i * size, (i + 1) * size)
        moved = following[i] + beta * jump_ref[:, block] + image[:, block]
        out_ref[:, i, :] = residual_ref[:, block] - step * moved
        before = before_ref[:, block]
        direction = precond_ref[:, block] + beta * before
        multipliers_ref[:, i, :] = step_before * before + step * direction


VMEM = pl.BlockSpec(memory_space=pltpu.VMEM)
OUTSIDE = pl.BlockSpec(memory_space=pltpu.HBM)


def call(kernel, args, outs, scratch=(), outside=(), flops=0):
    specs = [OUTSIDE if i in outside else VMEM for i in range(len(args))]
    shapes = [(x, jnp.float32) if isinstance(x[0], int) else x for x in outs]
    return pl.pallas_call(
        kernel,
        in_specs=specs,
        out_specs=[VMEM] * len(outs),
        out_shape=[jax.ShapeDtypeStruct(*x) for x in shapes],
        scratch_shapes=list(scratch),
        compiler_params=pltpu.CompilerParams(vmem_limit_bytes=28 * 2**20),
        cost_estimate=pl.CostEstimate(flops=flops, bytes_accessed=2**22, transcendentals=0),
    )(*args)


def shards(
    applied_loads,
    flex_matrix,
    schur_matrix,
    corner_coupling,
    coarse_inverse,
    face_match,
    corner_map,
):
    loads = applied_loads[0, 0]
    flex = flex_matrix[0, 0]
    schur = schur_matrix[0, 0]
    match = face_match[0, 0]
    cases, interface = loads.shape
    size = interface // 4
    slots = corner_coupling.shape[2]
    coarse_size = coarse_inverse.shape[0]
    width = -(-(coarse_size + 3) // LANES) * LANES
    work = 2 * cases * interface * interface

    inverse = jnp.pad(coarse_inverse, ((0, width - coarse_size), (0, width - coarse_size)))
    field = (cases, interface)
    face = (cases, size)
    result = pltpu.VMEM(field, jnp.float32)
    both_parts = ((2 * width, interface), jnp.bfloat16)

    held = [pltpu.with_memory_space_constraint(x, pltpu.HBM) for x in (loads, match, schur)]
    near = exchange(
        swapped([loads[:, i * size : (i + 1) * size] for i in range(4)], (odd("sub"), odd("grp")))
    )
    loads, hots, schur = call(
        prepare_kernel,
        held,
        [field, ((4 * size, size), jnp.bfloat16), (schur.shape, jnp.bfloat16)],
        [pltpu.VMEM(match.shape, jnp.int32), pltpu.SemaphoreType.DMA((3,))],
        outside=(0, 1, 2),
        flops=work,
    )
    residual, *own_first = call(
        first_kernel, [*near, loads, hots, schur], [field] + [face] * 4, [result], flops=work
    )
    near = exchange(own_first)
    residual, coupling, corners, flex = lax.optimization_barrier(
        (residual, corner_coupling[0, 0], corner_map[0], flex)
    )
    (flex,) = call(
        turn_matrix_kernel, [flex, hots], [(flex.shape, jnp.bfloat16)], flops=2 * work
    )
    extra, own_spread, coupling, down, up = call(
        extra_kernel,
        [coupling, corners, inverse, hots],
        [
            (slots + 4, interface),
            (width, interface),
            ((3 * (slots + 4), interface), jnp.bfloat16),
            ((3 * width, width), jnp.bfloat16),
            ((width, 3 * width), jnp.bfloat16),
        ],
        flops=work // 4,
    )
    before, *own_free = call(
        functools.partial(direction_kernel, coarse_size, 1),
        [*own_first, *near, extra, coupling, residual, flex],
        [field] + [(cases + slots + 4, size)] * 3 + [(cases + slots + 4, size + width)],
        [result],
        flops=work,
    )
    first_sums, near, schur = sum_and_exchange(own_free, cases, schur)
    (schur,) = call(
        turn_matrix_kernel, [schur, hots], [(schur.shape, jnp.bfloat16)], flops=2 * work
    )
    half = ((2 * width, interface // 2), jnp.bfloat16)
    image, rest = call(
        functools.partial(coarse_kernel, cases),
        [own_spread, near[0], near[2], near[3]],
        [half, (width, interface // 2)],
        flops=work // 4,
    )
    (rest,) = call(
        functools.partial(coarse_rest_kernel, cases), [rest, near[1]], [half], flops=work // 8
    )
    residual, moved, step, *own = call(
        functools.partial(step_kernel, coarse_size),
        [first_sums, down, up, image, rest, *own_free, *near, residual, schur],
        [field, field, (cases, LANES)] + [face] * 4,
        [result],
        flops=work,
    )
    near = exchange(own)
    precond, *own = call(
        functools.partial(direction_kernel, coarse_size, 2),
        [*own, *near, extra, coupling, residual, flex, before, *own_free],
        [field] + [face] * 3 + [(cases, size + width)],
        [result],
        flops=work,
    )
    fields = call(
        home_kernel,
        [residual, before, precond, moved, image, rest, hots],
        [field] * 4 + [both_parts],
        flops=work // 2,
    )
    sums, near, _ = sum_and_exchange(own, cases)
    layout = (cases, 4, size)
    multipliers, residual = call(
        functools.partial(last_kernel, coarse_size),
        [first_sums, sums, down, up, step, *fields, hots, *own, *near],
        [layout, layout],
        flops=work // 4,
    )
    return multipliers[None, None], residual[None, None]


def solution(mesh):
    return jax.shard_map(
        shards,
        mesh=mesh,
        in_specs=(
            P("sub", "grp", None, None),
            P("sub", "grp", None, None),
            P("sub", "grp", None, None),
            P("sub", "grp", None, None),
            P(),
            P("sub", "grp", None, None),
            P("sub", "grp", None),
        ),
        out_specs=(P("sub", "grp", None, None, None), P("sub", "grp", None, None, None)),
        check_vma=False,
    )
```

```python
import functools

import jax
import jax.numpy as jnp
from jax import lax
from jax.experimental import pallas as pl
from jax.experimental.pallas import tpu as pltpu
from jax.sharding import PartitionSpec as P

HIGHEST = lax.Precision.HIGHEST
PLAIN = (((1,), (0,)), ((), ()))
LAST = (((1,), (1,)), ((), ()))
LANES = 128
SIGNS = (-1.0, 1.0, -1.0, 1.0)


def odd(axis):
    return lax.axis_index(axis) % 2 == 1


def swapped(faces, odds):
    far, near = [], []
    for (low, high), is_odd in zip((faces[0:2], faces[2:4]), odds):
        far.append(jnp.where(is_odd, high, low))
        near.append(jnp.where(is_odd, low, high))
    return far + near


def swap(face, i):
    axis = ("sub", "grp", "sub", "grp")[i]
    peers = lax.axis_size(axis)
    if i < 2:
        pairs = [(j, (j + 2 * (j % 2) - 1) % peers) for j in range(peers)]
    else:
        pairs = [(j, j ^ 1) for j in range(peers)]
    return lax.ppermute(face, axis, pairs)


def exchange(faces):
    return lax.optimization_barrier([swap(face, i) for i, face in enumerate(faces)])


def sum_over(values, axis, step, before=(), after=()):
    peers = lax.axis_size(axis)
    first = True
    while step < peers:
        count = 4 if 4 * step <= peers else 2
        others = [
            lax.ppermute(values, axis, [(i, i ^ (k * step)) for i in range(peers)])
            for k in ((2, 1, 3) if count == 4 else (1,))
        ]
        if first:
            before, others, after = lax.optimization_barrier((before, others, after))
            first = False
        if count == 4:
            values = (values + others[1]) + (others[0] + others[2])
        else:
            values = values + others[0]
        step *= count
    return values, before, after


def sum_and_exchange(faces, cases):
    far, high, near, core = faces
    size = near.shape[1]
    other = swap(core, 3)
    values = core[:cases, size:] + other[:cases, size:]
    near, values = lax.optimization_barrier((near, values))
    values, far, near = sum_over(values, "grp", 2, [swap(far, 0)], [swap(near, 2)])
    far, near, high, values = lax.optimization_barrier((far, near, high, values))
    values, high, _ = sum_over(values, "sub", 1, [swap(high, 1)])
    return values, [*far, *high, *near, other]


def one_hot(match_ref, i):
    row = match_ref[i : i + 1, :]
    size = row.shape[1]
    nodes = lax.broadcasted_iota(jnp.int32, (size, size), 0)
    return jnp.where(nodes == row, 1.0, 0.0).astype(jnp.bfloat16)


def parts(x, count):
    out = []
    for _ in range(count):
        part = x.astype(jnp.bfloat16)
        out.append(part)
        x = x - part.astype(jnp.float32)
    return out


def mxu(x, y, dims=PLAIN):
    return lax.dot_general(x, y, dims, preferred_element_type=jnp.float32)


def exact(x, y, dims=PLAIN):
    return lax.dot_general(x, y, dims, precision=HIGHEST, preferred_element_type=jnp.float32)


def reorder(x, hot, dims):
    rows = x.shape[0]
    both = mxu(jnp.concatenate(parts(x, 3), axis=0), hot, dims)
    return both[:rows] + both[rows : 2 * rows] + both[2 * rows :]


def turn(x, hot):
    return reorder(x, hot, LAST)


def turn_back(x, hot):
    return reorder(x, hot, PLAIN)


def jump(received, own):
    return [
        received[0] - own[0],
        own[1] - received[1],
        received[2] - own[2],
        own[3] - received[3],
    ]


def odds():
    return odd("sub"), odd("grp")


def faces_in(values):
    out = []
    for far, near, is_odd in zip(values[0:2], values[2:4], odds()):
        out += [jnp.where(is_odd, near, far), jnp.where(is_odd, far, near)]
    return out


def faces_of(ref, size):
    return [ref[:, i * size : (i + 1) * size] for i in range(4)]


def store(ref, faces):
    size = faces[0].shape[1]
    for i in range(4):
        ref[:, i * size : (i + 1) * size] = faces[i]


def store_some(ref, faces):
    size = faces[0].shape[1]
    for i, face in enumerate(faces):
        ref[:, i * size : (i + 1) * size] = face


def total(xs, ys):
    return sum(jnp.sum(x * y, axis=1, keepdims=True) for x, y in zip(xs, ys))


def blocks_of(interface):
    width = 256 if interface % 256 == 0 else interface
    return [slice(i, i + width) for i in range(0, interface, width)]


def product(matrix_ref, result_ref, left, groups):
    for block in blocks_of(matrix_ref.shape[1]):
        both = mxu(left, matrix_ref[:, block])
        at = 0
        for first, rows, count in groups:
            value = both[first : first + rows]
            for i in range(1, count):
                value = value + both[first + i * rows : first + (i + 1) * rows]
            result_ref[at : at + rows, block] = value
            at += rows


def local_order(faces, hots, count):
    split = [jnp.concatenate(parts(x, count), axis=0) for x in faces]
    split[0] = mxu(split[0], hots[0]).astype(jnp.bfloat16)
    split[2] = mxu(split[2], hots[2]).astype(jnp.bfloat16)
    return jnp.concatenate(split, axis=1)


def face_parts(faces, count):
    return jnp.concatenate(
        [jnp.concatenate(parts(x, count), axis=0) for x in faces], axis=1
    )


def turned_result(result_ref, hots):
    size = result_ref.shape[1] // 4
    own = faces_of(result_ref, size)
    own[0] = turn(own[0], hots[0])
    own[2] = turn(own[2], hots[2])
    return own


def weighted(faces):
    return [(0.5 * s) * x for s, x in zip(SIGNS, faces)]


def hots_of(hots_ref):
    size = hots_ref.shape[1]
    return [hots_ref[i * size : (i + 1) * size, :] for i in range(4)]


def signed(faces):
    return [s * x for s, x in zip(SIGNS, faces)]


def lane_is(shape, lane):
    return lax.broadcasted_iota(jnp.int32, shape, 1) == lane


def pick(values, lane):
    return jnp.sum(jnp.where(lane_is(values.shape, lane), values, 0.0), axis=1, keepdims=True)


def numbering(extra, slots, width):
    numbers = extra[slots : slots + 1, :LANES]
    nodes = lax.broadcasted_iota(jnp.int32, (width, LANES), 0).astype(jnp.float32)
    hot = jnp.where(nodes == numbers, 1.0, 0.0)
    return hot[:, : 3 * extra.shape[0]].astype(jnp.bfloat16)


def spread(extra, slots, width):
    return mxu(numbering(extra, slots, width), jnp.concatenate(parts(extra, 3), axis=0))


def partial_sums(left, coupling, extra, slots, scalars, coarse_size, width):
    out = reorder(mxu(left, coupling, LAST), numbering(extra, slots, width), LAST)
    rows = out.shape[0] // 2
    out = out[:rows] + out[rows:]
    for i, value in enumerate(scalars):
        out = out + jnp.where(lane_is(out.shape, coarse_size + i), value, 0.0)
    return out


def by_parts(x, matrix, dims):
    rows = x.shape[0]
    both = mxu(jnp.concatenate(parts(x, 3), axis=0), matrix, dims)
    both = both[:rows] + (both[rows : 2 * rows] + both[2 * rows :])
    width = both.shape[1] // 3
    return both[:, :width] + (both[:, width : 2 * width] + both[:, 2 * width :])


def coarse_solve(right, down_ref, up_ref):
    lowered = by_parts(right, down_ref[...], LAST)
    return by_parts(lowered, up_ref[...], PLAIN), jnp.sum(lowered * lowered, axis=1, keepdims=True)


def coarse_part(sums, coarse_size):
    lanes = lax.broadcasted_iota(jnp.int32, sums.shape, 1)
    return jnp.where(lanes < coarse_size, sums, 0.0)


def two_high(x):
    return jnp.concatenate(parts(x, 2), axis=0)


def two_wide(x):
    high, low = parts(x, 2)
    return jnp.concatenate(
        [jnp.concatenate([high, high], axis=1), jnp.concatenate([low, low], axis=1)], axis=0
    )


def coarse_times(coarse, *image_refs):
    rows = coarse.shape[0]
    left = two_wide(coarse)
    both = [mxu(left, image[...]) for image in image_refs]
    return jnp.concatenate([x[:rows] + x[rows:] for x in both], axis=1)


def prepare_kernel(loads_ref, match_ref, schur_ref,
                   loads_out, hots_out, schur_out, match_held, sems):
    copies = [
        pltpu.make_async_copy(x, y, sems.at[i])
        for i, (x, y) in enumerate(
            ((match_ref, match_held), (loads_ref, loads_out), (schur_ref, schur_out))
        )
    ]
    for copy in copies:
        copy.start()
    size = loads_ref.shape[1] // 4
    copies[0].wait()
    for i in range(4):
        hots_out[i * size : (i + 1) * size, :] = one_hot(match_held, i)
    copies[1].wait()
    for i in (0, 2):
        block = slice(i * size, (i + 1) * size)
        loads_out[:, block] = turn(loads_out[:, block], hots_out[block, :])
    copies[2].wait()


def extra_kernel(coupling_ref, corners_ref, inverse_ref, hots_ref,
                 extra_out, spread_out, coupling_out, down_out, up_out):
    size = hots_ref.shape[1]
    slots = coupling_ref.shape[0]
    rows = extra_out.shape[0]
    hots = hots_of(hots_ref)
    extra_out[...] = jnp.full(extra_out.shape, -1.0, jnp.float32)
    corners = corners_ref[...].astype(jnp.float32)
    for i in range(4):
        extra_out[:slots, i * size : (i + 1) * size] = coupling_ref[:, i * size : (i + 1) * size]
        for k in range(3):
            at = i * size + k * rows
            extra_out[slots : slots + 1, at : at + slots] = corners
    for i in (0, 2):
        block = slice(i * size, (i + 1) * size)
        extra_out[:slots, block] = turn(coupling_ref[:, block], hots[i])
    coupling_out[...] = jnp.concatenate(parts(extra_out[...], 3), axis=0)
    spread_out[...] = spread(extra_out[...], slots, spread_out.shape[0])
    inverse = parts(inverse_ref[...], 3)
    down_out[...] = jnp.concatenate(inverse, axis=0)
    up_out[...] = jnp.concatenate(inverse, axis=1)


def turn_matrix_kernel(matrix_ref, hots_ref, out_ref):
    size = hots_ref.shape[1]
    hots = hots_of(hots_ref)
    for i in range(4):
        rows = slice(i * size, (i + 1) * size)
        block = faces_of(matrix_ref.at[rows, :], size)
        for j in (0, 2):
            block[j] = mxu(block[j], hots[j], LAST).astype(jnp.bfloat16)
        for j in range(4):
            if i in (0, 2):
                block[j] = mxu(hots[i], block[j]).astype(jnp.bfloat16)
            out_ref[rows, j * size : (j + 1) * size] = block[j]


def first_kernel(near0, near1, near2, near3, loads_ref, hots_ref, schur_ref,
                 residual_ref, send0, send1, send2, send3, result_ref):
    cases = loads_ref.shape[0]
    size = loads_ref.shape[1] // 4
    hots = hots_of(hots_ref)
    near = faces_in([x[...] for x in (near0, near1, near2, near3)])
    for i in (1, 3):
        near[i] = reorder(near[i], hots[i], PLAIN)
    residual = jump(near, faces_of(loads_ref, size))
    store(residual_ref, residual)
    product(schur_ref, result_ref, local_order(weighted(residual), hots, 1), [(0, cases, 1)])
    for ref, value in zip(
        (send0, send1, send2, send3), swapped(turned_result(result_ref, hots), odds())
    ):
        ref[...] = value


def coarse_kernel(cases, spread_ref, far_ref, near_ref, core_ref, image_ref, rest_ref):
    width, interface = spread_ref.shape
    size = interface // 4
    slots = near_ref.shape[0] - cases - 4
    own = faces_of(spread_ref, size)
    far, near, core = [
        spread(x[cases:, :size], slots, width) for x in (far_ref, near_ref, core_ref)
    ]
    zero = jnp.zeros_like(core)
    image = jump(faces_in([far, zero, near, core]), own)
    store_some(image_ref, [two_high(x) for x in image[:2]])
    store_some(rest_ref, image[2:])


def coarse_rest_kernel(cases, rest_ref, high_ref, image_ref):
    size = rest_ref.shape[1] // 2
    width = rest_ref.shape[0]
    slots = high_ref.shape[0] - cases - 4
    share = spread(high_ref[cases:, :size], slots, width)
    zero = jnp.zeros_like(share)
    low, high = faces_in([zero, share, zero, zero])[2:]
    store_some(image_ref, [two_high(rest_ref[:, :size] + low), two_high(rest_ref[:, size:] - high)])


def direction_kernel(coarse_size, count, *refs):
    own = refs[0:4]
    near = refs[4:8]
    extra_ref, coupling_ref, residual_ref, flex_ref = refs[8:12]
    n = 12
    if count > 1:
        before_ref = refs[12]
        before_free = refs[13:17]
        n = 17
    precond_ref, free0, free1, free2, free3, result_ref = refs[n:]
    size = own[0].shape[1]
    cases = residual_ref.shape[0]
    slots = extra_ref.shape[0] - 4
    precond = jump(faces_in([x[...] for x in near]), faces_in([x[...] for x in own]))
    precond = [0.5 * x for x in precond]
    store(precond_ref, precond)
    forces = signed(precond)
    left = face_parts(forces, 2)
    product(flex_ref, result_ref, left[: count * cases], [(0, cases, count)])
    free = faces_of(result_ref, size)
    extra = faces_of(extra_ref, size)
    for ref, value, rows in zip(
        (free0, free1, free2, free3), swapped(free, odds()), swapped(extra, odds())
    ):
        ref[:cases, :size] = value
        if count == 1:
            ref[cases:, :size] = rows
    scalars = [0.5 * total(faces_of(residual_ref, size), precond), total(forces, free)]
    if count > 1:
        before = signed(faces_of(before_ref, size))
        scalars.append(total(forces, faces_in([x[:cases, :size] for x in before_free])) + total(before, free))
    width = free3.shape[1] - size
    free3[:cases, size:] = partial_sums(
        left, coupling_ref[...], extra[0], slots, scalars, coarse_size, width
    )
    if count == 1:
        free3[cases:, size:] = jnp.zeros((free3.shape[0] - cases, width), jnp.float32)


def step_kernel(coarse_size, sums_ref, down_ref, up_ref, image_ref, rest_ref, own0, own1, own2, own3,
                near0, near1, near2, near3, residual_ref, hots_ref, schur_ref,
                new_ref, jump_ref, step_ref, send0, send1, send2, send3, result_ref):
    size = own0.shape[1]
    cases = sums_ref.shape[0]
    hots = hots_of(hots_ref)
    moved = jump(
        faces_in([x[:cases, :size] for x in (near0, near1, near2, near3)]),
        faces_in([x[:cases, :size] for x in (own0, own1, own2, own3)]),
    )
    store(jump_ref, moved)
    sums = sums_ref[...]
    coarse, energy = coarse_solve(coarse_part(sums, coarse_size), down_ref, up_ref)
    step = pick(sums, coarse_size) / (pick(sums, coarse_size + 1) + energy)
    step_ref[...] = jnp.broadcast_to(step, step_ref.shape)
    image = coarse_times(coarse, image_ref, rest_ref)
    residual = [
        residual_ref[:, i * size : (i + 1) * size]
        - step * (moved[i] + image[:, i * size : (i + 1) * size])
        for i in range(4)
    ]
    store(new_ref, residual)
    product(schur_ref, result_ref, local_order(weighted(residual), hots, 1), [(0, cases, 1)])
    for ref, value in zip(
        (send0, send1, send2, send3), swapped(turned_result(result_ref, hots), odds())
    ):
        ref[...] = value


def home_kernel(residual_ref, before_ref, precond_ref, jump_ref, image_ref, rest_ref, hots_ref,
                residual_out, before_out, precond_out, jump_out, image_out):
    size = hots_ref.shape[1]
    hots = hots_of(hots_ref)
    fields = [faces_of(x, size) for x in (residual_ref, before_ref, precond_ref, jump_ref)]
    image = [
        ref[:, block] for ref in (image_ref, rest_ref) for block in (slice(size), slice(size, None))
    ]
    for i in (0, 2):
        image[i] = mxu(image[i], hots[i]).astype(jnp.bfloat16)
        for field in fields:
            field[i] = turn_back(field[i], hots[i])
    store(image_out, image)
    for ref, field in zip((residual_out, before_out, precond_out, jump_out), fields):
        store(ref, field)


def last_kernel(coarse_size, first_ref, sums_ref, down_ref, up_ref, step_ref, residual_ref, before_ref,
                precond_ref, jump_ref, image_ref, hots_ref, own0, own1, own2, own3,
                near0, near1, near2, near3, multipliers_ref, out_ref):
    size = hots_ref.shape[1]
    hots = hots_of(hots_ref)
    following = jump(
        faces_in([x[:, :size] for x in (near0, near1, near2, near3)]),
        faces_in([x[:, :size] for x in (own0, own1, own2, own3)]),
    )
    for i in (0, 2):
        following[i] = turn_back(following[i], hots[i])
    first = first_ref[...]
    sums = sums_ref[...]
    beta = pick(sums, coarse_size) / pick(first, coarse_size)
    right = coarse_part(sums, coarse_size) + beta * coarse_part(first, coarse_size)
    coarse, energy = coarse_solve(right, down_ref, up_ref)
    local = pick(sums, coarse_size + 1) + beta * (
        pick(sums, coarse_size + 2) + beta * pick(first, coarse_size + 1)
    )
    step = pick(sums, coarse_size) / (local + energy)
    step_before = step_ref[:, 0:1]
    image = coarse_times(coarse, image_ref)
    for i in range(4):
        block = slice(i * size, (i + 1) * size)
        moved = following[i] + beta * jump_ref[:, block] + image[:, block]
        out_ref[:, i, :] = residual_ref[:, block] - step * moved
        before = before_ref[:, block]
        direction = precond_ref[:, block] + beta * before
        multipliers_ref[:, i, :] = step_before * before + step * direction


VMEM = pl.BlockSpec(memory_space=pltpu.VMEM)
OUTSIDE = pl.BlockSpec(memory_space=pltpu.HBM)


def call(kernel, args, outs, scratch=(), outside=(), flops=0):
    specs = [OUTSIDE if i in outside else VMEM for i in range(len(args))]
    shapes = [(x, jnp.float32) if isinstance(x[0], int) else x for x in outs]
    return pl.pallas_call(
        kernel,
        in_specs=specs,
        out_specs=[VMEM] * len(outs),
        out_shape=[jax.ShapeDtypeStruct(*x) for x in shapes],
        scratch_shapes=list(scratch),
        compiler_params=pltpu.CompilerParams(vmem_limit_bytes=28 * 2**20),
        cost_estimate=pl.CostEstimate(flops=flops, bytes_accessed=2**22, transcendentals=0),
    )(*args)


def shards(
    applied_loads,
    flex_matrix,
    schur_matrix,
    corner_coupling,
    coarse_inverse,
    face_match,
    corner_map,
):
    loads = applied_loads[0, 0]
    flex = flex_matrix[0, 0]
    schur = schur_matrix[0, 0]
    match = face_match[0, 0]
    cases, interface = loads.shape
    size = interface // 4
    slots = corner_coupling.shape[2]
    coarse_size = coarse_inverse.shape[0]
    width = -(-(coarse_size + 3) // LANES) * LANES
    work = 2 * cases * interface * interface

    inverse = jnp.pad(coarse_inverse, ((0, width - coarse_size), (0, width - coarse_size)))
    field = (cases, interface)
    face = (cases, size)
    result = pltpu.VMEM(field, jnp.float32)
    both_parts = ((2 * width, interface), jnp.bfloat16)

    held = [pltpu.with_memory_space_constraint(x, pltpu.HBM) for x in (loads, match, schur)]
    sends = swapped(
        [loads[:, i * size : (i + 1) * size] for i in range(4)], (odd("sub"), odd("grp"))
    )
    sends = lax.optimization_barrier(sends)
    near = exchange(sends)
    loads, hots, schur = call(
        prepare_kernel,
        held,
        [field, ((4 * size, size), jnp.bfloat16), (schur.shape, jnp.bfloat16)],
        [pltpu.VMEM(match.shape, jnp.int32), pltpu.SemaphoreType.DMA((3,))],
        outside=(0, 1, 2),
        flops=work,
    )
    residual, *own_first = call(
        first_kernel, [*near, loads, hots, schur], [field] + [face] * 4, [result], flops=work
    )
    near = exchange(own_first)
    residual, coupling, corners, flex = lax.optimization_barrier(
        (residual, corner_coupling[0, 0], corner_map[0], flex)
    )
    (flex,) = call(
        turn_matrix_kernel, [flex, hots], [(flex.shape, jnp.bfloat16)], flops=2 * work
    )
    extra, own_spread, coupling, down, up = call(
        extra_kernel,
        [coupling, corners, inverse, hots],
        [
            (slots + 4, interface),
            (width, interface),
            ((3 * (slots + 4), interface), jnp.bfloat16),
            ((3 * width, width), jnp.bfloat16),
            ((width, 3 * width), jnp.bfloat16),
        ],
        flops=work // 4,
    )
    before, *own_free = call(
        functools.partial(direction_kernel, coarse_size, 1),
        [*own_first, *near, extra, coupling, residual, flex],
        [field] + [(cases + slots + 4, size)] * 3 + [(cases + slots + 4, size + width)],
        [result],
        flops=work,
    )
    first_sums, near = sum_and_exchange(own_free, cases)
    half = ((2 * width, interface // 2), jnp.bfloat16)
    image, rest = call(
        functools.partial(coarse_kernel, cases),
        [own_spread, near[0], near[2], near[3]],
        [half, (width, interface // 2)],
        flops=work // 4,
    )
    (rest,) = call(
        functools.partial(coarse_rest_kernel, cases), [rest, near[1]], [half], flops=work // 8
    )
    residual, moved, step, *own = call(
        functools.partial(step_kernel, coarse_size),
        [first_sums, down, up, image, rest, *own_free, *near, residual, hots, schur],
        [field, field, (cases, LANES)] + [face] * 4,
        [result],
        flops=work,
    )
    near = exchange(own)
    precond, *own = call(
        functools.partial(direction_kernel, coarse_size, 2),
        [*own, *near, extra, coupling, residual, flex, before, *own_free],
        [field] + [face] * 3 + [(cases, size + width)],
        [result],
        flops=work,
    )
    fields = call(
        home_kernel,
        [residual, before, precond, moved, image, rest, hots],
        [field] * 4 + [both_parts],
        flops=work // 2,
    )
    sums, near = sum_and_exchange(own, cases)
    layout = (cases, 4, size)
    multipliers, residual = call(
        functools.partial(last_kernel, coarse_size),
        [first_sums, sums, down, up, step, *fields, hots, *own, *near],
        [layout, layout],
        flops=work // 4,
    )
    return multipliers[None, None], residual[None, None]


def solution(mesh):
    return jax.shard_map(
        shards,
        mesh=mesh,
        in_specs=(
            P("sub", "grp", None, None),
            P("sub", "grp", None, None),
            P("sub", "grp", None, None),
            P("sub", "grp", None, None),
            P(),
            P("sub", "grp", None, None),
            P("sub", "grp", None),
        ),
        out_specs=(P("sub", "grp", None, None, None), P("sub", "grp", None, None, None)),
        check_vma=False,
    )
```

```python
import functools

import jax
import jax.numpy as jnp
from jax import lax
from jax.experimental import pallas as pl
from jax.experimental.pallas import tpu as pltpu
from jax.sharding import PartitionSpec as P

HIGHEST = lax.Precision.HIGHEST
PLAIN = (((1,), (0,)), ((), ()))
LAST = (((1,), (1,)), ((), ()))
LANES = 128
SIGNS = (-1.0, 1.0, -1.0, 1.0)


def odd(axis):
    return lax.axis_index(axis) % 2 == 1


def swapped(faces, odds):
    far, near = [], []
    for (low, high), is_odd in zip((faces[0:2], faces[2:4]), odds):
        far.append(jnp.where(is_odd, high, low))
        near.append(jnp.where(is_odd, low, high))
    return far + near


def swap(face, i):
    axis = ("sub", "grp", "sub", "grp")[i]
    peers = lax.axis_size(axis)
    if i < 2:
        pairs = [(j, (j + 2 * (j % 2) - 1) % peers) for j in range(peers)]
    else:
        pairs = [(j, j ^ 1) for j in range(peers)]
    return lax.ppermute(face, axis, pairs)


def exchange(faces):
    return lax.optimization_barrier([swap(face, i) for i, face in enumerate(faces)])


def sum_over(values, axis, step, before=(), after=()):
    peers = lax.axis_size(axis)
    first = True
    while step < peers:
        count = 4 if 4 * step <= peers else 2
        others = [
            lax.ppermute(values, axis, [(i, i ^ (k * step)) for i in range(peers)])
            for k in ((2, 1, 3) if count == 4 else (1,))
        ]
        if first:
            before, others, after = lax.optimization_barrier((before, others, after))
            first = False
        if count == 4:
            values = (values + others[1]) + (others[0] + others[2])
        else:
            values = values + others[0]
        step *= count
    return values, before, after


def sum_and_exchange(faces, cases):
    far, high, near, core = faces
    size = near.shape[1]
    other = swap(core, 3)
    values = core[:cases, size:] + other[:cases, size:]
    near, values = lax.optimization_barrier((near, values))
    near = swap(near, 2)
    values, far, _ = sum_over(values, "grp", 2, [swap(far, 0)])
    far, high, values = lax.optimization_barrier((far, high, values))
    values, high, _ = sum_over(values, "sub", 1, [swap(high, 1)])
    return values, [*far, *high, near, other]


def one_hot(match_ref, i):
    row = match_ref[i : i + 1, :]
    size = row.shape[1]
    nodes = lax.broadcasted_iota(jnp.int32, (size, size), 0)
    return jnp.where(nodes == row, 1.0, 0.0).astype(jnp.bfloat16)


def parts(x, count):
    out = []
    for _ in range(count):
        part = x.astype(jnp.bfloat16)
        out.append(part)
        x = x - part.astype(jnp.float32)
    return out


def mxu(x, y, dims=PLAIN):
    return lax.dot_general(x, y, dims, preferred_element_type=jnp.float32)


def exact(x, y, dims=PLAIN):
    return lax.dot_general(x, y, dims, precision=HIGHEST, preferred_element_type=jnp.float32)


def reorder(x, hot, dims):
    rows = x.shape[0]
    both = mxu(jnp.concatenate(parts(x, 3), axis=0), hot, dims)
    return both[:rows] + both[rows : 2 * rows] + both[2 * rows :]


def turn(x, hot):
    return reorder(x, hot, LAST)


def turn_back(x, hot):
    return reorder(x, hot, PLAIN)


def jump(received, own):
    return [
        received[0] - own[0],
        own[1] - received[1],
        received[2] - own[2],
        own[3] - received[3],
    ]


def odds():
    return odd("sub"), odd("grp")


def faces_in(values):
    out = []
    for far, near, is_odd in zip(values[0:2], values[2:4], odds()):
        out += [jnp.where(is_odd, near, far), jnp.where(is_odd, far, near)]
    return out


def faces_of(ref, size):
    return [ref[:, i * size : (i + 1) * size] for i in range(4)]


def store(ref, faces):
    size = faces[0].shape[1]
    for i in range(4):
        ref[:, i * size : (i + 1) * size] = faces[i]


def store_some(ref, faces):
    size = faces[0].shape[1]
    for i, face in enumerate(faces):
        ref[:, i * size : (i + 1) * size] = face


def total(xs, ys):
    return sum(jnp.sum(x * y, axis=1, keepdims=True) for x, y in zip(xs, ys))


def blocks_of(interface):
    width = 256 if interface % 256 == 0 else interface
    return [slice(i, i + width) for i in range(0, interface, width)]


def product(matrix_ref, result_ref, left, groups):
    for block in blocks_of(matrix_ref.shape[1]):
        both = mxu(left, matrix_ref[:, block])
        at = 0
        for first, rows, count in groups:
            value = both[first : first + rows]
            for i in range(1, count):
                value = value + both[first + i * rows : first + (i + 1) * rows]
            result_ref[at : at + rows, block] = value
            at += rows


def local_order(faces, hots, count):
    split = [jnp.concatenate(parts(x, count), axis=0) for x in faces]
    split[0] = mxu(split[0], hots[0]).astype(jnp.bfloat16)
    split[2] = mxu(split[2], hots[2]).astype(jnp.bfloat16)
    return jnp.concatenate(split, axis=1)


def face_parts(faces, count):
    return jnp.concatenate(
        [jnp.concatenate(parts(x, count), axis=0) for x in faces], axis=1
    )


def turned_result(result_ref, hots):
    size = result_ref.shape[1] // 4
    own = faces_of(result_ref, size)
    own[0] = turn(own[0], hots[0])
    own[2] = turn(own[2], hots[2])
    return own


def weighted(faces):
    return [(0.5 * s) * x for s, x in zip(SIGNS, faces)]


def hots_of(hots_ref):
    size = hots_ref.shape[1]
    return [hots_ref[i * size : (i + 1) * size, :] for i in range(4)]


def signed(faces):
    return [s * x for s, x in zip(SIGNS, faces)]


def lane_is(shape, lane):
    return lax.broadcasted_iota(jnp.int32, shape, 1) == lane


def pick(values, lane):
    return jnp.sum(jnp.where(lane_is(values.shape, lane), values, 0.0), axis=1, keepdims=True)


def numbering(extra, slots, width):
    numbers = extra[slots : slots + 1, :LANES]
    nodes = lax.broadcasted_iota(jnp.int32, (width, LANES), 0).astype(jnp.float32)
    hot = jnp.where(nodes == numbers, 1.0, 0.0)
    return hot[:, : 3 * extra.shape[0]].astype(jnp.bfloat16)


def spread(extra, slots, width):
    return mxu(numbering(extra, slots, width), jnp.concatenate(parts(extra, 3), axis=0))


def partial_sums(left, coupling, extra, slots, scalars, coarse_size, width):
    out = reorder(mxu(left, coupling, LAST), numbering(extra, slots, width), LAST)
    rows = out.shape[0] // 2
    out = out[:rows] + out[rows:]
    for i, value in enumerate(scalars):
        out = out + jnp.where(lane_is(out.shape, coarse_size + i), value, 0.0)
    return out


def by_parts(x, matrix, dims):
    rows = x.shape[0]
    both = mxu(jnp.concatenate(parts(x, 3), axis=0), matrix, dims)
    both = both[:rows] + (both[rows : 2 * rows] + both[2 * rows :])
    width = both.shape[1] // 3
    return both[:, :width] + (both[:, width : 2 * width] + both[:, 2 * width :])


def coarse_solve(right, down_ref, up_ref):
    lowered = by_parts(right, down_ref[...], LAST)
    return by_parts(lowered, up_ref[...], PLAIN), jnp.sum(lowered * lowered, axis=1, keepdims=True)


def coarse_part(sums, coarse_size):
    lanes = lax.broadcasted_iota(jnp.int32, sums.shape, 1)
    return jnp.where(lanes < coarse_size, sums, 0.0)


def two_high(x):
    return jnp.concatenate(parts(x, 2), axis=0)


def two_wide(x):
    high, low = parts(x, 2)
    return jnp.concatenate(
        [jnp.concatenate([high, high], axis=1), jnp.concatenate([low, low], axis=1)], axis=0
    )


def coarse_times(coarse, *image_refs):
    rows = coarse.shape[0]
    left = two_wide(coarse)
    both = [mxu(left, image[...]) for image in image_refs]
    return jnp.concatenate([x[:rows] + x[rows:] for x in both], axis=1)


def prepare_kernel(loads_ref, match_ref, schur_ref,
                   loads_out, hots_out, schur_out, match_held, sems):
    copies = [
        pltpu.make_async_copy(x, y, sems.at[i])
        for i, (x, y) in enumerate(
            ((match_ref, match_held), (loads_ref, loads_out), (schur_ref, schur_out))
        )
    ]
    for copy in copies:
        copy.start()
    size = loads_ref.shape[1] // 4
    copies[0].wait()
    for i in range(4):
        hots_out[i * size : (i + 1) * size, :] = one_hot(match_held, i)
    copies[1].wait()
    for i in (0, 2):
        block = slice(i * size, (i + 1) * size)
        loads_out[:, block] = turn(loads_out[:, block], hots_out[block, :])
    copies[2].wait()


def extra_kernel(coupling_ref, corners_ref, inverse_ref, hots_ref,
                 extra_out, spread_out, coupling_out, down_out, up_out):
    size = hots_ref.shape[1]
    slots = coupling_ref.shape[0]
    rows = extra_out.shape[0]
    hots = hots_of(hots_ref)
    extra_out[...] = jnp.full(extra_out.shape, -1.0, jnp.float32)
    corners = corners_ref[...].astype(jnp.float32)
    for i in range(4):
        extra_out[:slots, i * size : (i + 1) * size] = coupling_ref[:, i * size : (i + 1) * size]
        for k in range(3):
            at = i * size + k * rows
            extra_out[slots : slots + 1, at : at + slots] = corners
    for i in (0, 2):
        block = slice(i * size, (i + 1) * size)
        extra_out[:slots, block] = turn(coupling_ref[:, block], hots[i])
    coupling_out[...] = jnp.concatenate(parts(extra_out[...], 3), axis=0)
    spread_out[...] = spread(extra_out[...], slots, spread_out.shape[0])
    inverse = parts(inverse_ref[...], 3)
    down_out[...] = jnp.concatenate(inverse, axis=0)
    up_out[...] = jnp.concatenate(inverse, axis=1)


def turn_matrix_kernel(matrix_ref, hots_ref, out_ref):
    size = hots_ref.shape[1]
    hots = hots_of(hots_ref)
    for i in range(4):
        rows = slice(i * size, (i + 1) * size)
        block = faces_of(matrix_ref.at[rows, :], size)
        for j in (0, 2):
            block[j] = mxu(block[j], hots[j], LAST).astype(jnp.bfloat16)
        for j in range(4):
            if i in (0, 2):
                block[j] = mxu(hots[i], block[j]).astype(jnp.bfloat16)
            out_ref[rows, j * size : (j + 1) * size] = block[j]


def first_kernel(near0, near1, near2, near3, loads_ref, hots_ref, schur_ref,
                 residual_ref, send0, send1, send2, send3, result_ref):
    cases = loads_ref.shape[0]
    size = loads_ref.shape[1] // 4
    hots = hots_of(hots_ref)
    near = faces_in([x[...] for x in (near0, near1, near2, near3)])
    for i in (1, 3):
        near[i] = reorder(near[i], hots[i], PLAIN)
    residual = jump(near, faces_of(loads_ref, size))
    store(residual_ref, residual)
    product(schur_ref, result_ref, local_order(weighted(residual), hots, 1), [(0, cases, 1)])
    for ref, value in zip(
        (send0, send1, send2, send3), swapped(turned_result(result_ref, hots), odds())
    ):
        ref[...] = value


def coarse_kernel(cases, spread_ref, far_ref, near_ref, core_ref, image_ref, rest_ref):
    width, interface = spread_ref.shape
    size = interface // 4
    slots = near_ref.shape[0] - cases - 4
    own = faces_of(spread_ref, size)
    far, near, core = [
        spread(x[cases:, :size], slots, width) for x in (far_ref, near_ref, core_ref)
    ]
    zero = jnp.zeros_like(core)
    image = jump(faces_in([far, zero, near, core]), own)
    store_some(image_ref, [two_high(x) for x in image[:2]])
    store_some(rest_ref, image[2:])


def coarse_rest_kernel(cases, rest_ref, high_ref, image_ref):
    size = rest_ref.shape[1] // 2
    width = rest_ref.shape[0]
    slots = high_ref.shape[0] - cases - 4
    share = spread(high_ref[cases:, :size], slots, width)
    zero = jnp.zeros_like(share)
    low, high = faces_in([zero, share, zero, zero])[2:]
    store_some(image_ref, [two_high(rest_ref[:, :size] + low), two_high(rest_ref[:, size:] - high)])


def direction_kernel(coarse_size, count, *refs):
    own = refs[0:4]
    near = refs[4:8]
    extra_ref, coupling_ref, residual_ref, flex_ref = refs[8:12]
    n = 12
    if count > 1:
        before_ref = refs[12]
        before_free = refs[13:17]
        n = 17
    precond_ref, free0, free1, free2, free3, result_ref = refs[n:]
    size = own[0].shape[1]
    cases = residual_ref.shape[0]
    slots = extra_ref.shape[0] - 4
    precond = jump(faces_in([x[...] for x in near]), faces_in([x[...] for x in own]))
    precond = [0.5 * x for x in precond]
    store(precond_ref, precond)
    forces = signed(precond)
    left = face_parts(forces, 2)
    product(flex_ref, result_ref, left[: count * cases], [(0, cases, count)])
    free = faces_of(result_ref, size)
    extra = faces_of(extra_ref, size)
    for ref, value, rows in zip(
        (free0, free1, free2, free3), swapped(free, odds()), swapped(extra, odds())
    ):
        ref[:cases, :size] = value
        if count == 1:
            ref[cases:, :size] = rows
    scalars = [0.5 * total(faces_of(residual_ref, size), precond), total(forces, free)]
    if count > 1:
        before = signed(faces_of(before_ref, size))
        scalars.append(total(forces, faces_in([x[:cases, :size] for x in before_free])) + total(before, free))
    width = free3.shape[1] - size
    free3[:cases, size:] = partial_sums(
        left, coupling_ref[...], extra[0], slots, scalars, coarse_size, width
    )
    if count == 1:
        free3[cases:, size:] = jnp.zeros((free3.shape[0] - cases, width), jnp.float32)


def step_kernel(coarse_size, sums_ref, down_ref, up_ref, image_ref, rest_ref, own0, own1, own2, own3,
                near0, near1, near2, near3, residual_ref, hots_ref, schur_ref,
                new_ref, jump_ref, step_ref, send0, send1, send2, send3, result_ref):
    size = own0.shape[1]
    cases = sums_ref.shape[0]
    hots = hots_of(hots_ref)
    moved = jump(
        faces_in([x[:cases, :size] for x in (near0, near1, near2, near3)]),
        faces_in([x[:cases, :size] for x in (own0, own1, own2, own3)]),
    )
    store(jump_ref, moved)
    sums = sums_ref[...]
    coarse, energy = coarse_solve(coarse_part(sums, coarse_size), down_ref, up_ref)
    step = pick(sums, coarse_size) / (pick(sums, coarse_size + 1) + energy)
    step_ref[...] = jnp.broadcast_to(step, step_ref.shape)
    image = coarse_times(coarse, image_ref, rest_ref)
    residual = [
        residual_ref[:, i * size : (i + 1) * size]
        - step * (moved[i] + image[:, i * size : (i + 1) * size])
        for i in range(4)
    ]
    store(new_ref, residual)
    product(schur_ref, result_ref, local_order(weighted(residual), hots, 1), [(0, cases, 1)])
    for ref, value in zip(
        (send0, send1, send2, send3), swapped(turned_result(result_ref, hots), odds())
    ):
        ref[...] = value


def home_kernel(residual_ref, before_ref, precond_ref, jump_ref, image_ref, rest_ref, hots_ref,
                own_far, own_near, far, near,
                residual_out, before_out, precond_out, jump_out, image_out, next_out):
    size = hots_ref.shape[1]
    hots = hots_of(hots_ref)
    fields = [faces_of(x, size) for x in (residual_ref, before_ref, precond_ref, jump_ref)]
    image = [
        ref[:, block] for ref in (image_ref, rest_ref) for block in (slice(size), slice(size, None))
    ]
    for i in (0, 2):
        image[i] = mxu(image[i], hots[i]).astype(jnp.bfloat16)
        for field in fields:
            field[i] = turn_back(field[i], hots[i])
    low, high = faces_in([far[...], far[...], near[...], near[...]])[:2]
    own = [own_far[...], own_near[...]]
    own_low, own_high = faces_in([own[0], own[0], own[1], own[1]])[:2]
    store_some(next_out, [turn_back(low - own_low, hots[0]), own_high - high])
    store(image_out, image)
    for ref, field in zip((residual_out, before_out, precond_out, jump_out), fields):
        store(ref, field)


def last_kernel(coarse_size, first_ref, sums_ref, down_ref, up_ref, step_ref, residual_ref, before_ref,
                precond_ref, jump_ref, image_ref, next_ref, hots_ref, own_high, own_core,
                high_ref, core_ref, multipliers_ref, out_ref):
    size = hots_ref.shape[1]
    hots = hots_of(hots_ref)
    grp = [high_ref[...], core_ref[:, :size]]
    own = [own_high[...], own_core[:, :size]]
    low, high = faces_in([grp[0], grp[0], grp[1], grp[1]])[2:]
    own_low, own_high = faces_in([own[0], own[0], own[1], own[1]])[2:]
    following = [
        next_ref[:, :size],
        next_ref[:, size:],
        turn_back(low - own_low, hots[2]),
        own_high - high,
    ]
    first = first_ref[...]
    sums = sums_ref[...]
    beta = pick(sums, coarse_size) / pick(first, coarse_size)
    right = coarse_part(sums, coarse_size) + beta * coarse_part(first, coarse_size)
    coarse, energy = coarse_solve(right, down_ref, up_ref)
    local = pick(sums, coarse_size + 1) + beta * (
        pick(sums, coarse_size + 2) + beta * pick(first, coarse_size + 1)
    )
    step = pick(sums, coarse_size) / (local + energy)
    step_before = step_ref[:, 0:1]
    image = coarse_times(coarse, image_ref)
    for i in range(4):
        block = slice(i * size, (i + 1) * size)
        moved = following[i] + beta * jump_ref[:, block] + image[:, block]
        out_ref[:, i, :] = residual_ref[:, block] - step * moved
        before = before_ref[:, block]
        direction = precond_ref[:, block] + beta * before
        multipliers_ref[:, i, :] = step_before * before + step * direction


VMEM = pl.BlockSpec(memory_space=pltpu.VMEM)
OUTSIDE = pl.BlockSpec(memory_space=pltpu.HBM)


def call(kernel, args, outs, scratch=(), outside=(), flops=0):
    specs = [OUTSIDE if i in outside else VMEM for i in range(len(args))]
    shapes = [(x, jnp.float32) if isinstance(x[0], int) else x for x in outs]
    return pl.pallas_call(
        kernel,
        in_specs=specs,
        out_specs=[VMEM] * len(outs),
        out_shape=[jax.ShapeDtypeStruct(*x) for x in shapes],
        scratch_shapes=list(scratch),
        compiler_params=pltpu.CompilerParams(vmem_limit_bytes=28 * 2**20),
        cost_estimate=pl.CostEstimate(flops=flops, bytes_accessed=2**22, transcendentals=0),
    )(*args)


def shards(
    applied_loads,
    flex_matrix,
    schur_matrix,
    corner_coupling,
    coarse_inverse,
    face_match,
    corner_map,
):
    loads = applied_loads[0, 0]
    flex = flex_matrix[0, 0]
    schur = schur_matrix[0, 0]
    match = face_match[0, 0]
    cases, interface = loads.shape
    size = interface // 4
    slots = corner_coupling.shape[2]
    coarse_size = coarse_inverse.shape[0]
    width = -(-(coarse_size + 3) // LANES) * LANES
    work = 2 * cases * interface * interface

    inverse = jnp.pad(coarse_inverse, ((0, width - coarse_size), (0, width - coarse_size)))
    field = (cases, interface)
    face = (cases, size)
    result = pltpu.VMEM(field, jnp.float32)
    both_parts = ((2 * width, interface), jnp.bfloat16)

    held = [pltpu.with_memory_space_constraint(x, pltpu.HBM) for x in (loads, match, schur)]
    sends = swapped(
        [loads[:, i * size : (i + 1) * size] for i in range(4)], (odd("sub"), odd("grp"))
    )
    sends = lax.optimization_barrier(sends)
    near = exchange(sends)
    loads, hots, schur = call(
        prepare_kernel,
        held,
        [field, ((4 * size, size), jnp.bfloat16), (schur.shape, jnp.bfloat16)],
        [pltpu.VMEM(match.shape, jnp.int32), pltpu.SemaphoreType.DMA((3,))],
        outside=(0, 1, 2),
        flops=work,
    )
    residual, *own_first = call(
        first_kernel, [*near, loads, hots, schur], [field] + [face] * 4, [result], flops=work
    )
    near = exchange(own_first)
    residual, coupling, corners, flex = lax.optimization_barrier(
        (residual, corner_coupling[0, 0], corner_map[0], flex)
    )
    (flex,) = call(
        turn_matrix_kernel, [flex, hots], [(flex.shape, jnp.bfloat16)], flops=2 * work
    )
    extra, own_spread, coupling, down, up = call(
        extra_kernel,
        [coupling, corners, inverse, hots],
        [
            (slots + 4, interface),
            (width, interface),
            ((3 * (slots + 4), interface), jnp.bfloat16),
            ((3 * width, width), jnp.bfloat16),
            ((width, 3 * width), jnp.bfloat16),
        ],
        flops=work // 4,
    )
    before, *own_free = call(
        functools.partial(direction_kernel, coarse_size, 1),
        [*own_first, *near, extra, coupling, residual, flex],
        [field] + [(cases + slots + 4, size)] * 3 + [(cases + slots + 4, size + width)],
        [result],
        flops=work,
    )
    first_sums, near = sum_and_exchange(own_free, cases)
    half = ((2 * width, interface // 2), jnp.bfloat16)
    image, rest = call(
        functools.partial(coarse_kernel, cases),
        [own_spread, near[0], near[2], near[3]],
        [half, (width, interface // 2)],
        flops=work // 4,
    )
    (rest,) = call(
        functools.partial(coarse_rest_kernel, cases), [rest, near[1]], [half], flops=work // 8
    )
    residual, moved, step, *own = call(
        functools.partial(step_kernel, coarse_size),
        [first_sums, down, up, image, rest, *own_free, *near, residual, hots, schur],
        [field, field, (cases, LANES)] + [face] * 4,
        [result],
        flops=work,
    )
    near = exchange(own)
    precond, *own = call(
        functools.partial(direction_kernel, coarse_size, 2),
        [*own, *near, extra, coupling, residual, flex, before, *own_free],
        [field] + [face] * 3 + [(cases, size + width)],
        [result],
        flops=work,
    )
    sums, near = sum_and_exchange(own, cases)
    fields = call(
        home_kernel,
        [residual, before, precond, moved, image, rest, hots, own[0], own[2], near[0], near[2]],
        [field] * 4 + [both_parts, (cases, 2 * size)],
        flops=work // 2,
    )
    layout = (cases, 4, size)
    multipliers, residual = call(
        functools.partial(last_kernel, coarse_size),
        [first_sums, sums, down, up, step, *fields, hots, own[1], own[3], near[1], near[3]],
        [layout, layout],
        flops=work // 4,
    )
    return multipliers[None, None], residual[None, None]


def solution(mesh):
    return jax.shard_map(
        shards,
        mesh=mesh,
        in_specs=(
            P("sub", "grp", None, None),
            P("sub", "grp", None, None),
            P("sub", "grp", None, None),
            P("sub", "grp", None, None),
            P(),
            P("sub", "grp", None, None),
            P("sub", "grp", None),
        ),
        out_specs=(P("sub", "grp", None, None, None), P("sub", "grp", None, None, None)),
        check_vma=False,
    )
```

```python
import functools

import jax
import jax.numpy as jnp
from jax import lax
from jax.experimental import pallas as pl
from jax.experimental.pallas import tpu as pltpu
from jax.sharding import PartitionSpec as P

HIGHEST = lax.Precision.HIGHEST
PLAIN = (((1,), (0,)), ((), ()))
LAST = (((1,), (1,)), ((), ()))
LANES = 128
SIGNS = (-1.0, 1.0, -1.0, 1.0)


def odd(axis):
    return lax.axis_index(axis) % 2 == 1


def swapped(faces, odds):
    far, near = [], []
    for (low, high), is_odd in zip((faces[0:2], faces[2:4]), odds):
        far.append(jnp.where(is_odd, high, low))
        near.append(jnp.where(is_odd, low, high))
    return far + near


def swap(face, i):
    axis = ("sub", "grp", "sub", "grp")[i]
    peers = lax.axis_size(axis)
    if i < 2:
        pairs = [(j, (j + 2 * (j % 2) - 1) % peers) for j in range(peers)]
    else:
        pairs = [(j, j ^ 1) for j in range(peers)]
    return lax.ppermute(face, axis, pairs)


def exchange(faces):
    return lax.optimization_barrier([swap(face, i) for i, face in enumerate(faces)])


def sum_over(values, axis, step, before=(), after=()):
    peers = lax.axis_size(axis)
    first = True
    while step < peers:
        count = 4 if 4 * step <= peers else 2
        others = [
            lax.ppermute(values, axis, [(i, i ^ (k * step)) for i in range(peers)])
            for k in ((2, 1, 3) if count == 4 else (1,))
        ]
        if first:
            before, others, after = lax.optimization_barrier((before, others, after))
            first = False
        if count == 4:
            values = (values + others[1]) + (others[0] + others[2])
        else:
            values = values + others[0]
        step *= count
    return values, before, after


def sum_and_exchange(faces, cases):
    far, high, near, core = faces
    size = near.shape[1]
    other = swap(core, 3)
    values = core[:cases, size:] + other[:cases, size:]
    near, high, values = lax.optimization_barrier((near, high, values))
    near = swap(near, 2)
    values, far, high = sum_over(values, "grp", 2, [swap(far, 0)], [swap(high, 1)])
    far, high, values = lax.optimization_barrier((far, high, values))
    values, _, _ = sum_over(values, "sub", 1)
    return values, [*far, *high, near, other]


def one_hot(match_ref, i):
    row = match_ref[i : i + 1, :]
    size = row.shape[1]
    nodes = lax.broadcasted_iota(jnp.int32, (size, size), 0)
    return jnp.where(nodes == row, 1.0, 0.0).astype(jnp.bfloat16)


def parts(x, count):
    out = []
    for _ in range(count):
        part = x.astype(jnp.bfloat16)
        out.append(part)
        x = x - part.astype(jnp.float32)
    return out


def mxu(x, y, dims=PLAIN):
    return lax.dot_general(x, y, dims, preferred_element_type=jnp.float32)


def exact(x, y, dims=PLAIN):
    return lax.dot_general(x, y, dims, precision=HIGHEST, preferred_element_type=jnp.float32)


def reorder(x, hot, dims):
    rows = x.shape[0]
    both = mxu(jnp.concatenate(parts(x, 3), axis=0), hot, dims)
    return both[:rows] + both[rows : 2 * rows] + both[2 * rows :]


def turn(x, hot):
    return reorder(x, hot, LAST)


def turn_back(x, hot):
    return reorder(x, hot, PLAIN)


def jump(received, own):
    return [
        received[0] - own[0],
        own[1] - received[1],
        received[2] - own[2],
        own[3] - received[3],
    ]


def odds():
    return odd("sub"), odd("grp")


def faces_in(values):
    out = []
    for far, near, is_odd in zip(values[0:2], values[2:4], odds()):
        out += [jnp.where(is_odd, near, far), jnp.where(is_odd, far, near)]
    return out


def faces_of(ref, size):
    return [ref[:, i * size : (i + 1) * size] for i in range(4)]


def store(ref, faces):
    size = faces[0].shape[1]
    for i in range(4):
        ref[:, i * size : (i + 1) * size] = faces[i]


def store_some(ref, faces):
    size = faces[0].shape[1]
    for i, face in enumerate(faces):
        ref[:, i * size : (i + 1) * size] = face


def total(xs, ys):
    return sum(jnp.sum(x * y, axis=1, keepdims=True) for x, y in zip(xs, ys))


def blocks_of(interface):
    width = 256 if interface % 256 == 0 else interface
    return [slice(i, i + width) for i in range(0, interface, width)]


def product(matrix_ref, result_ref, left, groups):
    for block in blocks_of(matrix_ref.shape[1]):
        both = mxu(left, matrix_ref[:, block])
        at = 0
        for first, rows, count in groups:
            value = both[first : first + rows]
            for i in range(1, count):
                value = value + both[first + i * rows : first + (i + 1) * rows]
            result_ref[at : at + rows, block] = value
            at += rows


def local_order(faces, hots, count):
    split = [jnp.concatenate(parts(x, count), axis=0) for x in faces]
    split[0] = mxu(split[0], hots[0]).astype(jnp.bfloat16)
    split[2] = mxu(split[2], hots[2]).astype(jnp.bfloat16)
    return jnp.concatenate(split, axis=1)


def face_parts(faces, count):
    return jnp.concatenate(
        [jnp.concatenate(parts(x, count), axis=0) for x in faces], axis=1
    )


def turned_result(result_ref, hots):
    size = result_ref.shape[1] // 4
    own = faces_of(result_ref, size)
    own[0] = turn(own[0], hots[0])
    own[2] = turn(own[2], hots[2])
    return own


def weighted(faces):
    return [(0.5 * s) * x for s, x in zip(SIGNS, faces)]


def hots_of(hots_ref):
    size = hots_ref.shape[1]
    return [hots_ref[i * size : (i + 1) * size, :] for i in range(4)]


def signed(faces):
    return [s * x for s, x in zip(SIGNS, faces)]


def lane_is(shape, lane):
    return lax.broadcasted_iota(jnp.int32, shape, 1) == lane


def pick(values, lane):
    return jnp.sum(jnp.where(lane_is(values.shape, lane), values, 0.0), axis=1, keepdims=True)


def numbering(extra, slots, width):
    numbers = extra[slots : slots + 1, :LANES]
    nodes = lax.broadcasted_iota(jnp.int32, (width, LANES), 0).astype(jnp.float32)
    hot = jnp.where(nodes == numbers, 1.0, 0.0)
    return hot[:, : 3 * extra.shape[0]].astype(jnp.bfloat16)


def spread(extra, slots, width):
    return mxu(numbering(extra, slots, width), jnp.concatenate(parts(extra, 3), axis=0))


def partial_sums(left, coupling, extra, slots, scalars, coarse_size, width):
    out = reorder(mxu(left, coupling, LAST), numbering(extra, slots, width), LAST)
    rows = out.shape[0] // 2
    out = out[:rows] + out[rows:]
    for i, value in enumerate(scalars):
        out = out + jnp.where(lane_is(out.shape, coarse_size + i), value, 0.0)
    return out


def by_parts(x, matrix, dims):
    rows = x.shape[0]
    both = mxu(jnp.concatenate(parts(x, 3), axis=0), matrix, dims)
    both = both[:rows] + (both[rows : 2 * rows] + both[2 * rows :])
    width = both.shape[1] // 3
    return both[:, :width] + (both[:, width : 2 * width] + both[:, 2 * width :])


def coarse_solve(right, down_ref, up_ref):
    lowered = by_parts(right, down_ref[...], LAST)
    return by_parts(lowered, up_ref[...], PLAIN), jnp.sum(lowered * lowered, axis=1, keepdims=True)


def coarse_part(sums, coarse_size):
    lanes = lax.broadcasted_iota(jnp.int32, sums.shape, 1)
    return jnp.where(lanes < coarse_size, sums, 0.0)


def two_high(x):
    return jnp.concatenate(parts(x, 2), axis=0)


def two_wide(x):
    high, low = parts(x, 2)
    return jnp.concatenate(
        [jnp.concatenate([high, high], axis=1), jnp.concatenate([low, low], axis=1)], axis=0
    )


def coarse_times(coarse, *image_refs):
    rows = coarse.shape[0]
    left = two_wide(coarse)
    both = [mxu(left, image[...]) for image in image_refs]
    return jnp.concatenate([x[:rows] + x[rows:] for x in both], axis=1)


def prepare_kernel(loads_ref, match_ref, schur_ref,
                   loads_out, hots_out, schur_out, match_held, sems):
    copies = [
        pltpu.make_async_copy(x, y, sems.at[i])
        for i, (x, y) in enumerate(
            ((match_ref, match_held), (loads_ref, loads_out), (schur_ref, schur_out))
        )
    ]
    for copy in copies:
        copy.start()
    size = loads_ref.shape[1] // 4
    copies[0].wait()
    for i in range(4):
        hots_out[i * size : (i + 1) * size, :] = one_hot(match_held, i)
    copies[1].wait()
    for i in (0, 2):
        block = slice(i * size, (i + 1) * size)
        loads_out[:, block] = turn(loads_out[:, block], hots_out[block, :])
    copies[2].wait()


def extra_kernel(coupling_ref, corners_ref, inverse_ref, hots_ref,
                 extra_out, spread_out, coupling_out, down_out, up_out):
    size = hots_ref.shape[1]
    slots = coupling_ref.shape[0]
    rows = extra_out.shape[0]
    hots = hots_of(hots_ref)
    extra_out[...] = jnp.full(extra_out.shape, -1.0, jnp.float32)
    corners = corners_ref[...].astype(jnp.float32)
    for i in range(4):
        extra_out[:slots, i * size : (i + 1) * size] = coupling_ref[:, i * size : (i + 1) * size]
        for k in range(3):
            at = i * size + k * rows
            extra_out[slots : slots + 1, at : at + slots] = corners
    for i in (0, 2):
        block = slice(i * size, (i + 1) * size)
        extra_out[:slots, block] = turn(coupling_ref[:, block], hots[i])
    coupling_out[...] = jnp.concatenate(parts(extra_out[...], 3), axis=0)
    spread_out[...] = spread(extra_out[...], slots, spread_out.shape[0])
    inverse = parts(inverse_ref[...], 3)
    down_out[...] = jnp.concatenate(inverse, axis=0)
    up_out[...] = jnp.concatenate(inverse, axis=1)


def turn_matrix_kernel(matrix_ref, hots_ref, out_ref):
    size = hots_ref.shape[1]
    hots = hots_of(hots_ref)
    for i in range(4):
        rows = slice(i * size, (i + 1) * size)
        block = faces_of(matrix_ref.at[rows, :], size)
        for j in (0, 2):
            block[j] = mxu(block[j], hots[j], LAST).astype(jnp.bfloat16)
        for j in range(4):
            if i in (0, 2):
                block[j] = mxu(hots[i], block[j]).astype(jnp.bfloat16)
            out_ref[rows, j * size : (j + 1) * size] = block[j]


def first_kernel(near0, near1, near2, near3, loads_ref, hots_ref, schur_ref,
                 residual_ref, send0, send1, send2, send3, result_ref):
    cases = loads_ref.shape[0]
    size = loads_ref.shape[1] // 4
    hots = hots_of(hots_ref)
    near = faces_in([x[...] for x in (near0, near1, near2, near3)])
    for i in (1, 3):
        near[i] = reorder(near[i], hots[i], PLAIN)
    residual = jump(near, faces_of(loads_ref, size))
    store(residual_ref, residual)
    product(schur_ref, result_ref, local_order(weighted(residual), hots, 1), [(0, cases, 1)])
    for ref, value in zip(
        (send0, send1, send2, send3), swapped(turned_result(result_ref, hots), odds())
    ):
        ref[...] = value


def coarse_kernel(cases, spread_ref, far_ref, near_ref, core_ref, image_ref, rest_ref):
    width, interface = spread_ref.shape
    size = interface // 4
    slots = near_ref.shape[0] - cases - 4
    own = faces_of(spread_ref, size)
    far, near, core = [
        spread(x[cases:, :size], slots, width) for x in (far_ref, near_ref, core_ref)
    ]
    zero = jnp.zeros_like(core)
    image = jump(faces_in([far, zero, near, core]), own)
    store_some(image_ref, [two_high(x) for x in image[:2]])
    store_some(rest_ref, image[2:])


def coarse_rest_kernel(cases, rest_ref, high_ref, image_ref):
    size = rest_ref.shape[1] // 2
    width = rest_ref.shape[0]
    slots = high_ref.shape[0] - cases - 4
    share = spread(high_ref[cases:, :size], slots, width)
    zero = jnp.zeros_like(share)
    low, high = faces_in([zero, share, zero, zero])[2:]
    store_some(image_ref, [two_high(rest_ref[:, :size] + low), two_high(rest_ref[:, size:] - high)])


def direction_kernel(coarse_size, count, *refs):
    own = refs[0:4]
    near = refs[4:8]
    extra_ref, coupling_ref, residual_ref, flex_ref = refs[8:12]
    n = 12
    if count > 1:
        before_ref = refs[12]
        before_free = refs[13:17]
        n = 17
    precond_ref, free0, free1, free2, free3, result_ref = refs[n:]
    size = own[0].shape[1]
    cases = residual_ref.shape[0]
    slots = extra_ref.shape[0] - 4
    precond = jump(faces_in([x[...] for x in near]), faces_in([x[...] for x in own]))
    precond = [0.5 * x for x in precond]
    store(precond_ref, precond)
    forces = signed(precond)
    left = face_parts(forces, 2)
    product(flex_ref, result_ref, left[: count * cases], [(0, cases, count)])
    free = faces_of(result_ref, size)
    extra = faces_of(extra_ref, size)
    for ref, value, rows in zip(
        (free0, free1, free2, free3), swapped(free, odds()), swapped(extra, odds())
    ):
        ref[:cases, :size] = value
        if count == 1:
            ref[cases:, :size] = rows
    scalars = [0.5 * total(faces_of(residual_ref, size), precond), total(forces, free)]
    if count > 1:
        before = signed(faces_of(before_ref, size))
        scalars.append(total(forces, faces_in([x[:cases, :size] for x in before_free])) + total(before, free))
    width = free3.shape[1] - size
    free3[:cases, size:] = partial_sums(
        left, coupling_ref[...], extra[0], slots, scalars, coarse_size, width
    )
    if count == 1:
        free3[cases:, size:] = jnp.zeros((free3.shape[0] - cases, width), jnp.float32)


def step_kernel(coarse_size, sums_ref, down_ref, up_ref, image_ref, rest_ref, own0, own1, own2, own3,
                near0, near1, near2, near3, residual_ref, hots_ref, schur_ref,
                new_ref, jump_ref, step_ref, send0, send1, send2, send3, result_ref):
    size = own0.shape[1]
    cases = sums_ref.shape[0]
    hots = hots_of(hots_ref)
    moved = jump(
        faces_in([x[:cases, :size] for x in (near0, near1, near2, near3)]),
        faces_in([x[:cases, :size] for x in (own0, own1, own2, own3)]),
    )
    store(jump_ref, moved)
    sums = sums_ref[...]
    coarse, energy = coarse_solve(coarse_part(sums, coarse_size), down_ref, up_ref)
    step = pick(sums, coarse_size) / (pick(sums, coarse_size + 1) + energy)
    step_ref[...] = jnp.broadcast_to(step, step_ref.shape)
    image = coarse_times(coarse, image_ref, rest_ref)
    residual = [
        residual_ref[:, i * size : (i + 1) * size]
        - step * (moved[i] + image[:, i * size : (i + 1) * size])
        for i in range(4)
    ]
    store(new_ref, residual)
    product(schur_ref, result_ref, local_order(weighted(residual), hots, 1), [(0, cases, 1)])
    for ref, value in zip(
        (send0, send1, send2, send3), swapped(turned_result(result_ref, hots), odds())
    ):
        ref[...] = value


def home_kernel(residual_ref, before_ref, precond_ref, jump_ref, image_ref, rest_ref, hots_ref,
                own_far, own_near, far, near,
                residual_out, before_out, precond_out, jump_out, image_out, next_out):
    size = hots_ref.shape[1]
    hots = hots_of(hots_ref)
    fields = [faces_of(x, size) for x in (residual_ref, before_ref, precond_ref, jump_ref)]
    image = [
        ref[:, block] for ref in (image_ref, rest_ref) for block in (slice(size), slice(size, None))
    ]
    for i in (0, 2):
        image[i] = mxu(image[i], hots[i]).astype(jnp.bfloat16)
        for field in fields:
            field[i] = turn_back(field[i], hots[i])
    low, high = faces_in([far[...], far[...], near[...], near[...]])[:2]
    own = [own_far[...], own_near[...]]
    own_low, own_high = faces_in([own[0], own[0], own[1], own[1]])[:2]
    store_some(next_out, [turn_back(low - own_low, hots[0]), own_high - high])
    store(image_out, image)
    for ref, field in zip((residual_out, before_out, precond_out, jump_out), fields):
        store(ref, field)


def last_kernel(coarse_size, first_ref, sums_ref, down_ref, up_ref, step_ref, residual_ref, before_ref,
                precond_ref, jump_ref, image_ref, next_ref, hots_ref, own_high, own_core,
                high_ref, core_ref, multipliers_ref, out_ref):
    size = hots_ref.shape[1]
    hots = hots_of(hots_ref)
    grp = [high_ref[...], core_ref[:, :size]]
    own = [own_high[...], own_core[:, :size]]
    low, high = faces_in([grp[0], grp[0], grp[1], grp[1]])[2:]
    own_low, own_high = faces_in([own[0], own[0], own[1], own[1]])[2:]
    following = [
        next_ref[:, :size],
        next_ref[:, size:],
        turn_back(low - own_low, hots[2]),
        own_high - high,
    ]
    first = first_ref[...]
    sums = sums_ref[...]
    beta = pick(sums, coarse_size) / pick(first, coarse_size)
    right = coarse_part(sums, coarse_size) + beta * coarse_part(first, coarse_size)
    coarse, energy = coarse_solve(right, down_ref, up_ref)
    local = pick(sums, coarse_size + 1) + beta * (
        pick(sums, coarse_size + 2) + beta * pick(first, coarse_size + 1)
    )
    step = pick(sums, coarse_size) / (local + energy)
    step_before = step_ref[:, 0:1]
    image = coarse_times(coarse, image_ref)
    for i in range(4):
        block = slice(i * size, (i + 1) * size)
        moved = following[i] + beta * jump_ref[:, block] + image[:, block]
        out_ref[:, i, :] = residual_ref[:, block] - step * moved
        before = before_ref[:, block]
        direction = precond_ref[:, block] + beta * before
        multipliers_ref[:, i, :] = step_before * before + step * direction


VMEM = pl.BlockSpec(memory_space=pltpu.VMEM)
OUTSIDE = pl.BlockSpec(memory_space=pltpu.HBM)


def call(kernel, args, outs, scratch=(), outside=(), flops=0):
    specs = [OUTSIDE if i in outside else VMEM for i in range(len(args))]
    shapes = [(x, jnp.float32) if isinstance(x[0], int) else x for x in outs]
    return pl.pallas_call(
        kernel,
        in_specs=specs,
        out_specs=[VMEM] * len(outs),
        out_shape=[jax.ShapeDtypeStruct(*x) for x in shapes],
        scratch_shapes=list(scratch),
        compiler_params=pltpu.CompilerParams(vmem_limit_bytes=28 * 2**20),
        cost_estimate=pl.CostEstimate(flops=flops, bytes_accessed=2**22, transcendentals=0),
    )(*args)


def shards(
    applied_loads,
    flex_matrix,
    schur_matrix,
    corner_coupling,
    coarse_inverse,
    face_match,
    corner_map,
):
    loads = applied_loads[0, 0]
    flex = flex_matrix[0, 0]
    schur = schur_matrix[0, 0]
    match = face_match[0, 0]
    cases, interface = loads.shape
    size = interface // 4
    slots = corner_coupling.shape[2]
    coarse_size = coarse_inverse.shape[0]
    width = -(-(coarse_size + 3) // LANES) * LANES
    work = 2 * cases * interface * interface

    inverse = jnp.pad(coarse_inverse, ((0, width - coarse_size), (0, width - coarse_size)))
    field = (cases, interface)
    face = (cases, size)
    result = pltpu.VMEM(field, jnp.float32)
    both_parts = ((2 * width, interface), jnp.bfloat16)

    held = [pltpu.with_memory_space_constraint(x, pltpu.HBM) for x in (loads, match, schur)]
    sends = swapped(
        [loads[:, i * size : (i + 1) * size] for i in range(4)], (odd("sub"), odd("grp"))
    )
    sends = lax.optimization_barrier(sends)
    near = exchange(sends)
    loads, hots, schur = call(
        prepare_kernel,
        held,
        [field, ((4 * size, size), jnp.bfloat16), (schur.shape, jnp.bfloat16)],
        [pltpu.VMEM(match.shape, jnp.int32), pltpu.SemaphoreType.DMA((3,))],
        outside=(0, 1, 2),
        flops=work,
    )
    residual, *own_first = call(
        first_kernel, [*near, loads, hots, schur], [field] + [face] * 4, [result], flops=work
    )
    near = exchange(own_first)
    residual, coupling, corners, flex = lax.optimization_barrier(
        (residual, corner_coupling[0, 0], corner_map[0], flex)
    )
    (flex,) = call(
        turn_matrix_kernel, [flex, hots], [(flex.shape, jnp.bfloat16)], flops=2 * work
    )
    extra, own_spread, coupling, down, up = call(
        extra_kernel,
        [coupling, corners, inverse, hots],
        [
            (slots + 4, interface),
            (width, interface),
            ((3 * (slots + 4), interface), jnp.bfloat16),
            ((3 * width, width), jnp.bfloat16),
            ((width, 3 * width), jnp.bfloat16),
        ],
        flops=work // 4,
    )
    before, *own_free = call(
        functools.partial(direction_kernel, coarse_size, 1),
        [*own_first, *near, extra, coupling, residual, flex],
        [field] + [(cases + slots + 4, size)] * 3 + [(cases + slots + 4, size + width)],
        [result],
        flops=work,
    )
    first_sums, near = sum_and_exchange(own_free, cases)
    half = ((2 * width, interface // 2), jnp.bfloat16)
    image, rest = call(
        functools.partial(coarse_kernel, cases),
        [own_spread, near[0], near[2], near[3]],
        [half, (width, interface // 2)],
        flops=work // 4,
    )
    (rest,) = call(
        functools.partial(coarse_rest_kernel, cases), [rest, near[1]], [half], flops=work // 8
    )
    residual, moved, step, *own = call(
        functools.partial(step_kernel, coarse_size),
        [first_sums, down, up, image, rest, *own_free, *near, residual, hots, schur],
        [field, field, (cases, LANES)] + [face] * 4,
        [result],
        flops=work,
    )
    near = exchange(own)
    precond, *own = call(
        functools.partial(direction_kernel, coarse_size, 2),
        [*own, *near, extra, coupling, residual, flex, before, *own_free],
        [field] + [face] * 3 + [(cases, size + width)],
        [result],
        flops=work,
    )
    sums, near = sum_and_exchange(own, cases)
    fields = call(
        home_kernel,
        [residual, before, precond, moved, image, rest, hots, own[0], own[2], near[0], near[2]],
        [field] * 4 + [both_parts, (cases, 2 * size)],
        flops=work // 2,
    )
    layout = (cases, 4, size)
    multipliers, residual = call(
        functools.partial(last_kernel, coarse_size),
        [first_sums, sums, down, up, step, *fields, hots, own[1], own[3], near[1], near[3]],
        [layout, layout],
        flops=work // 4,
    )
    return multipliers[None, None], residual[None, None]


def solution(mesh):
    return jax.shard_map(
        shards,
        mesh=mesh,
        in_specs=(
            P("sub", "grp", None, None),
            P("sub", "grp", None, None),
            P("sub", "grp", None, None),
            P("sub", "grp", None, None),
            P(),
            P("sub", "grp", None, None),
            P("sub", "grp", None),
        ),
        out_specs=(P("sub", "grp", None, None, None), P("sub", "grp", None, None, None)),
        check_vma=False,
    )
```

```python
import functools

import jax
import jax.numpy as jnp
from jax import lax
from jax.experimental import pallas as pl
from jax.experimental.pallas import tpu as pltpu
from jax.sharding import PartitionSpec as P

HIGHEST = lax.Precision.HIGHEST
PLAIN = (((1,), (0,)), ((), ()))
LAST = (((1,), (1,)), ((), ()))
LANES = 128
SIGNS = (-1.0, 1.0, -1.0, 1.0)


def odd(axis):
    return lax.axis_index(axis) % 2 == 1


def swapped(faces, odds):
    far, near = [], []
    for (low, high), is_odd in zip((faces[0:2], faces[2:4]), odds):
        far.append(jnp.where(is_odd, high, low))
        near.append(jnp.where(is_odd, low, high))
    return far + near


def swap(face, i):
    axis = ("sub", "grp", "sub", "grp")[i]
    peers = lax.axis_size(axis)
    if i < 2:
        pairs = [(j, (j + 2 * (j % 2) - 1) % peers) for j in range(peers)]
    else:
        pairs = [(j, j ^ 1) for j in range(peers)]
    return lax.ppermute(face, axis, pairs)


def exchange(faces):
    return lax.optimization_barrier([swap(face, i) for i, face in enumerate(faces)])


def sum_over(values, axis, step, before=(), after=()):
    peers = lax.axis_size(axis)
    first = True
    while step < peers:
        count = 4 if 4 * step <= peers else 2
        others = [
            lax.ppermute(values, axis, [(i, i ^ (k * step)) for i in range(peers)])
            for k in ((3, 1, 2) if count == 4 else (1,))
        ]
        if first:
            before, others, after = lax.optimization_barrier((before, others, after))
            first = False
        if count == 4:
            values = (values + others[1]) + (others[2] + others[0])
        else:
            values = values + others[0]
        step *= count
    return values, before, after


def sum_and_exchange(faces, cases, later=()):
    far, high, near, core = faces
    size = near.shape[1]
    other = swap(core, 3)
    values = core[:cases, size:] + other[:cases, size:]
    near, values = lax.optimization_barrier((near, values))
    near = swap(near, 2)
    values, far, _ = sum_over(values, "grp", 2, [swap(far, 0)])
    far, high, values, later = lax.optimization_barrier((far, high, values, later))
    values, high, _ = sum_over(values, "sub", 1, [swap(high, 1)])
    return values, [*far, *high, near, other], later


def one_hot(match_ref, i):
    row = match_ref[i : i + 1, :]
    size = row.shape[1]
    nodes = lax.broadcasted_iota(jnp.int32, (size, size), 0)
    return jnp.where(nodes == row, 1.0, 0.0).astype(jnp.bfloat16)


def parts(x, count):
    out = []
    for _ in range(count):
        part = x.astype(jnp.bfloat16)
        out.append(part)
        x = x - part.astype(jnp.float32)
    return out


def mxu(x, y, dims=PLAIN):
    return lax.dot_general(x, y, dims, preferred_element_type=jnp.float32)


def exact(x, y, dims=PLAIN):
    return lax.dot_general(x, y, dims, precision=HIGHEST, preferred_element_type=jnp.float32)


def reorder(x, hot, dims):
    rows = x.shape[0]
    both = mxu(jnp.concatenate(parts(x, 3), axis=0), hot, dims)
    return both[:rows] + both[rows : 2 * rows] + both[2 * rows :]


def turn(x, hot):
    return reorder(x, hot, LAST)


def turn_back(x, hot):
    return reorder(x, hot, PLAIN)


def jump(received, own):
    return [
        received[0] - own[0],
        own[1] - received[1],
        received[2] - own[2],
        own[3] - received[3],
    ]


def odds():
    return odd("sub"), odd("grp")


def faces_in(values):
    out = []
    for far, near, is_odd in zip(values[0:2], values[2:4], odds()):
        out += [jnp.where(is_odd, near, far), jnp.where(is_odd, far, near)]
    return out


def faces_of(ref, size):
    return [ref[:, i * size : (i + 1) * size] for i in range(4)]


def store(ref, faces):
    size = faces[0].shape[1]
    for i in range(4):
        ref[:, i * size : (i + 1) * size] = faces[i]


def store_some(ref, faces):
    size = faces[0].shape[1]
    for i, face in enumerate(faces):
        ref[:, i * size : (i + 1) * size] = face


def total(xs, ys):
    return sum(jnp.sum(x * y, axis=1, keepdims=True) for x, y in zip(xs, ys))


def blocks_of(interface):
    width = 256 if interface % 256 == 0 else interface
    return [slice(i, i + width) for i in range(0, interface, width)]


def product(matrix_ref, result_ref, left, groups):
    for block in blocks_of(matrix_ref.shape[1]):
        both = mxu(left, matrix_ref[:, block])
        at = 0
        for first, rows, count in groups:
            value = both[first : first + rows]
            for i in range(1, count):
                value = value + both[first + i * rows : first + (i + 1) * rows]
            result_ref[at : at + rows, block] = value
            at += rows


def local_order(faces, hots, count):
    split = [jnp.concatenate(parts(x, count), axis=0) for x in faces]
    split[0] = mxu(split[0], hots[0]).astype(jnp.bfloat16)
    split[2] = mxu(split[2], hots[2]).astype(jnp.bfloat16)
    return jnp.concatenate(split, axis=1)


def face_parts(faces, count):
    return jnp.concatenate(
        [jnp.concatenate(parts(x, count), axis=0) for x in faces], axis=1
    )


def turned_result(result_ref, hots):
    size = result_ref.shape[1] // 4
    own = faces_of(result_ref, size)
    own[0] = turn(own[0], hots[0])
    own[2] = turn(own[2], hots[2])
    return own


def weighted(faces):
    return [(0.5 * s) * x for s, x in zip(SIGNS, faces)]


def hots_of(hots_ref):
    size = hots_ref.shape[1]
    return [hots_ref[i * size : (i + 1) * size, :] for i in range(4)]


def signed(faces):
    return [s * x for s, x in zip(SIGNS, faces)]


def lane_is(shape, lane):
    return lax.broadcasted_iota(jnp.int32, shape, 1) == lane


def pick(values, lane):
    return jnp.sum(jnp.where(lane_is(values.shape, lane), values, 0.0), axis=1, keepdims=True)


def numbering(extra, slots, width):
    numbers = extra[slots : slots + 1, :LANES]
    nodes = lax.broadcasted_iota(jnp.int32, (width, LANES), 0).astype(jnp.float32)
    hot = jnp.where(nodes == numbers, 1.0, 0.0)
    return hot[:, : 3 * extra.shape[0]].astype(jnp.bfloat16)


def spread(extra, slots, width):
    return mxu(numbering(extra, slots, width), jnp.concatenate(parts(extra, 3), axis=0))


def partial_sums(left, coupling, extra, slots, scalars, coarse_size, width):
    out = reorder(mxu(left, coupling, LAST), numbering(extra, slots, width), LAST)
    rows = out.shape[0] // 2
    out = out[:rows] + out[rows:]
    for i, value in enumerate(scalars):
        out = out + jnp.where(lane_is(out.shape, coarse_size + i), value, 0.0)
    return out


def by_parts(x, matrix, dims):
    rows = x.shape[0]
    both = mxu(jnp.concatenate(parts(x, 3), axis=0), matrix, dims)
    both = both[:rows] + (both[rows : 2 * rows] + both[2 * rows :])
    width = both.shape[1] // 3
    return both[:, :width] + (both[:, width : 2 * width] + both[:, 2 * width :])


def coarse_solve(right, down_ref, up_ref):
    lowered = by_parts(right, down_ref[...], LAST)
    return by_parts(lowered, up_ref[...], PLAIN), jnp.sum(lowered * lowered, axis=1, keepdims=True)


def coarse_part(sums, coarse_size):
    lanes = lax.broadcasted_iota(jnp.int32, sums.shape, 1)
    return jnp.where(lanes < coarse_size, sums, 0.0)


def two_high(x):
    return jnp.concatenate(parts(x, 2), axis=0)


def two_wide(x):
    high, low = parts(x, 2)
    return jnp.concatenate(
        [jnp.concatenate([high, high], axis=1), jnp.concatenate([low, low], axis=1)], axis=0
    )


def coarse_times(coarse, *image_refs):
    rows = coarse.shape[0]
    left = two_wide(coarse)
    both = [mxu(left, image[...]) for image in image_refs]
    return jnp.concatenate([x[:rows] + x[rows:] for x in both], axis=1)


def prepare_kernel(loads_ref, match_ref, schur_ref,
                   loads_out, hots_out, schur_out, match_held, sems):
    copies = [
        pltpu.make_async_copy(x, y, sems.at[i])
        for i, (x, y) in enumerate(
            ((match_ref, match_held), (loads_ref, loads_out), (schur_ref, schur_out))
        )
    ]
    for copy in copies:
        copy.start()
    size = loads_ref.shape[1] // 4
    copies[0].wait()
    for i in range(4):
        hots_out[i * size : (i + 1) * size, :] = one_hot(match_held, i)
    copies[1].wait()
    for i in (0, 2):
        block = slice(i * size, (i + 1) * size)
        loads_out[:, block] = turn(loads_out[:, block], hots_out[block, :])
    copies[2].wait()


def extra_kernel(coupling_ref, corners_ref, inverse_ref, hots_ref,
                 extra_out, spread_out, coupling_out, down_out, up_out):
    size = hots_ref.shape[1]
    slots = coupling_ref.shape[0]
    rows = extra_out.shape[0]
    hots = hots_of(hots_ref)
    extra_out[...] = jnp.full(extra_out.shape, -1.0, jnp.float32)
    corners = corners_ref[...].astype(jnp.float32)
    for i in range(4):
        extra_out[:slots, i * size : (i + 1) * size] = coupling_ref[:, i * size : (i + 1) * size]
        for k in range(3):
            at = i * size + k * rows
            extra_out[slots : slots + 1, at : at + slots] = corners
    for i in (0, 2):
        block = slice(i * size, (i + 1) * size)
        extra_out[:slots, block] = turn(coupling_ref[:, block], hots[i])
    coupling_out[...] = jnp.concatenate(parts(extra_out[...], 3), axis=0)
    spread_out[...] = spread(extra_out[...], slots, spread_out.shape[0])
    inverse = parts(inverse_ref[...], 3)
    down_out[...] = jnp.concatenate(inverse, axis=0)
    up_out[...] = jnp.concatenate(inverse, axis=1)


def turn_matrix_kernel(matrix_ref, hots_ref, out_ref):
    size = hots_ref.shape[1]
    hots = hots_of(hots_ref)
    for i in range(4):
        rows = slice(i * size, (i + 1) * size)
        block = faces_of(matrix_ref.at[rows, :], size)
        for j in (0, 2):
            block[j] = mxu(block[j], hots[j], LAST).astype(jnp.bfloat16)
        block = jnp.concatenate(block, axis=1)
        if i in (0, 2):
            block = mxu(hots[i], block).astype(jnp.bfloat16)
        out_ref[rows, :] = block


def first_kernel(near0, near1, near2, near3, loads_ref, hots_ref, schur_ref,
                 residual_ref, send0, send1, send2, send3, result_ref):
    cases = loads_ref.shape[0]
    size = loads_ref.shape[1] // 4
    hots = hots_of(hots_ref)
    near = faces_in([x[...] for x in (near0, near1, near2, near3)])
    for i in (1, 3):
        near[i] = reorder(near[i], hots[i], PLAIN)
    residual = jump(near, faces_of(loads_ref, size))
    store(residual_ref, residual)
    product(schur_ref, result_ref, local_order(weighted(residual), hots, 1), [(0, cases, 1)])
    for ref, value in zip(
        (send0, send1, send2, send3), swapped(turned_result(result_ref, hots), odds())
    ):
        ref[...] = value


def coarse_kernel(cases, spread_ref, far_ref, near_ref, core_ref, image_ref, rest_ref):
    width, interface = spread_ref.shape
    size = interface // 4
    slots = near_ref.shape[0] - cases - 4
    own = faces_of(spread_ref, size)
    far, near, core = [
        spread(x[cases:, :size], slots, width) for x in (far_ref, near_ref, core_ref)
    ]
    zero = jnp.zeros_like(core)
    image = jump(faces_in([far, zero, near, core]), own)
    store_some(image_ref, [two_high(x) for x in image[:2]])
    store_some(rest_ref, image[2:])


def coarse_rest_kernel(cases, rest_ref, high_ref, image_ref):
    size = rest_ref.shape[1] // 2
    width = rest_ref.shape[0]
    slots = high_ref.shape[0] - cases - 4
    share = spread(high_ref[cases:, :size], slots, width)
    zero = jnp.zeros_like(share)
    low, high = faces_in([zero, share, zero, zero])[2:]
    store_some(image_ref, [two_high(rest_ref[:, :size] + low), two_high(rest_ref[:, size:] - high)])


def direction_kernel(coarse_size, count, *refs):
    own = refs[0:4]
    near = refs[4:8]
    extra_ref, coupling_ref, residual_ref, flex_ref = refs[8:12]
    n = 12
    if count > 1:
        before_ref = refs[12]
        before_free = refs[13:17]
        n = 17
    precond_ref, free0, free1, free2, free3, result_ref = refs[n:]
    size = own[0].shape[1]
    cases = residual_ref.shape[0]
    slots = extra_ref.shape[0] - 4
    precond = jump(faces_in([x[...] for x in near]), faces_in([x[...] for x in own]))
    precond = [0.5 * x for x in precond]
    store(precond_ref, precond)
    forces = signed(precond)
    left = face_parts(forces, 2)
    product(flex_ref, result_ref, left[: count * cases], [(0, cases, count)])
    free = faces_of(result_ref, size)
    extra = faces_of(extra_ref, size)
    for ref, value, rows in zip(
        (free0, free1, free2, free3), swapped(free, odds()), swapped(extra, odds())
    ):
        ref[:cases, :size] = value
        if count == 1:
            ref[cases:, :size] = rows
    scalars = [0.5 * total(faces_of(residual_ref, size), precond), total(forces, free)]
    if count > 1:
        before = signed(faces_of(before_ref, size))
        scalars.append(total(forces, faces_in([x[:cases, :size] for x in before_free])) + total(before, free))
    width = free3.shape[1] - size
    free3[:cases, size:] = partial_sums(
        left, coupling_ref[...], extra[0], slots, scalars, coarse_size, width
    )
    if count == 1:
        free3[cases:, size:] = jnp.zeros((free3.shape[0] - cases, width), jnp.float32)


def step_kernel(coarse_size, sums_ref, down_ref, up_ref, image_ref, rest_ref, own0, own1, own2, own3,
                near0, near1, near2, near3, residual_ref, schur_ref,
                new_ref, jump_ref, step_ref, send0, send1, send2, send3, result_ref):
    size = own0.shape[1]
    cases = sums_ref.shape[0]
    moved = jump(
        faces_in([x[:cases, :size] for x in (near0, near1, near2, near3)]),
        faces_in([x[:cases, :size] for x in (own0, own1, own2, own3)]),
    )
    store(jump_ref, moved)
    sums = sums_ref[...]
    coarse, energy = coarse_solve(coarse_part(sums, coarse_size), down_ref, up_ref)
    step = pick(sums, coarse_size) / (pick(sums, coarse_size + 1) + energy)
    step_ref[...] = jnp.broadcast_to(step, step_ref.shape)
    image = coarse_times(coarse, image_ref, rest_ref)
    residual = [
        residual_ref[:, i * size : (i + 1) * size]
        - step * (moved[i] + image[:, i * size : (i + 1) * size])
        for i in range(4)
    ]
    store(new_ref, residual)
    product(schur_ref, result_ref, face_parts(weighted(residual), 1), [(0, cases, 1)])
    for ref, value in zip(
        (send0, send1, send2, send3), swapped(faces_of(result_ref, size), odds())
    ):
        ref[...] = value


def home_kernel(residual_ref, before_ref, precond_ref, jump_ref, image_ref, rest_ref, hots_ref,
                own_far, own_near, far, near,
                residual_out, before_out, precond_out, jump_out, image_out, next_out):
    size = hots_ref.shape[1]
    hots = hots_of(hots_ref)
    fields = [faces_of(x, size) for x in (residual_ref, before_ref, precond_ref, jump_ref)]
    image = [
        ref[:, block] for ref in (image_ref, rest_ref) for block in (slice(size), slice(size, None))
    ]
    for i in (0, 2):
        image[i] = mxu(image[i], hots[i]).astype(jnp.bfloat16)
        for field in fields:
            field[i] = turn_back(field[i], hots[i])
    low, high = faces_in([far[...], far[...], near[...], near[...]])[:2]
    own = [own_far[...], own_near[...]]
    own_low, own_high = faces_in([own[0], own[0], own[1], own[1]])[:2]
    store_some(next_out, [turn_back(low - own_low, hots[0]), own_high - high])
    store(image_out, image)
    for ref, field in zip((residual_out, before_out, precond_out, jump_out), fields):
        store(ref, field)


def last_kernel(coarse_size, first_ref, sums_ref, down_ref, up_ref, step_ref, residual_ref, before_ref,
                precond_ref, jump_ref, image_ref, next_ref, hots_ref, own_high, own_core,
                high_ref, core_ref, multipliers_ref, out_ref):
    size = hots_ref.shape[1]
    hots = hots_of(hots_ref)
    grp = [high_ref[...], core_ref[:, :size]]
    own = [own_high[...], own_core[:, :size]]
    low, high = faces_in([grp[0], grp[0], grp[1], grp[1]])[2:]
    own_low, own_high = faces_in([own[0], own[0], own[1], own[1]])[2:]
    following = [
        next_ref[:, :size],
        next_ref[:, size:],
        turn_back(low - own_low, hots[2]),
        own_high - high,
    ]
    first = first_ref[...]
    sums = sums_ref[...]
    beta = pick(sums, coarse_size) / pick(first, coarse_size)
    right = coarse_part(sums, coarse_size) + beta * coarse_part(first, coarse_size)
    coarse, energy = coarse_solve(right, down_ref, up_ref)
    local = pick(sums, coarse_size + 1) + beta * (
        pick(sums, coarse_size + 2) + beta * pick(first, coarse_size + 1)
    )
    step = pick(sums, coarse_size) / (local + energy)
    step_before = step_ref[:, 0:1]
    image = coarse_times(coarse, image_ref)
    for i in range(4):
        block = slice(i * size, (i + 1) * size)
        moved = following[i] + beta * jump_ref[:, block] + image[:, block]
        out_ref[:, i, :] = residual_ref[:, block] - step * moved
        before = before_ref[:, block]
        direction = precond_ref[:, block] + beta * before
        multipliers_ref[:, i, :] = step_before * before + step * direction


VMEM = pl.BlockSpec(memory_space=pltpu.VMEM)
OUTSIDE = pl.BlockSpec(memory_space=pltpu.HBM)


def call(kernel, args, outs, scratch=(), outside=(), flops=0):
    specs = [OUTSIDE if i in outside else VMEM for i in range(len(args))]
    shapes = [(x, jnp.float32) if isinstance(x[0], int) else x for x in outs]
    return pl.pallas_call(
        kernel,
        in_specs=specs,
        out_specs=[VMEM] * len(outs),
        out_shape=[jax.ShapeDtypeStruct(*x) for x in shapes],
        scratch_shapes=list(scratch),
        compiler_params=pltpu.CompilerParams(vmem_limit_bytes=28 * 2**20),
        cost_estimate=pl.CostEstimate(flops=flops, bytes_accessed=2**22, transcendentals=0),
    )(*args)


def shards(
    applied_loads,
    flex_matrix,
    schur_matrix,
    corner_coupling,
    coarse_inverse,
    face_match,
    corner_map,
):
    loads = applied_loads[0, 0]
    flex = flex_matrix[0, 0]
    schur = schur_matrix[0, 0]
    match = face_match[0, 0]
    cases, interface = loads.shape
    size = interface // 4
    slots = corner_coupling.shape[2]
    coarse_size = coarse_inverse.shape[0]
    width = -(-(coarse_size + 3) // LANES) * LANES
    work = 2 * cases * interface * interface

    inverse = jnp.pad(coarse_inverse, ((0, width - coarse_size), (0, width - coarse_size)))
    field = (cases, interface)
    face = (cases, size)
    result = pltpu.VMEM(field, jnp.float32)
    both_parts = ((2 * width, interface), jnp.bfloat16)

    held = [pltpu.with_memory_space_constraint(x, pltpu.HBM) for x in (loads, match, schur)]
    sends = swapped(
        [loads[:, i * size : (i + 1) * size] for i in range(4)], (odd("sub"), odd("grp"))
    )
    sends = lax.optimization_barrier(sends)
    near = exchange(sends)
    loads, hots, schur = call(
        prepare_kernel,
        held,
        [field, ((4 * size, size), jnp.bfloat16), (schur.shape, jnp.bfloat16)],
        [pltpu.VMEM(match.shape, jnp.int32), pltpu.SemaphoreType.DMA((3,))],
        outside=(0, 1, 2),
        flops=work,
    )
    residual, *own_first = call(
        first_kernel, [*near, loads, hots, schur], [field] + [face] * 4, [result], flops=work
    )
    near = exchange(own_first)
    residual, coupling, corners, flex = lax.optimization_barrier(
        (residual, corner_coupling[0, 0], corner_map[0], flex)
    )
    (flex,) = call(
        turn_matrix_kernel, [flex, hots], [(flex.shape, jnp.bfloat16)], flops=2 * work
    )
    extra, own_spread, coupling, down, up = call(
        extra_kernel,
        [coupling, corners, inverse, hots],
        [
            (slots + 4, interface),
            (width, interface),
            ((3 * (slots + 4), interface), jnp.bfloat16),
            ((3 * width, width), jnp.bfloat16),
            ((width, 3 * width), jnp.bfloat16),
        ],
        flops=work // 4,
    )
    before, *own_free = call(
        functools.partial(direction_kernel, coarse_size, 1),
        [*own_first, *near, extra, coupling, residual, flex],
        [field] + [(cases + slots + 4, size)] * 3 + [(cases + slots + 4, size + width)],
        [result],
        flops=work,
    )
    first_sums, near, schur = sum_and_exchange(own_free, cases, schur)
    (schur,) = call(
        turn_matrix_kernel, [schur, hots], [(schur.shape, jnp.bfloat16)], flops=2 * work
    )
    half = ((2 * width, interface // 2), jnp.bfloat16)
    image, rest = call(
        functools.partial(coarse_kernel, cases),
        [own_spread, near[0], near[2], near[3]],
        [half, (width, interface // 2)],
        flops=work // 4,
    )
    (rest,) = call(
        functools.partial(coarse_rest_kernel, cases), [rest, near[1]], [half], flops=work // 8
    )
    residual, moved, step, *own = call(
        functools.partial(step_kernel, coarse_size),
        [first_sums, down, up, image, rest, *own_free, *near, residual, schur],
        [field, field, (cases, LANES)] + [face] * 4,
        [result],
        flops=work,
    )
    near = exchange(own)
    precond, *own = call(
        functools.partial(direction_kernel, coarse_size, 2),
        [*own, *near, extra, coupling, residual, flex, before, *own_free],
        [field] + [face] * 3 + [(cases, size + width)],
        [result],
        flops=work,
    )
    sums, near, _ = sum_and_exchange(own, cases)
    fields = call(
        home_kernel,
        [residual, before, precond, moved, image, rest, hots, own[0], own[2], near[0], near[2]],
        [field] * 4 + [both_parts, (cases, 2 * size)],
        flops=work // 2,
    )
    layout = (cases, 4, size)
    multipliers, residual = call(
        functools.partial(last_kernel, coarse_size),
        [first_sums, sums, down, up, step, *fields, hots, own[1], own[3], near[1], near[3]],
        [layout, layout],
        flops=work // 4,
    )
    return multipliers[None, None], residual[None, None]


def solution(mesh):
    return jax.shard_map(
        shards,
        mesh=mesh,
        in_specs=(
            P("sub", "grp", None, None),
            P("sub", "grp", None, None),
            P("sub", "grp", None, None),
            P("sub", "grp", None, None),
            P(),
            P("sub", "grp", None, None),
            P("sub", "grp", None),
        ),
        out_specs=(P("sub", "grp", None, None, None), P("sub", "grp", None, None, None)),
        check_vma=False,
    )
```

```python
import functools

import jax
import jax.numpy as jnp
from jax import lax
from jax.experimental import pallas as pl
from jax.experimental.pallas import tpu as pltpu
from jax.sharding import PartitionSpec as P

HIGHEST = lax.Precision.HIGHEST
PLAIN = (((1,), (0,)), ((), ()))
LAST = (((1,), (1,)), ((), ()))
LANES = 128
SIGNS = (-1.0, 1.0, -1.0, 1.0)


def odd(axis):
    return lax.axis_index(axis) % 2 == 1


def swapped(faces, odds):
    far, near = [], []
    for (low, high), is_odd in zip((faces[0:2], faces[2:4]), odds):
        far.append(jnp.where(is_odd, high, low))
        near.append(jnp.where(is_odd, low, high))
    return far + near


def swap(face, i):
    axis = ("sub", "grp", "sub", "grp")[i]
    peers = lax.axis_size(axis)
    if i < 2:
        pairs = [(j, (j + 2 * (j % 2) - 1) % peers) for j in range(peers)]
    else:
        pairs = [(j, j ^ 1) for j in range(peers)]
    return lax.ppermute(face, axis, pairs)


def exchange(faces):
    return lax.optimization_barrier([swap(face, i) for i, face in enumerate(faces)])


def sum_over(values, axis, step, before=(), after=()):
    peers = lax.axis_size(axis)
    first = True
    while step < peers:
        count = 4 if 4 * step <= peers else 2
        others = [
            lax.ppermute(values, axis, [(i, i ^ (k * step)) for i in range(peers)])
            for k in ((2, 1, 3) if count == 4 else (1,))
        ]
        if first:
            before, others, after = lax.optimization_barrier((before, others, after))
            first = False
        if count == 4:
            values = (values + others[1]) + (others[0] + others[2])
        else:
            values = values + others[0]
        step *= count
    return values, before, after


def sum_and_exchange(faces, cases):
    far, high, near, core = faces
    size = near.shape[1]
    other = swap(core, 3)
    values = core[:cases, size:] + other[:cases, size:]
    near, values = lax.optimization_barrier((near, values))
    near = swap(near, 2)
    values, far, _ = sum_over(values, "grp", 2, [swap(far, 0)])
    far, high, values = lax.optimization_barrier((far, high, values))
    values, high, _ = sum_over(values, "sub", 1, [swap(high, 1)])
    return values, [*far, *high, near, other]


def one_hot(match_ref, i):
    row = match_ref[i : i + 1, :]
    size = row.shape[1]
    nodes = lax.broadcasted_iota(jnp.int32, (size, size), 0)
    return jnp.where(nodes == row, 1.0, 0.0).astype(jnp.bfloat16)


def parts(x, count):
    out = []
    for _ in range(count):
        part = x.astype(jnp.bfloat16)
        out.append(part)
        x = x - part.astype(jnp.float32)
    return out


def mxu(x, y, dims=PLAIN):
    return lax.dot_general(x, y, dims, preferred_element_type=jnp.float32)


def exact(x, y, dims=PLAIN):
    return lax.dot_general(x, y, dims, precision=HIGHEST, preferred_element_type=jnp.float32)


def reorder(x, hot, dims):
    rows = x.shape[0]
    both = mxu(jnp.concatenate(parts(x, 3), axis=0), hot, dims)
    return both[:rows] + both[rows : 2 * rows] + both[2 * rows :]


def turn(x, hot):
    return reorder(x, hot, LAST)


def turn_back(x, hot):
    return reorder(x, hot, PLAIN)


def jump(received, own):
    return [
        received[0] - own[0],
        own[1] - received[1],
        received[2] - own[2],
        own[3] - received[3],
    ]


def odds():
    return odd("sub"), odd("grp")


def faces_in(values):
    out = []
    for far, near, is_odd in zip(values[0:2], values[2:4], odds()):
        out += [jnp.where(is_odd, near, far), jnp.where(is_odd, far, near)]
    return out


def faces_of(ref, size):
    return [ref[:, i * size : (i + 1) * size] for i in range(4)]


def store(ref, faces):
    size = faces[0].shape[1]
    for i in range(4):
        ref[:, i * size : (i + 1) * size] = faces[i]


def store_some(ref, faces):
    size = faces[0].shape[1]
    for i, face in enumerate(faces):
        ref[:, i * size : (i + 1) * size] = face


def total(xs, ys):
    return sum(jnp.sum(x * y, axis=1, keepdims=True) for x, y in zip(xs, ys))


def blocks_of(interface):
    width = 256 if interface % 256 == 0 else interface
    return [slice(i, i + width) for i in range(0, interface, width)]


def product(matrix_ref, result_ref, left, groups):
    for block in blocks_of(matrix_ref.shape[1]):
        both = mxu(left, matrix_ref[:, block])
        at = 0
        for first, rows, count in groups:
            value = both[first : first + rows]
            for i in range(1, count):
                value = value + both[first + i * rows : first + (i + 1) * rows]
            result_ref[at : at + rows, block] = value
            at += rows


def local_order(faces, hots, count):
    split = [jnp.concatenate(parts(x, count), axis=0) for x in faces]
    split[0] = mxu(split[0], hots[0]).astype(jnp.bfloat16)
    split[2] = mxu(split[2], hots[2]).astype(jnp.bfloat16)
    return jnp.concatenate(split, axis=1)


def face_parts(faces, count):
    return jnp.concatenate(
        [jnp.concatenate(parts(x, count), axis=0) for x in faces], axis=1
    )


def turned_result(result_ref, hots):
    size = result_ref.shape[1] // 4
    own = faces_of(result_ref, size)
    own[0] = turn(own[0], hots[0])
    own[2] = turn(own[2], hots[2])
    return own


def weighted(faces):
    return [(0.5 * s) * x for s, x in zip(SIGNS, faces)]


def hots_of(hots_ref):
    size = hots_ref.shape[1]
    return [hots_ref[i * size : (i + 1) * size, :] for i in range(4)]


def signed(faces):
    return [s * x for s, x in zip(SIGNS, faces)]


def lane_is(shape, lane):
    return lax.broadcasted_iota(jnp.int32, shape, 1) == lane


def pick(values, lane):
    return jnp.sum(jnp.where(lane_is(values.shape, lane), values, 0.0), axis=1, keepdims=True)


def numbering(extra, slots, width):
    numbers = extra[slots : slots + 1, :LANES]
    nodes = lax.broadcasted_iota(jnp.int32, (width, LANES), 0).astype(jnp.float32)
    hot = jnp.where(nodes == numbers, 1.0, 0.0)
    return hot[:, : 3 * extra.shape[0]].astype(jnp.bfloat16)


def spread(extra, slots, width):
    return mxu(numbering(extra, slots, width), jnp.concatenate(parts(extra, 3), axis=0))


def partial_sums(left, coupling, extra, slots, scalars, coarse_size, width):
    out = reorder(mxu(left, coupling, LAST), numbering(extra, slots, width), LAST)
    rows = out.shape[0] // 2
    out = out[:rows] + out[rows:]
    for i, value in enumerate(scalars):
        out = out + jnp.where(lane_is(out.shape, coarse_size + i), value, 0.0)
    return out


def by_parts(x, matrix, dims):
    rows = x.shape[0]
    both = mxu(jnp.concatenate(parts(x, 3), axis=0), matrix, dims)
    both = both[:rows] + (both[rows : 2 * rows] + both[2 * rows :])
    width = both.shape[1] // 3
    return both[:, :width] + (both[:, width : 2 * width] + both[:, 2 * width :])


def coarse_solve(right, down_ref, up_ref):
    lowered = by_parts(right, down_ref[...], LAST)
    return by_parts(lowered, up_ref[...], PLAIN), jnp.sum(lowered * lowered, axis=1, keepdims=True)


def coarse_part(sums, coarse_size):
    lanes = lax.broadcasted_iota(jnp.int32, sums.shape, 1)
    return jnp.where(lanes < coarse_size, sums, 0.0)


def two_high(x):
    return jnp.concatenate(parts(x, 2), axis=0)


def two_wide(x):
    high, low = parts(x, 2)
    return jnp.concatenate(
        [jnp.concatenate([high, high], axis=1), jnp.concatenate([low, low], axis=1)], axis=0
    )


def coarse_times(coarse, *image_refs):
    rows = coarse.shape[0]
    left = two_wide(coarse)
    both = [mxu(left, image[...]) for image in image_refs]
    return jnp.concatenate([x[:rows] + x[rows:] for x in both], axis=1)


def prepare_kernel(loads_ref, match_ref, schur_ref,
                   loads_out, hots_out, schur_out, match_held, sems):
    copies = [
        pltpu.make_async_copy(x, y, sems.at[i])
        for i, (x, y) in enumerate(
            ((match_ref, match_held), (loads_ref, loads_out), (schur_ref, schur_out))
        )
    ]
    for copy in copies:
        copy.start()
    size = loads_ref.shape[1] // 4
    copies[0].wait()
    for i in range(4):
        hots_out[i * size : (i + 1) * size, :] = one_hot(match_held, i)
    copies[1].wait()
    for i in (0, 2):
        block = slice(i * size, (i + 1) * size)
        loads_out[:, block] = turn(loads_out[:, block], hots_out[block, :])
    copies[2].wait()


def extra_kernel(coupling_ref, corners_ref, inverse_ref, hots_ref,
                 extra_out, spread_out, coupling_out, down_out, up_out):
    size = hots_ref.shape[1]
    slots = coupling_ref.shape[0]
    rows = extra_out.shape[0]
    hots = hots_of(hots_ref)
    extra_out[...] = jnp.full(extra_out.shape, -1.0, jnp.float32)
    corners = corners_ref[...].astype(jnp.float32)
    for i in range(4):
        extra_out[:slots, i * size : (i + 1) * size] = coupling_ref[:, i * size : (i + 1) * size]
        for k in range(3):
            at = i * size + k * rows
            extra_out[slots : slots + 1, at : at + slots] = corners
    for i in (0, 2):
        block = slice(i * size, (i + 1) * size)
        extra_out[:slots, block] = turn(coupling_ref[:, block], hots[i])
    coupling_out[...] = jnp.concatenate(parts(extra_out[...], 3), axis=0)
    spread_out[...] = spread(extra_out[...], slots, spread_out.shape[0])
    inverse = parts(inverse_ref[...], 3)
    down_out[...] = jnp.concatenate(inverse, axis=0)
    up_out[...] = jnp.concatenate(inverse, axis=1)


def turn_matrix_kernel(matrix_ref, hots_ref, out_ref):
    size = hots_ref.shape[1]
    hots = hots_of(hots_ref)
    for i in range(4):
        rows = slice(i * size, (i + 1) * size)
        block = faces_of(matrix_ref.at[rows, :], size)
        for j in (0, 2):
            block[j] = mxu(block[j], hots[j], LAST).astype(jnp.bfloat16)
        for j in range(4):
            if i in (0, 2):
                block[j] = mxu(hots[i], block[j]).astype(jnp.bfloat16)
            out_ref[rows, j * size : (j + 1) * size] = block[j]


def first_kernel(near0, near1, near2, near3, loads_ref, hots_ref, schur_ref,
                 residual_ref, send0, send1, send2, send3, result_ref):
    cases = loads_ref.shape[0]
    size = loads_ref.shape[1] // 4
    hots = hots_of(hots_ref)
    near = faces_in([x[...] for x in (near0, near1, near2, near3)])
    for i in (1, 3):
        near[i] = reorder(near[i], hots[i], PLAIN)
    residual = jump(near, faces_of(loads_ref, size))
    store(residual_ref, residual)
    product(schur_ref, result_ref, local_order(weighted(residual), hots, 1), [(0, cases, 1)])
    for ref, value in zip(
        (send0, send1, send2, send3), swapped(turned_result(result_ref, hots), odds())
    ):
        ref[...] = value


def coarse_kernel(cases, spread_ref, far_ref, near_ref, core_ref, image_ref, rest_ref):
    width, interface = spread_ref.shape
    size = interface // 4
    slots = near_ref.shape[0] - cases - 4
    own = faces_of(spread_ref, size)
    far, near, core = [
        spread(x[cases:, :size], slots, width) for x in (far_ref, near_ref, core_ref)
    ]
    zero = jnp.zeros_like(core)
    image = jump(faces_in([far, zero, near, core]), own)
    store_some(image_ref, [two_high(x) for x in image[:2]])
    store_some(rest_ref, image[2:])


def coarse_rest_kernel(cases, rest_ref, high_ref, image_ref):
    size = rest_ref.shape[1] // 2
    width = rest_ref.shape[0]
    slots = high_ref.shape[0] - cases - 4
    share = spread(high_ref[cases:, :size], slots, width)
    zero = jnp.zeros_like(share)
    low, high = faces_in([zero, share, zero, zero])[2:]
    store_some(image_ref, [two_high(rest_ref[:, :size] + low), two_high(rest_ref[:, size:] - high)])


def direction_kernel(coarse_size, count, *refs):
    own = refs[0:4]
    near = [refs[i] for i in (4, 6, 5, 7)]
    extra_ref, coupling_ref, residual_ref, flex_ref = refs[8:12]
    n = 12
    if count > 1:
        before_ref = refs[12]
        before_free = refs[13:17]
        n = 17
    precond_ref, free0, free1, free2, free3, result_ref = refs[n:]
    size = own[0].shape[1]
    cases = residual_ref.shape[0]
    slots = extra_ref.shape[0] - 4
    precond = jump(faces_in([x[...] for x in near]), faces_in([x[...] for x in own]))
    precond = [0.5 * x for x in precond]
    store(precond_ref, precond)
    forces = signed(precond)
    left = face_parts(forces, 2)
    product(flex_ref, result_ref, left[: count * cases], [(0, cases, count)])
    free = faces_of(result_ref, size)
    extra = faces_of(extra_ref, size)
    for ref, value, rows in zip(
        (free0, free1, free2, free3), swapped(free, odds()), swapped(extra, odds())
    ):
        ref[:cases, :size] = value
        if count == 1:
            ref[cases:, :size] = rows
    scalars = [0.5 * total(faces_of(residual_ref, size), precond), total(forces, free)]
    if count > 1:
        before = signed(faces_of(before_ref, size))
        scalars.append(total(forces, faces_in([x[:cases, :size] for x in before_free])) + total(before, free))
    width = free3.shape[1] - size
    free3[:cases, size:] = partial_sums(
        left, coupling_ref[...], extra[0], slots, scalars, coarse_size, width
    )
    if count == 1:
        free3[cases:, size:] = jnp.zeros((free3.shape[0] - cases, width), jnp.float32)


def step_kernel(coarse_size, sums_ref, down_ref, up_ref, image_ref, rest_ref, own0, own1, own2, own3,
                near0, near1, near2, near3, residual_ref, hots_ref, schur_ref,
                new_ref, jump_ref, step_ref, send0, send1, send2, send3, result_ref):
    size = own0.shape[1]
    cases = sums_ref.shape[0]
    hots = hots_of(hots_ref)
    moved = jump(
        faces_in([x[:cases, :size] for x in (near0, near1, near2, near3)]),
        faces_in([x[:cases, :size] for x in (own0, own1, own2, own3)]),
    )
    store(jump_ref, moved)
    sums = sums_ref[...]
    coarse, energy = coarse_solve(coarse_part(sums, coarse_size), down_ref, up_ref)
    step = pick(sums, coarse_size) / (pick(sums, coarse_size + 1) + energy)
    step_ref[...] = jnp.broadcast_to(step, step_ref.shape)
    image = coarse_times(coarse, image_ref, rest_ref)
    residual = [
        residual_ref[:, i * size : (i + 1) * size]
        - step * (moved[i] + image[:, i * size : (i + 1) * size])
        for i in range(4)
    ]
    store(new_ref, residual)
    product(schur_ref, result_ref, local_order(weighted(residual), hots, 1), [(0, cases, 1)])
    for ref, value in zip(
        (send0, send1, send2, send3), swapped(turned_result(result_ref, hots), odds())
    ):
        ref[...] = value


def home_kernel(residual_ref, before_ref, precond_ref, jump_ref, image_ref, rest_ref, hots_ref,
                own_far, own_near, far, near,
                residual_out, before_out, precond_out, jump_out, image_out, next_out):
    size = hots_ref.shape[1]
    hots = hots_of(hots_ref)
    fields = [faces_of(x, size) for x in (residual_ref, before_ref, precond_ref, jump_ref)]
    image = [
        ref[:, block] for ref in (image_ref, rest_ref) for block in (slice(size), slice(size, None))
    ]
    for i in (0, 2):
        image[i] = mxu(image[i], hots[i]).astype(jnp.bfloat16)
        for field in fields:
            field[i] = turn_back(field[i], hots[i])
    low, high = faces_in([far[...], far[...], near[...], near[...]])[:2]
    own = [own_far[...], own_near[...]]
    own_low, own_high = faces_in([own[0], own[0], own[1], own[1]])[:2]
    store_some(next_out, [turn_back(low - own_low, hots[0]), own_high - high])
    store(image_out, image)
    for ref, field in zip((residual_out, before_out, precond_out, jump_out), fields):
        store(ref, field)


def last_kernel(coarse_size, first_ref, sums_ref, down_ref, up_ref, step_ref, residual_ref, before_ref,
                precond_ref, jump_ref, image_ref, next_ref, hots_ref, own_high, own_core,
                high_ref, core_ref, multipliers_ref, out_ref):
    size = hots_ref.shape[1]
    hots = hots_of(hots_ref)
    grp = [high_ref[...], core_ref[:, :size]]
    own = [own_high[...], own_core[:, :size]]
    low, high = faces_in([grp[0], grp[0], grp[1], grp[1]])[2:]
    own_low, own_high = faces_in([own[0], own[0], own[1], own[1]])[2:]
    following = [
        next_ref[:, :size],
        next_ref[:, size:],
        turn_back(low - own_low, hots[2]),
        own_high - high,
    ]
    first = first_ref[...]
    sums = sums_ref[...]
    beta = pick(sums, coarse_size) / pick(first, coarse_size)
    right = coarse_part(sums, coarse_size) + beta * coarse_part(first, coarse_size)
    coarse, energy = coarse_solve(right, down_ref, up_ref)
    local = pick(sums, coarse_size + 1) + beta * (
        pick(sums, coarse_size + 2) + beta * pick(first, coarse_size + 1)
    )
    step = pick(sums, coarse_size) / (local + energy)
    step_before = step_ref[:, 0:1]
    image = coarse_times(coarse, image_ref)
    for i in range(4):
        block = slice(i * size, (i + 1) * size)
        moved = following[i] + beta * jump_ref[:, block] + image[:, block]
        out_ref[:, i, :] = residual_ref[:, block] - step * moved
        before = before_ref[:, block]
        direction = precond_ref[:, block] + beta * before
        multipliers_ref[:, i, :] = step_before * before + step * direction


VMEM = pl.BlockSpec(memory_space=pltpu.VMEM)
OUTSIDE = pl.BlockSpec(memory_space=pltpu.HBM)


def call(kernel, args, outs, scratch=(), outside=(), flops=0):
    specs = [OUTSIDE if i in outside else VMEM for i in range(len(args))]
    shapes = [(x, jnp.float32) if isinstance(x[0], int) else x for x in outs]
    return pl.pallas_call(
        kernel,
        in_specs=specs,
        out_specs=[VMEM] * len(outs),
        out_shape=[jax.ShapeDtypeStruct(*x) for x in shapes],
        scratch_shapes=list(scratch),
        compiler_params=pltpu.CompilerParams(vmem_limit_bytes=28 * 2**20),
        cost_estimate=pl.CostEstimate(flops=flops, bytes_accessed=2**22, transcendentals=0),
    )(*args)


def shards(
    applied_loads,
    flex_matrix,
    schur_matrix,
    corner_coupling,
    coarse_inverse,
    face_match,
    corner_map,
):
    loads = applied_loads[0, 0]
    flex = flex_matrix[0, 0]
    schur = schur_matrix[0, 0]
    match = face_match[0, 0]
    cases, interface = loads.shape
    size = interface // 4
    slots = corner_coupling.shape[2]
    coarse_size = coarse_inverse.shape[0]
    width = -(-(coarse_size + 3) // LANES) * LANES
    work = 2 * cases * interface * interface

    inverse = jnp.pad(coarse_inverse, ((0, width - coarse_size), (0, width - coarse_size)))
    field = (cases, interface)
    face = (cases, size)
    result = pltpu.VMEM(field, jnp.float32)
    both_parts = ((2 * width, interface), jnp.bfloat16)

    held = [pltpu.with_memory_space_constraint(x, pltpu.HBM) for x in (loads, match, schur)]
    sends = swapped(
        [loads[:, i * size : (i + 1) * size] for i in range(4)], (odd("sub"), odd("grp"))
    )
    sends = lax.optimization_barrier(sends)
    near = exchange(sends)
    loads, hots, schur = call(
        prepare_kernel,
        held,
        [field, ((4 * size, size), jnp.bfloat16), (schur.shape, jnp.bfloat16)],
        [pltpu.VMEM(match.shape, jnp.int32), pltpu.SemaphoreType.DMA((3,))],
        outside=(0, 1, 2),
        flops=work,
    )
    residual, *own_first = call(
        first_kernel, [*near, loads, hots, schur], [field] + [face] * 4, [result], flops=work
    )
    near = exchange(own_first)
    residual, coupling, corners, flex = lax.optimization_barrier(
        (residual, corner_coupling[0, 0], corner_map[0], flex)
    )
    (flex,) = call(
        turn_matrix_kernel, [flex, hots], [(flex.shape, jnp.bfloat16)], flops=2 * work
    )
    extra, own_spread, coupling, down, up = call(
        extra_kernel,
        [coupling, corners, inverse, hots],
        [
            (slots + 4, interface),
            (width, interface),
            ((3 * (slots + 4), interface), jnp.bfloat16),
            ((3 * width, width), jnp.bfloat16),
            ((width, 3 * width), jnp.bfloat16),
        ],
        flops=work // 4,
    )
    before, *own_free = call(
        functools.partial(direction_kernel, coarse_size, 1),
        [*own_first, near[0], near[2], near[1], near[3], extra, coupling, residual, flex],
        [field] + [(cases + slots + 4, size)] * 3 + [(cases + slots + 4, size + width)],
        [result],
        flops=work,
    )
    first_sums, near = sum_and_exchange(own_free, cases)
    half = ((2 * width, interface // 2), jnp.bfloat16)
    image, rest = call(
        functools.partial(coarse_kernel, cases),
        [own_spread, near[0], near[2], near[3]],
        [half, (width, interface // 2)],
        flops=work // 4,
    )
    (rest,) = call(
        functools.partial(coarse_rest_kernel, cases), [rest, near[1]], [half], flops=work // 8
    )
    residual, moved, step, *own = call(
        functools.partial(step_kernel, coarse_size),
        [first_sums, down, up, image, rest, *own_free, *near, residual, hots, schur],
        [field, field, (cases, LANES)] + [face] * 4,
        [result],
        flops=work,
    )
    near = exchange(own)
    precond, *own = call(
        functools.partial(direction_kernel, coarse_size, 2),
        [*own, near[0], near[2], near[1], near[3], extra, coupling, residual, flex, before, *own_free],
        [field] + [face] * 3 + [(cases, size + width)],
        [result],
        flops=work,
    )
    sums, near = sum_and_exchange(own, cases)
    fields = call(
        home_kernel,
        [residual, before, precond, moved, image, rest, hots, own[0], own[2], near[0], near[2]],
        [field] * 4 + [both_parts, (cases, 2 * size)],
        flops=work // 2,
    )
    layout = (cases, 4, size)
    multipliers, residual = call(
        functools.partial(last_kernel, coarse_size),
        [first_sums, sums, down, up, step, *fields, hots, own[1], own[3], near[1], near[3]],
        [layout, layout],
        flops=work // 4,
    )
    return multipliers[None, None], residual[None, None]


def solution(mesh):
    return jax.shard_map(
        shards,
        mesh=mesh,
        in_specs=(
            P("sub", "grp", None, None),
            P("sub", "grp", None, None),
            P("sub", "grp", None, None),
            P("sub", "grp", None, None),
            P(),
            P("sub", "grp", None, None),
            P("sub", "grp", None),
        ),
        out_specs=(P("sub", "grp", None, None, None), P("sub", "grp", None, None, None)),
        check_vma=False,
    )
```

```python
import functools

import jax
import jax.numpy as jnp
from jax import lax
from jax.experimental import pallas as pl
from jax.experimental.pallas import tpu as pltpu
from jax.sharding import PartitionSpec as P

HIGHEST = lax.Precision.HIGHEST
PLAIN = (((1,), (0,)), ((), ()))
LAST = (((1,), (1,)), ((), ()))
LANES = 128
SIGNS = (-1.0, 1.0, -1.0, 1.0)


def odd(axis):
    return lax.axis_index(axis) % 2 == 1


def swapped(faces, odds):
    far, near = [], []
    for (low, high), is_odd in zip((faces[0:2], faces[2:4]), odds):
        far.append(jnp.where(is_odd, high, low))
        near.append(jnp.where(is_odd, low, high))
    return far + near


def swap(face, i):
    axis = ("sub", "grp", "sub", "grp")[i]
    peers = lax.axis_size(axis)
    if i < 2:
        pairs = [(j, (j + 2 * (j % 2) - 1) % peers) for j in range(peers)]
    else:
        pairs = [(j, j ^ 1) for j in range(peers)]
    return lax.ppermute(face, axis, pairs)


def exchange(faces):
    order = (0, 2, 1, 3)
    far, near, high, core = [
        swap(face, i)
        for i, face in zip(order, lax.optimization_barrier([faces[i] for i in order]))
    ]
    return [far, high, near, core]


def sum_over(values, axis, step, before=(), after=()):
    peers = lax.axis_size(axis)
    first = True
    while step < peers:
        count = 4 if 4 * step <= peers else 2
        others = [
            lax.ppermute(values, axis, [(i, i ^ (k * step)) for i in range(peers)])
            for k in ((2, 1, 3) if count == 4 else (1,))
        ]
        if first:
            before, others, after = lax.optimization_barrier((before, others, after))
            first = False
        if count == 4:
            values = (values + others[1]) + (others[0] + others[2])
        else:
            values = values + others[0]
        step *= count
    return values, before, after


def sum_and_exchange(faces, cases):
    far, high, near, core = faces
    size = near.shape[1]
    other = swap(core, 3)
    values = core[:cases, size:] + other[:cases, size:]
    near, values = lax.optimization_barrier((near, values))
    near = swap(near, 2)
    values, far, _ = sum_over(values, "grp", 2, [swap(far, 0)])
    far, high, values = lax.optimization_barrier((far, high, values))
    values, high, _ = sum_over(values, "sub", 1, [swap(high, 1)])
    return values, [*far, *high, near, other]


def one_hot(match_ref, i):
    row = match_ref[i : i + 1, :]
    size = row.shape[1]
    nodes = lax.broadcasted_iota(jnp.int32, (size, size), 0)
    return jnp.where(nodes == row, 1.0, 0.0).astype(jnp.bfloat16)


def parts(x, count):
    out = []
    for _ in range(count):
        part = x.astype(jnp.bfloat16)
        out.append(part)
        x = x - part.astype(jnp.float32)
    return out


def mxu(x, y, dims=PLAIN):
    return lax.dot_general(x, y, dims, preferred_element_type=jnp.float32)


def exact(x, y, dims=PLAIN):
    return lax.dot_general(x, y, dims, precision=HIGHEST, preferred_element_type=jnp.float32)


def reorder(x, hot, dims):
    rows = x.shape[0]
    both = mxu(jnp.concatenate(parts(x, 3), axis=0), hot, dims)
    return both[:rows] + both[rows : 2 * rows] + both[2 * rows :]


def turn(x, hot):
    return reorder(x, hot, LAST)


def turn_back(x, hot):
    return reorder(x, hot, PLAIN)


def jump(received, own):
    return [
        received[0] - own[0],
        own[1] - received[1],
        received[2] - own[2],
        own[3] - received[3],
    ]


def odds():
    return odd("sub"), odd("grp")


def faces_in(values):
    out = []
    for far, near, is_odd in zip(values[0:2], values[2:4], odds()):
        out += [jnp.where(is_odd, near, far), jnp.where(is_odd, far, near)]
    return out


def faces_of(ref, size):
    return [ref[:, i * size : (i + 1) * size] for i in range(4)]


def store(ref, faces):
    size = faces[0].shape[1]
    for i in range(4):
        ref[:, i * size : (i + 1) * size] = faces[i]


def store_some(ref, faces):
    size = faces[0].shape[1]
    for i, face in enumerate(faces):
        ref[:, i * size : (i + 1) * size] = face


def total(xs, ys):
    return sum(jnp.sum(x * y, axis=1, keepdims=True) for x, y in zip(xs, ys))


def blocks_of(interface):
    width = 256 if interface % 256 == 0 else interface
    return [slice(i, i + width) for i in range(0, interface, width)]


def product(matrix_ref, result_ref, left, groups):
    for block in blocks_of(matrix_ref.shape[1]):
        both = mxu(left, matrix_ref[:, block])
        at = 0
        for first, rows, count in groups:
            value = both[first : first + rows]
            for i in range(1, count):
                value = value + both[first + i * rows : first + (i + 1) * rows]
            result_ref[at : at + rows, block] = value
            at += rows


def local_order(faces, hots, count):
    split = [jnp.concatenate(parts(x, count), axis=0) for x in faces]
    split[0] = mxu(split[0], hots[0]).astype(jnp.bfloat16)
    split[2] = mxu(split[2], hots[2]).astype(jnp.bfloat16)
    return jnp.concatenate(split, axis=1)


def face_parts(faces, count):
    return jnp.concatenate(
        [jnp.concatenate(parts(x, count), axis=0) for x in faces], axis=1
    )


def turned_result(result_ref, hots):
    size = result_ref.shape[1] // 4
    own = faces_of(result_ref, size)
    own[0] = turn(own[0], hots[0])
    own[2] = turn(own[2], hots[2])
    return own


def weighted(faces):
    return [(0.5 * s) * x for s, x in zip(SIGNS, faces)]


def hots_of(hots_ref):
    size = hots_ref.shape[1]
    return [hots_ref[i * size : (i + 1) * size, :] for i in range(4)]


def signed(faces):
    return [s * x for s, x in zip(SIGNS, faces)]


def lane_is(shape, lane):
    return lax.broadcasted_iota(jnp.int32, shape, 1) == lane


def pick(values, lane):
    return jnp.sum(jnp.where(lane_is(values.shape, lane), values, 0.0), axis=1, keepdims=True)


def numbering(extra, slots, width):
    numbers = extra[slots : slots + 1, :LANES]
    nodes = lax.broadcasted_iota(jnp.int32, (width, LANES), 0).astype(jnp.float32)
    hot = jnp.where(nodes == numbers, 1.0, 0.0)
    return hot[:, : 3 * extra.shape[0]].astype(jnp.bfloat16)


def spread(extra, slots, width):
    return mxu(numbering(extra, slots, width), jnp.concatenate(parts(extra, 3), axis=0))


def partial_sums(left, coupling, extra, slots, scalars, coarse_size, width):
    out = reorder(mxu(left, coupling, LAST), numbering(extra, slots, width), LAST)
    rows = out.shape[0] // 2
    out = out[:rows] + out[rows:]
    for i, value in enumerate(scalars):
        out = out + jnp.where(lane_is(out.shape, coarse_size + i), value, 0.0)
    return out


def by_parts(x, matrix, dims):
    rows = x.shape[0]
    both = mxu(jnp.concatenate(parts(x, 3), axis=0), matrix, dims)
    both = both[:rows] + (both[rows : 2 * rows] + both[2 * rows :])
    width = both.shape[1] // 3
    return both[:, :width] + (both[:, width : 2 * width] + both[:, 2 * width :])


def coarse_solve(right, down_ref, up_ref):
    lowered = by_parts(right, down_ref[...], LAST)
    return by_parts(lowered, up_ref[...], PLAIN), jnp.sum(lowered * lowered, axis=1, keepdims=True)


def coarse_part(sums, coarse_size):
    lanes = lax.broadcasted_iota(jnp.int32, sums.shape, 1)
    return jnp.where(lanes < coarse_size, sums, 0.0)


def two_high(x):
    return jnp.concatenate(parts(x, 2), axis=0)


def two_wide(x):
    high, low = parts(x, 2)
    return jnp.concatenate(
        [jnp.concatenate([high, high], axis=1), jnp.concatenate([low, low], axis=1)], axis=0
    )


def coarse_times(coarse, *image_refs):
    rows = coarse.shape[0]
    left = two_wide(coarse)
    both = [mxu(left, image[...]) for image in image_refs]
    return jnp.concatenate([x[:rows] + x[rows:] for x in both], axis=1)


def prepare_kernel(loads_ref, match_ref, schur_ref,
                   loads_out, hots_out, schur_out, match_held, sems):
    copies = [
        pltpu.make_async_copy(x, y, sems.at[i])
        for i, (x, y) in enumerate(
            ((match_ref, match_held), (loads_ref, loads_out), (schur_ref, schur_out))
        )
    ]
    for copy in copies:
        copy.start()
    size = loads_ref.shape[1] // 4
    copies[0].wait()
    for i in range(4):
        hots_out[i * size : (i + 1) * size, :] = one_hot(match_held, i)
    copies[1].wait()
    for i in (0, 2):
        block = slice(i * size, (i + 1) * size)
        loads_out[:, block] = turn(loads_out[:, block], hots_out[block, :])
    copies[2].wait()


def extra_kernel(coupling_ref, corners_ref, inverse_ref, hots_ref,
                 extra_out, spread_out, coupling_out, down_out, up_out):
    size = hots_ref.shape[1]
    slots = coupling_ref.shape[0]
    rows = extra_out.shape[0]
    hots = hots_of(hots_ref)
    extra_out[...] = jnp.full(extra_out.shape, -1.0, jnp.float32)
    corners = corners_ref[...].astype(jnp.float32)
    for i in range(4):
        extra_out[:slots, i * size : (i + 1) * size] = coupling_ref[:, i * size : (i + 1) * size]
        for k in range(3):
            at = i * size + k * rows
            extra_out[slots : slots + 1, at : at + slots] = corners
    for i in (0, 2):
        block = slice(i * size, (i + 1) * size)
        extra_out[:slots, block] = turn(coupling_ref[:, block], hots[i])
    coupling_out[...] = jnp.concatenate(parts(extra_out[...], 3), axis=0)
    spread_out[...] = spread(extra_out[...], slots, spread_out.shape[0])
    inverse = parts(inverse_ref[...], 3)
    down_out[...] = jnp.concatenate(inverse, axis=0)
    up_out[...] = jnp.concatenate(inverse, axis=1)


def turn_matrix_kernel(matrix_ref, hots_ref, out_ref):
    size = hots_ref.shape[1]
    hots = hots_of(hots_ref)
    for i in range(4):
        rows = slice(i * size, (i + 1) * size)
        block = faces_of(matrix_ref.at[rows, :], size)
        for j in (0, 2):
            block[j] = mxu(block[j], hots[j], LAST).astype(jnp.bfloat16)
        for j in range(4):
            if i in (0, 2):
                block[j] = mxu(hots[i], block[j]).astype(jnp.bfloat16)
            out_ref[rows, j * size : (j + 1) * size] = block[j]


def first_kernel(near0, near1, near2, near3, loads_ref, hots_ref, schur_ref,
                 residual_ref, send0, send1, send2, send3, result_ref):
    cases = loads_ref.shape[0]
    size = loads_ref.shape[1] // 4
    hots = hots_of(hots_ref)
    near = faces_in([x[...] for x in (near0, near1, near2, near3)])
    for i in (1, 3):
        near[i] = reorder(near[i], hots[i], PLAIN)
    residual = jump(near, faces_of(loads_ref, size))
    store(residual_ref, residual)
    product(schur_ref, result_ref, local_order(weighted(residual), hots, 1), [(0, cases, 1)])
    for ref, value in zip(
        (send0, send1, send2, send3), swapped(turned_result(result_ref, hots), odds())
    ):
        ref[...] = value


def coarse_kernel(cases, spread_ref, far_ref, near_ref, core_ref, image_ref, rest_ref):
    width, interface = spread_ref.shape
    size = interface // 4
    slots = near_ref.shape[0] - cases - 4
    own = faces_of(spread_ref, size)
    far, near, core = [
        spread(x[cases:, :size], slots, width) for x in (far_ref, near_ref, core_ref)
    ]
    zero = jnp.zeros_like(core)
    image = jump(faces_in([far, zero, near, core]), own)
    store_some(image_ref, [two_high(x) for x in image[:2]])
    store_some(rest_ref, image[2:])


def coarse_rest_kernel(cases, rest_ref, high_ref, image_ref):
    size = rest_ref.shape[1] // 2
    width = rest_ref.shape[0]
    slots = high_ref.shape[0] - cases - 4
    share = spread(high_ref[cases:, :size], slots, width)
    zero = jnp.zeros_like(share)
    low, high = faces_in([zero, share, zero, zero])[2:]
    store_some(image_ref, [two_high(rest_ref[:, :size] + low), two_high(rest_ref[:, size:] - high)])


def direction_kernel(coarse_size, count, *refs):
    own = refs[0:4]
    near = [refs[i] for i in (4, 6, 5, 7)]
    extra_ref, coupling_ref, residual_ref, flex_ref = refs[8:12]
    n = 12
    if count > 1:
        before_ref = refs[12]
        before_free = refs[13:17]
        n = 17
    precond_ref, free0, free1, free2, free3, result_ref = refs[n:]
    size = own[0].shape[1]
    cases = residual_ref.shape[0]
    slots = extra_ref.shape[0] - 4
    precond = jump(faces_in([x[...] for x in near]), faces_in([x[...] for x in own]))
    precond = [0.5 * x for x in precond]
    store(precond_ref, precond)
    forces = signed(precond)
    left = face_parts(forces, 2)
    product(flex_ref, result_ref, left[: count * cases], [(0, cases, count)])
    free = faces_of(result_ref, size)
    extra = faces_of(extra_ref, size)
    for ref, value, rows in zip(
        (free0, free1, free2, free3), swapped(free, odds()), swapped(extra, odds())
    ):
        ref[:cases, :size] = value
        if count == 1:
            ref[cases:, :size] = rows
    scalars = [0.5 * total(faces_of(residual_ref, size), precond), total(forces, free)]
    if count > 1:
        before = signed(faces_of(before_ref, size))
        scalars.append(total(forces, faces_in([x[:cases, :size] for x in before_free])) + total(before, free))
    width = free3.shape[1] - size
    free3[:cases, size:] = partial_sums(
        left, coupling_ref[...], extra[0], slots, scalars, coarse_size, width
    )
    if count == 1:
        free3[cases:, size:] = jnp.zeros((free3.shape[0] - cases, width), jnp.float32)


def step_kernel(coarse_size, sums_ref, down_ref, up_ref, image_ref, rest_ref, own0, own1, own2, own3,
                near0, near1, near2, near3, residual_ref, hots_ref, schur_ref,
                new_ref, jump_ref, step_ref, send0, send1, send2, send3, result_ref):
    size = own0.shape[1]
    cases = sums_ref.shape[0]
    hots = hots_of(hots_ref)
    moved = jump(
        faces_in([x[:cases, :size] for x in (near0, near1, near2, near3)]),
        faces_in([x[:cases, :size] for x in (own0, own1, own2, own3)]),
    )
    store(jump_ref, moved)
    sums = sums_ref[...]
    coarse, energy = coarse_solve(coarse_part(sums, coarse_size), down_ref, up_ref)
    step = pick(sums, coarse_size) / (pick(sums, coarse_size + 1) + energy)
    step_ref[...] = jnp.broadcast_to(step, step_ref.shape)
    image = coarse_times(coarse, image_ref, rest_ref)
    residual = [
        residual_ref[:, i * size : (i + 1) * size]
        - step * (moved[i] + image[:, i * size : (i + 1) * size])
        for i in range(4)
    ]
    store(new_ref, residual)
    product(schur_ref, result_ref, local_order(weighted(residual), hots, 1), [(0, cases, 1)])
    for ref, value in zip(
        (send0, send1, send2, send3), swapped(turned_result(result_ref, hots), odds())
    ):
        ref[...] = value


def home_kernel(residual_ref, before_ref, precond_ref, jump_ref, image_ref, rest_ref, hots_ref,
                own_far, own_near, far, near,
                residual_out, before_out, precond_out, jump_out, image_out, next_out):
    size = hots_ref.shape[1]
    hots = hots_of(hots_ref)
    fields = [faces_of(x, size) for x in (residual_ref, before_ref, precond_ref, jump_ref)]
    image = [
        ref[:, block] for ref in (image_ref, rest_ref) for block in (slice(size), slice(size, None))
    ]
    for i in (0, 2):
        image[i] = mxu(image[i], hots[i]).astype(jnp.bfloat16)
        for field in fields:
            field[i] = turn_back(field[i], hots[i])
    low, high = faces_in([far[...], far[...], near[...], near[...]])[:2]
    own = [own_far[...], own_near[...]]
    own_low, own_high = faces_in([own[0], own[0], own[1], own[1]])[:2]
    store_some(next_out, [turn_back(low - own_low, hots[0]), own_high - high])
    store(image_out, image)
    for ref, field in zip((residual_out, before_out, precond_out, jump_out), fields):
        store(ref, field)


def last_kernel(coarse_size, first_ref, sums_ref, down_ref, up_ref, step_ref, residual_ref, before_ref,
                precond_ref, jump_ref, image_ref, next_ref, hots_ref, own_high, own_core,
                high_ref, core_ref, multipliers_ref, out_ref):
    size = hots_ref.shape[1]
    hots = hots_of(hots_ref)
    grp = [high_ref[...], core_ref[:, :size]]
    own = [own_high[...], own_core[:, :size]]
    low, high = faces_in([grp[0], grp[0], grp[1], grp[1]])[2:]
    own_low, own_high = faces_in([own[0], own[0], own[1], own[1]])[2:]
    following = [
        next_ref[:, :size],
        next_ref[:, size:],
        turn_back(low - own_low, hots[2]),
        own_high - high,
    ]
    first = first_ref[...]
    sums = sums_ref[...]
    beta = pick(sums, coarse_size) / pick(first, coarse_size)
    right = coarse_part(sums, coarse_size) + beta * coarse_part(first, coarse_size)
    coarse, energy = coarse_solve(right, down_ref, up_ref)
    local = pick(sums, coarse_size + 1) + beta * (
        pick(sums, coarse_size + 2) + beta * pick(first, coarse_size + 1)
    )
    step = pick(sums, coarse_size) / (local + energy)
    step_before = step_ref[:, 0:1]
    image = coarse_times(coarse, image_ref)
    for i in range(4):
        block = slice(i * size, (i + 1) * size)
        moved = following[i] + beta * jump_ref[:, block] + image[:, block]
        out_ref[:, i, :] = residual_ref[:, block] - step * moved
        before = before_ref[:, block]
        direction = precond_ref[:, block] + beta * before
        multipliers_ref[:, i, :] = step_before * before + step * direction


VMEM = pl.BlockSpec(memory_space=pltpu.VMEM)
OUTSIDE = pl.BlockSpec(memory_space=pltpu.HBM)


def call(kernel, args, outs, scratch=(), outside=(), flops=0):
    specs = [OUTSIDE if i in outside else VMEM for i in range(len(args))]
    shapes = [(x, jnp.float32) if isinstance(x[0], int) else x for x in outs]
    return pl.pallas_call(
        kernel,
        in_specs=specs,
        out_specs=[VMEM] * len(outs),
        out_shape=[jax.ShapeDtypeStruct(*x) for x in shapes],
        scratch_shapes=list(scratch),
        compiler_params=pltpu.CompilerParams(vmem_limit_bytes=28 * 2**20),
        cost_estimate=pl.CostEstimate(flops=flops, bytes_accessed=2**22, transcendentals=0),
    )(*args)


def shards(
    applied_loads,
    flex_matrix,
    schur_matrix,
    corner_coupling,
    coarse_inverse,
    face_match,
    corner_map,
):
    loads = applied_loads[0, 0]
    flex = flex_matrix[0, 0]
    schur = schur_matrix[0, 0]
    match = face_match[0, 0]
    cases, interface = loads.shape
    size = interface // 4
    slots = corner_coupling.shape[2]
    coarse_size = coarse_inverse.shape[0]
    width = -(-(coarse_size + 3) // LANES) * LANES
    work = 2 * cases * interface * interface

    inverse = jnp.pad(coarse_inverse, ((0, width - coarse_size), (0, width - coarse_size)))
    field = (cases, interface)
    face = (cases, size)
    result = pltpu.VMEM(field, jnp.float32)
    both_parts = ((2 * width, interface), jnp.bfloat16)

    held = [pltpu.with_memory_space_constraint(x, pltpu.HBM) for x in (loads, match, schur)]
    sends = swapped(
        [loads[:, i * size : (i + 1) * size] for i in range(4)], (odd("sub"), odd("grp"))
    )
    sends = lax.optimization_barrier(sends)
    near = exchange(sends)
    loads, hots, schur = call(
        prepare_kernel,
        held,
        [field, ((4 * size, size), jnp.bfloat16), (schur.shape, jnp.bfloat16)],
        [pltpu.VMEM(match.shape, jnp.int32), pltpu.SemaphoreType.DMA((3,))],
        outside=(0, 1, 2),
        flops=work,
    )
    residual, *own_first = call(
        first_kernel, [*near, loads, hots, schur], [field] + [face] * 4, [result], flops=work
    )
    near = exchange(own_first)
    residual, coupling, corners, flex = lax.optimization_barrier(
        (residual, corner_coupling[0, 0], corner_map[0], flex)
    )
    (flex,) = call(
        turn_matrix_kernel, [flex, hots], [(flex.shape, jnp.bfloat16)], flops=2 * work
    )
    extra, own_spread, coupling, down, up = call(
        extra_kernel,
        [coupling, corners, inverse, hots],
        [
            (slots + 4, interface),
            (width, interface),
            ((3 * (slots + 4), interface), jnp.bfloat16),
            ((3 * width, width), jnp.bfloat16),
            ((width, 3 * width), jnp.bfloat16),
        ],
        flops=work // 4,
    )
    before, *own_free = call(
        functools.partial(direction_kernel, coarse_size, 1),
        [*own_first, near[0], near[2], near[1], near[3], extra, coupling, residual, flex],
        [field] + [(cases + slots + 4, size)] * 3 + [(cases + slots + 4, size + width)],
        [result],
        flops=work,
    )
    first_sums, near = sum_and_exchange(own_free, cases)
    half = ((2 * width, interface // 2), jnp.bfloat16)
    image, rest = call(
        functools.partial(coarse_kernel, cases),
        [own_spread, near[0], near[2], near[3]],
        [half, (width, interface // 2)],
        flops=work // 4,
    )
    (rest,) = call(
        functools.partial(coarse_rest_kernel, cases), [rest, near[1]], [half], flops=work // 8
    )
    residual, moved, step, *own = call(
        functools.partial(step_kernel, coarse_size),
        [first_sums, down, up, image, rest, *own_free, *near, residual, hots, schur],
        [field, field, (cases, LANES)] + [face] * 4,
        [result],
        flops=work,
    )
    near = exchange(own)
    precond, *own = call(
        functools.partial(direction_kernel, coarse_size, 2),
        [*own, near[0], near[2], near[1], near[3], extra, coupling, residual, flex, before, *own_free],
        [field] + [face] * 3 + [(cases, size + width)],
        [result],
        flops=work,
    )
    sums, near = sum_and_exchange(own, cases)
    fields = call(
        home_kernel,
        [residual, before, precond, moved, image, rest, hots, own[0], own[2], near[0], near[2]],
        [field] * 4 + [both_parts, (cases, 2 * size)],
        flops=work // 2,
    )
    layout = (cases, 4, size)
    multipliers, residual = call(
        functools.partial(last_kernel, coarse_size),
        [first_sums, sums, down, up, step, *fields, hots, own[1], own[3], near[1], near[3]],
        [layout, layout],
        flops=work // 4,
    )
    return multipliers[None, None], residual[None, None]


def solution(mesh):
    return jax.shard_map(
        shards,
        mesh=mesh,
        in_specs=(
            P("sub", "grp", None, None),
            P("sub", "grp", None, None),
            P("sub", "grp", None, None),
            P("sub", "grp", None, None),
            P(),
            P("sub", "grp", None, None),
            P("sub", "grp", None),
        ),
        out_specs=(P("sub", "grp", None, None, None), P("sub", "grp", None, None, None)),
        check_vma=False,
    )
```
